32 devices in a mesh: frame: 4 (over z), row: 4 (over x, core), dp: 2 (over y).
Axes of the slice: x: 2, y: 2, z: 4, core: 2. Of those that a mesh axis runs over, the one named last changes fastest.
Arguments:
- queries: bfloat16 [8, 48, 80, 512], P(('dp', 'frame'), None, None, 'row'), parts along dimension 0, may hold values from -24 to 24
- keys: bfloat16 [8, 48, 80, 512], P(('dp', 'frame'), None, None, 'row'), parts along dimension 0, may hold values from -6 to 6
- values: bfloat16 [8, 48, 80, 512], P(('dp', 'frame'), None, None, 'row'), parts along dimension 0, may hold values from -6 to 6
- back_reach: int32 [12, 10], P('dp'), parts along dimension 0, may hold values from 0 to 3
- fwd_reach: int32 [12, 10], P('dp'), parts along dimension 0, may hold values from 0 to 3
- valid_rows: int32 [8], P('dp'), parts along dimension 0, may hold values from 41 to 48
- valid_cols: int32 [8], P('dp'), parts along dimension 0, may hold values from 73 to 80
Outputs:
- block_out: bfloat16 [8, 48, 80, 512], P(('dp', 'frame'), None, None, 'row'), parts along dimension 0
The draws below stay inside these ranges and needn't reach their ends.
There are 2 independent parts, one for each index of `dp`. The reference program is written for one: setup_inputs(seed, part) draws one part's arguments, and reference() takes and returns one part's arrays. A program takes and returns all parts, laid end to end along the dimension named above; each array names one. Nothing has to cross between parts.
All inputs are finite; a program needn't handle non-finite values.
Results may differ from the reference program's by a relative error of at most 0.012.
Values may be sent and summed in bfloat16 or wider, within the bound.
No kernel may reach another device: no remote copies, remote signals or barrier semaphores. Data moves between devices by JAX's collectives and lax.ppermute only.
A program may use at most 64 MiB of HBM per device.

```python
import math
import jax
import jax.numpy as jnp
from jax import lax

HEADS = 4
DH = 128
TS = 8
NTR = 6
TC = 10
NF = 4
HT = 48
WT = 80


def shared_keys(key):
    return jnp.clip(jax.random.normal(jax.random.fold_in(key, 11), (NF, HT, WT, HEADS * DH), jnp.float32), -6.0, 6.0)


def draw_keys(key, part):
    return shared_keys(key).astype(jnp.bfloat16)


def draw_queries(key, part):
    full_shape = (NF, HT, WT, HEADS * DH)
    drawn = jax.random.normal(jax.random.fold_in(key, 23), full_shape, jnp.float32)
    return jnp.clip(drawn, -6.0, 6.0).astype(jnp.bfloat16)


def place_ends(entries, stream_key, low, top_value):
    spot = [jax.random.randint(jax.random.fold_in(stream_key, axis), (), 0, length) for axis, length in enumerate(entries.shape)]
    longest = entries.shape.index(max(entries.shape))
    neighbour = spot[:longest] + [(spot[longest] + 1) % entries.shape[longest]] + spot[longest + 1:]
    return entries.at[tuple(spot)].set(low).at[tuple(neighbour)].set(top_value)


def block_levels(rng, extent, shards, least, top_value):
    gain, own = 1.0, jax.random.fold_in(rng, 6)
    for dim, shards_of in shards:
        steps = jnp.exp(jax.random.uniform(jax.random.fold_in(own, dim), (shards_of,), jnp.float32, least / len(shards), top_value / len(shards)))
        gain = gain * jnp.repeat(steps, extent[dim] // shards_of).reshape([-1 if axis == dim else 1 for axis in range(len(extent))])
    return gain


def gaussian(rng, dims, width, limit, shards=(), held_as=jnp.bfloat16):
    result = jax.random.normal(rng, dims, jnp.float32) * width
    if len(shards) > 0:
        result = block_levels(rng, dims, shards, -0.22, 0.18) * result
    return jnp.clip(result, min=-limit, max=limit).astype(held_as)


def setup_inputs(seed: int = 0, part: int = 0) -> dict:
    seeds = jax.random.split(jax.random.key(seed), 8)
    part_keys = jax.random.split(jax.random.fold_in(seeds[7], part), 8)
    queries = draw_queries(jax.random.fold_in(jax.random.fold_in(seeds[7], part), 71), part)
    keys = draw_keys(jax.random.fold_in(jax.random.fold_in(seeds[7], part), 71), part)
    values = gaussian(part_keys[2], (NF, HT, WT, HEADS * DH), 1.0, 6.0, ((0, 4), (3, 4)))
    back_reach = place_ends(jax.random.randint(part_keys[3], (NTR, TC), 0, NF), jax.random.fold_in(part_keys[3], 1), 0, NF - 1).astype(jnp.int32)
    fwd_reach = place_ends(jax.random.randint(part_keys[4], (NTR, TC), 0, NF), jax.random.fold_in(part_keys[4], 1), 0, NF - 1).astype(jnp.int32)
    valid_rows = place_ends(jax.random.randint(part_keys[5], (NF,), HT - TS + 1, HT + 1), jax.random.fold_in(part_keys[5], 1), HT - TS + 1, HT).astype(jnp.int32)
    valid_cols = place_ends(jax.random.randint(part_keys[6], (NF,), WT - TS + 1, WT + 1), jax.random.fold_in(part_keys[6], 1), WT - TS + 1, WT).astype(jnp.int32)
    return {"queries": queries, "keys": keys, "values": values, "back_reach": back_reach, "fwd_reach": fwd_reach, "valid_rows": valid_rows, "valid_cols": valid_cols}


def attend(query_rows, key_rows, value_rows, allowed):
    dot_terms = jnp.dot(query_rows, key_rows.T, preferred_element_type=jnp.float32)
    query_sq = lax.optimization_barrier(jnp.sum(jnp.square(query_rows.astype(jnp.float32)), axis=1))
    key_sq = lax.optimization_barrier(jnp.sum(jnp.square(key_rows.astype(jnp.float32)), axis=1))
    distance = query_sq[:, None] + key_sq[None, :] - 2.0 * dot_terms
    scores = jnp.where(allowed, -distance * (0.5 / math.sqrt(query_rows.shape[1])), -jnp.inf)
    highest = lax.optimization_barrier(jnp.max(scores, axis=1, keepdims=True))
    weights = jnp.exp(scores - highest)
    totals = lax.optimization_barrier(jnp.sum(weights, axis=1, keepdims=True))
    mixed = jnp.dot(weights.astype(jnp.bfloat16), value_rows, preferred_element_type=jnp.float32)
    return mixed / totals

def tile_split(block):
    frames = block.shape[0]
    heads = block.shape[3] // DH
    return block.reshape(frames, NTR, TS, TC, TS, heads, DH).transpose(5, 0, 1, 3, 2, 4, 6).reshape(heads, frames, NTR * TC, TS * TS, DH)

def neighbours(tiles):
    count = tiles.shape[0]
    grid = tiles.reshape((count, NTR, TC) + tiles.shape[2:])
    padded = jnp.pad(grid, ((0, 0), (1, 1), (1, 1), (0, 0), (0, 0)))
    views = [padded[:, dy:dy + NTR, dx:dx + TC] for dy in range(3) for dx in range(3)]
    stacked = jnp.stack(views, axis=3)
    return stacked.reshape(count * NTR * TC, 9 * tiles.shape[2], tiles.shape[3])

def reference(queries, keys, values, back_reach, fwd_reach, valid_rows, valid_cols):
    tile_area = TS * TS
    count_tiles = NTR * TC
    row_ids = jnp.arange(HT, dtype=jnp.int32)
    col_ids = jnp.arange(WT, dtype=jnp.int32)
    row_ok = row_ids[None, :] < valid_rows[:, None]
    col_ok = col_ids[None, :] < valid_cols[:, None]
    token_valid = row_ok[:, :, None] & col_ok[:, None, :]
    tile_valid = token_valid.reshape(NF, NTR, TS, TC, TS).transpose(0, 1, 3, 2, 4).reshape(NF, NTR, TC, tile_area)
    padded_valid = jnp.pad(tile_valid, ((0, 0), (1, 1), (1, 1), (0, 0)))
    near_valid = jnp.stack([padded_valid[:, dy:dy + NTR, dx:dx + TC] for dy in range(3) for dx in range(3)], axis=3)
    near_valid = near_valid.reshape(NF, count_tiles, 1, 9 * tile_area)
    query_factor = tile_valid.reshape(NF, count_tiles, tile_area).astype(jnp.float32)
    query_t = tile_split(queries)
    key_t = tile_split(keys)
    value_t = tile_split(values)

    def spatial_frame(frame_index):
        frame_q = lax.dynamic_index_in_dim(query_t, frame_index, 1, keepdims=False)
        frame_k = lax.dynamic_index_in_dim(key_t, frame_index, 1, keepdims=False)
        frame_v = lax.dynamic_index_in_dim(value_t, frame_index, 1, keepdims=False)
        frame_mask = lax.dynamic_index_in_dim(near_valid, frame_index, 0, keepdims=False)
        frame_factor = lax.dynamic_index_in_dim(query_factor, frame_index, 0, keepdims=False)
        near_k = neighbours(frame_k)
        near_v = neighbours(frame_v)
        flat_q = frame_q.reshape(HEADS * count_tiles, tile_area, DH)
        masks = jnp.broadcast_to(frame_mask[None], (HEADS, count_tiles, 1, 9 * tile_area)).reshape(HEADS * count_tiles, 1, 9 * tile_area)
        mixed = jax.vmap(attend)(flat_q, near_k, near_v, masks).reshape(HEADS, count_tiles, tile_area, DH)
        return (mixed * frame_factor[None, :, :, None]).astype(jnp.bfloat16)
    spatial_t = lax.map(spatial_frame, jnp.arange(NF, dtype=jnp.int32)).transpose(1, 0, 2, 3, 4)
    length = NF * tile_area
    frame_of = jnp.arange(length, dtype=jnp.int32) // tile_area
    frame_gap = frame_of[None, :] - frame_of[:, None]
    back_flat = back_reach.reshape(count_tiles)
    fwd_flat = fwd_reach.reshape(count_tiles)
    valid_flat = tile_valid.reshape(NF, count_tiles, tile_area).transpose(1, 0, 2).reshape(count_tiles, length)

    def temporal_tile(tile_index):
        tile_q = lax.dynamic_index_in_dim(query_t, tile_index, 2, keepdims=False).reshape(HEADS, length, DH)
        tile_k = lax.dynamic_index_in_dim(key_t, tile_index, 2, keepdims=False).reshape(HEADS, length, DH)
        tile_v = lax.dynamic_index_in_dim(spatial_t, tile_index, 2, keepdims=False).reshape(HEADS, length, DH)
        key_ok = lax.dynamic_index_in_dim(valid_flat, tile_index, 0, keepdims=False)
        back_one = lax.dynamic_index_in_dim(back_flat, tile_index, 0, keepdims=False)
        fwd_one = lax.dynamic_index_in_dim(fwd_flat, tile_index, 0, keepdims=False)
        allowed = (frame_gap >= -back_one) & (frame_gap <= fwd_one) & key_ok[None, :]
        mixed = jax.vmap(attend, in_axes=(0, 0, 0, None))(tile_q, tile_k, tile_v, allowed)
        return mixed.astype(jnp.bfloat16)
    temporal = lax.map(temporal_tile, jnp.arange(count_tiles, dtype=jnp.int32))
    temporal = temporal.reshape(count_tiles, HEADS, NF, tile_area, DH).transpose(1, 2, 0, 3, 4)
    combined = (spatial_t.astype(jnp.float32) + temporal.astype(jnp.float32)) * query_factor[None, :, :, :, None]
    combined = combined.astype(jnp.bfloat16).reshape(HEADS, NF, NTR, TC, TS, TS, DH)
    return combined.transpose(1, 2, 4, 3, 5, 0, 6).reshape(NF, HT, WT, HEADS * DH)
```

```python
import functools
import math

import jax
import jax.numpy as jnp
from jax import lax
from jax.experimental import pallas as pl
from jax.experimental.pallas import tpu as pltpu
from jax.sharding import PartitionSpec as P

DH = 128
TS = 8


def group_size(item_count, row_count):
    size = 1
    for option in range(1, item_count + 1):
        if item_count % option == 0 and option * row_count <= 1024:
            size = option
    return size


def attend_group(group_parts):
    query_rows, key_rows, value_rows, allowed = group_parts
    dot_terms = jnp.einsum("gmd,gnd->gmn", query_rows, key_rows, preferred_element_type=jnp.float32)
    query_sq = jnp.einsum("gmd,gmd->gm", query_rows, query_rows, preferred_element_type=jnp.float32)
    key_sq = jnp.einsum("gnd,gnd->gn", key_rows, key_rows, preferred_element_type=jnp.float32)
    distance = query_sq[:, :, None] + key_sq[:, None, :] - 2.0 * dot_terms
    scores = jnp.where(allowed, -distance * (0.5 / math.sqrt(query_rows.shape[2])), -jnp.inf)
    highest = jnp.max(scores, axis=2, keepdims=True)
    weights = jnp.exp(scores - highest)
    totals = jnp.sum(weights, axis=2, keepdims=True)
    mixed = jnp.einsum(
        "gmn,gnd->gmd", weights.astype(jnp.bfloat16), value_rows, preferred_element_type=jnp.float32
    )
    return mixed / totals


def attend_items(query_items, key_items, value_items, masks):
    item_count = query_items.shape[0]
    per_group = group_size(item_count, query_items.shape[1])
    groups = item_count // per_group

    def regroup(array):
        return array.reshape((groups, per_group) + array.shape[1:])

    mixed = lax.map(
        attend_group,
        (regroup(query_items), regroup(key_items), regroup(value_items), regroup(masks)),
    )
    return mixed.reshape((item_count,) + mixed.shape[2:])


def tile_split(block):
    frames, token_rows, token_cols, channels = block.shape
    heads = channels // DH
    return (
        block.reshape(frames, token_rows // TS, TS, token_cols // TS, TS, heads, DH)
        .transpose(5, 0, 1, 3, 2, 4, 6)
        .reshape(heads, frames, token_rows // TS * (token_cols // TS), TS * TS, DH)
    )


def neighbours(tiles, tile_rows, tile_cols):
    heads, frames, count_tiles, area, depth = tiles.shape
    grid = tiles.reshape(heads * frames, tile_rows, tile_cols, area, depth)
    padded = jnp.pad(grid, ((0, 0), (1, 1), (1, 1), (0, 0), (0, 0)))
    views = [
        padded[:, dy : dy + tile_rows, dx : dx + tile_cols] for dy in range(3) for dx in range(3)
    ]
    stacked = jnp.stack(views, axis=3)
    return stacked.reshape(heads * frames * count_tiles, 9 * area, depth)


def pad_tiles(tiles, total):
    return jnp.pad(tiles, ((0, 0), (0, 0), (0, total - tiles.shape[2]), (0, 0), (0, 0)))


def per_device(queries, keys, values, back_reach, fwd_reach, valid_rows, valid_cols):
    frames, token_rows, token_cols, channels = queries.shape
    heads = channels // DH
    tile_rows = token_rows // TS
    tile_cols = token_cols // TS
    count_tiles = tile_rows * tile_cols
    area = TS * TS
    frame_count = lax.axis_size("frame")
    frame_index = lax.axis_index("frame")
    padded_count = (count_tiles + frame_count - 1) // frame_count * frame_count
    tiles_here = padded_count // frame_count
    all_frames = frames * frame_count
    row_ids = jnp.arange(token_rows, dtype=jnp.int32)
    col_ids = jnp.arange(token_cols, dtype=jnp.int32)
    row_ok = row_ids[None, :] < valid_rows[:, None]
    col_ok = col_ids[None, :] < valid_cols[:, None]
    token_valid = row_ok[:, :, None] & col_ok[:, None, :]
    tile_valid_all = (
        token_valid.reshape(all_frames, tile_rows, TS, tile_cols, TS)
        .transpose(0, 1, 3, 2, 4)
        .reshape(all_frames, tile_rows, tile_cols, area)
    )
    tile_valid = lax.dynamic_slice_in_dim(tile_valid_all, frame_index * frames, frames, 0)
    padded_valid = jnp.pad(tile_valid, ((0, 0), (1, 1), (1, 1), (0, 0)))
    near_valid = jnp.stack(
        [
            padded_valid[:, dy : dy + tile_rows, dx : dx + tile_cols]
            for dy in range(3)
            for dx in range(3)
        ],
        axis=3,
    )
    near_valid = near_valid.reshape(frames, count_tiles, 1, 9 * area)
    query_factor = tile_valid.reshape(frames, count_tiles, area).astype(jnp.float32)
    query_t = tile_split(queries)
    key_t = tile_split(keys)
    masks = near_valid[None].reshape(heads * frames * count_tiles, 1, 9 * area)
    spatial = attend_items(
        query_t.reshape(heads * frames * count_tiles, area, DH),
        neighbours(key_t, tile_rows, tile_cols),
        neighbours(tile_split(values), tile_rows, tile_cols),
        masks,
    )
    spatial = spatial.reshape(heads, frames, count_tiles, area, DH)
    spatial_t = (spatial * query_factor[None, :, :, :, None]).astype(jnp.bfloat16)
    triple = jnp.stack(
        [
            pad_tiles(query_t, padded_count),
            pad_tiles(key_t, padded_count),
            pad_tiles(spatial_t, padded_count),
        ]
    )
    sent = lax.all_to_all(triple, "frame", split_axis=3, concat_axis=2, tiled=True)
    query_here, key_here, value_here = (sent[0], sent[1], sent[2])
    start = frame_index * tiles_here
    length = all_frames * area
    frame_of = jnp.arange(length, dtype=jnp.int32) // area
    frame_gap = frame_of[None, :] - frame_of[:, None]
    valid_flat = tile_valid_all.reshape(all_frames, count_tiles, area).transpose(1, 0, 2)
    valid_flat = jnp.pad(
        valid_flat, ((0, padded_count - count_tiles), (0, 0), (0, 0)), constant_values=True
    )
    valid_here = lax.dynamic_slice_in_dim(valid_flat, start, tiles_here, 0)
    back_here = lax.dynamic_slice_in_dim(
        jnp.pad(back_reach.reshape(count_tiles), (0, padded_count - count_tiles)),
        start,
        tiles_here,
        0,
    )
    fwd_here = lax.dynamic_slice_in_dim(
        jnp.pad(fwd_reach.reshape(count_tiles), (0, padded_count - count_tiles)),
        start,
        tiles_here,
        0,
    )
    key_ok = valid_here.reshape(tiles_here, length)
    allowed = (
        (frame_gap[None] >= -back_here[:, None, None])
        & (frame_gap[None] <= fwd_here[:, None, None])
        & key_ok[:, None, :]
    )
    time_masks = allowed[None].reshape(heads * tiles_here, length, length)

    def by_tile(array):
        return array.transpose(0, 2, 1, 3, 4).reshape(heads * tiles_here, length, DH)

    temporal = attend_items(
        by_tile(query_here), by_tile(key_here), by_tile(value_here), time_masks
    ).astype(jnp.bfloat16)
    temporal = temporal.reshape(heads, tiles_here, all_frames, area, DH).transpose(0, 2, 1, 3, 4)
    returned = lax.all_to_all(temporal, "frame", split_axis=1, concat_axis=2, tiled=True)[
        :, :, :count_tiles
    ]
    combined = (spatial_t.astype(jnp.float32) + returned.astype(jnp.float32)) * query_factor[
        None, :, :, :, None
    ]
    combined = combined.astype(jnp.bfloat16).reshape(
        heads, frames, tile_rows, tile_cols, TS, TS, DH
    )
    return combined.transpose(1, 2, 4, 3, 5, 0, 6).reshape(frames, token_rows, token_cols, channels)


SCALE = 1.0 / math.sqrt(DH)
MASKED = -1e30
AREA = TS * TS
VMEM_LIMIT = 48 * 1024 * 1024
NT_DIMS = (((1,), (1,)), ((), ()))


def scalar_spec():
    return pl.BlockSpec(memory_space=pltpu.SMEM)


def vector_spec():
    return pl.BlockSpec(memory_space=pltpu.VMEM)


def read_tile(ref, row, col):
    return ref[pl.ds(row * TS, TS), col].reshape(AREA, DH)


def key_norms(keys):
    wide = keys.astype(jnp.float32)
    square = wide * wide
    high = square.astype(jnp.bfloat16)
    low = (square - high.astype(jnp.float32)).astype(jnp.bfloat16)
    ones = jnp.ones((8, DH), jnp.bfloat16)
    total = lax.dot_general(ones, high, NT_DIMS, preferred_element_type=jnp.float32)
    total += lax.dot_general(ones, low, NT_DIMS, preferred_element_type=jnp.float32)
    return total * (-0.5 * SCALE)


def row_valid(row, col, row_limit, col_limit):
    token = lax.broadcasted_iota(jnp.int32, (AREA, DH), 0)
    return (row * TS + (token >> 3) < row_limit) & (col * TS + (token & 7) < col_limit)


def pack_kernel(tile_rows, tile_cols, levels, me, back, fwd, keys, packed, reach, place, level):
    left = me[0] < 2
    most = [None, None, None]
    tiles = [(r, c) for r in range(tile_rows) for c in range(tile_cols)]
    for order in range(2):
        counts = [jnp.int32(0)] * 4
        for index, (r, c) in enumerate(tiles):
            toward, away = back[r, c], fwd[r, c]
            value = jnp.where(left, toward, away) if order == 0 else jnp.where(left, away, toward)
            reach[order, index] = value
            counts = [counts[v] + (value >= v).astype(jnp.int32) for v in range(4)]
        for v in (1, 2):
            most[v] = counts[v] if order == 0 else jnp.maximum(most[v], counts[v])
        spots = [counts[1], counts[2], counts[3], jnp.int32(0)]
        for index in range(len(tiles)):
            value = jnp.minimum(reach[order, index], 3)
            spot = spots[0]
            for v in (1, 2, 3):
                spot = jnp.where(value == v, spots[v], spot)
            spots = [spots[v] + (value == v).astype(jnp.int32) for v in range(4)]
            place[order, index] = spot
    chosen = jnp.int32(0)
    for one, two in levels[:-1]:
        chosen += ((most[1] > one) | (most[2] > two)).astype(jnp.int32)
    level[0] = chosen

    def pack_row(r, carry):
        for c in range(tile_cols):
            packed[place[0, r * tile_cols + c]] = read_tile(keys, r, c)
        return carry

    lax.fori_loop(0, tile_rows, pack_row, 0)


def spatial_kernel(
    tile_rows, tile_cols, me, place, rows_ok, cols_ok, queries, keys, values, mixed, packed_q,
    query_t, key_t, value_t, bias_even, bias_odd,
):
    row_limit, col_limit = rows_ok[me[0]], cols_ok[me[0]]
    wide = tile_cols * AREA
    value_t[:, DH:] = jnp.ones((value_t.shape[0], DH), jnp.bfloat16)

    def lane_bias(r, first, count):
        start = pl.multiple_of((r * tile_cols + first) * AREA, AREA)
        norms = key_norms(key_t[pl.ds(start, count * AREA)])
        lane = lax.broadcasted_iota(jnp.int32, (8, count * AREA), 1) + first * AREA
        valid = (r * TS + ((lane >> 3) & 7) < row_limit) & (
            (lane >> 6) * TS + (lane & 7) < col_limit
        )
        return jnp.where(valid, norms, MASKED)

    def retile_row(r, carry):
        for c in range(tile_cols):
            index = r * tile_cols + c
            span = pl.ds(pl.multiple_of(index * AREA, AREA), AREA)
            tile_q = read_tile(queries, r, c)
            query_t[span] = tile_q
            packed_q[place[1, index]] = tile_q
            key_t[span] = read_tile(keys, r, c)
            value_t[span, :DH] = read_tile(values, r, c)
        bias_even[r] = lane_bias(r, 0, tile_cols)
        bias_odd[r] = lane_bias(r, 1, tile_cols - 2)
        return carry

    lax.fori_loop(0, tile_rows, retile_row, 0)
    lane_tile = lax.broadcasted_iota(jnp.int32, (8, 4 * AREA), 1) >> 6

    def attend_row(r, carry):
        first_row = jnp.clip(r - 1, 0, tile_rows - 3)
        for pair in range(tile_cols // 2):
            first_col = min(max(2 * pair - 1, 0), tile_cols - 4)
            index = r * tile_cols + 2 * pair
            query = query_t[pl.ds(pl.multiple_of(index * AREA, AREA), 2 * AREA)]
            scores, spans = [], []
            for step in range(3):
                key_row = first_row + step
                start = (key_row * tile_cols + first_col) * AREA
                span = pl.ds(pl.multiple_of(start, AREA), 4 * AREA)
                spans.append(span)
                dots = lax.dot_general(
                    query, key_t[span], NT_DIMS, preferred_element_type=jnp.float32
                )
                if first_col % 2:
                    lane_start = (first_col - 1) * AREA
                    bias = bias_odd[key_row, :, lane_start : lane_start + 4 * AREA]
                else:
                    lane_start = first_col * AREA
                    bias = bias_even[key_row, :, lane_start : lane_start + 4 * AREA]
                near_row = jnp.abs(key_row - r) <= 1
                both = []
                for half in range(2):
                    gap = lane_tile + (first_col - 2 * pair - half)
                    near = (gap >= -1) & (gap <= 1) & near_row
                    part = dots[half * AREA : (half + 1) * AREA].reshape(TS, 8, 4 * AREA)
                    part = part * SCALE + jnp.where(near, bias, MASKED)[None]
                    both.append(part.reshape(AREA, 4 * AREA))
                scores.append(jnp.concatenate(both, axis=0))
            highest = jnp.maximum(jnp.maximum(scores[0], scores[1]), scores[2])
            highest = jnp.max(highest, axis=1, keepdims=True)
            total = None
            for step in range(3):
                weights = jnp.exp(scores[step] - highest).astype(jnp.bfloat16)
                part = jnp.dot(weights, value_t[spans[step]], preferred_element_type=jnp.float32)
                total = part if total is None else total + part
            result = total[:, :DH] / total[:, DH:]
            for half in range(2):
                valid = row_valid(r, 2 * pair + half, row_limit, col_limit)
                tile = jnp.where(valid, result[half * AREA : (half + 1) * AREA], 0.0)
                mixed[place[0, index + half]] = tile.astype(jnp.bfloat16)
        return carry

    lax.fori_loop(0, tile_rows, attend_row, 0)


def weights_kernel(
    tile_rows, tile_cols, one, two, me, reach, place, rows_ok, cols_ok, queries, keys, near_k,
    far_k, far_k2, hosted_q, weights,
):
    mine = me[0]
    inner = (mine == 1) | (mine == 2)
    left = mine < 2
    frames_of = (
        mine,
        jnp.where(left, 0, 3),
        jnp.where(left, 2, 1),
        jnp.where(left, 3, 0),
    )
    lane = lax.broadcasted_iota(jnp.int32, (8, 4 * AREA), 1)
    block = lane >> 6

    def by_block(picks):
        chosen = jnp.where(block == 0, picks[0], picks[1])
        chosen = jnp.where(block == 2, picks[2], chosen)
        return jnp.where(block == 3, picks[3], chosen)

    row_room = by_block([rows_ok[frame] for frame in frames_of]) - ((lane >> 3) & 7)
    col_room = by_block([cols_ok[frame] for frame in frames_of]) - (lane & 7)

    def weigh_row(r, carry):
        for c in range(tile_cols):
            index = r * tile_cols + c
            near_reach, far_reach = reach[0, index], reach[1, index]
            spot = place[1, index]
            spot_one = jnp.minimum(spot, one - 1)
            spot_two = jnp.minimum(spot, two - 1)
            keys_here = jnp.concatenate(
                [
                    read_tile(keys, r, c),
                    near_k[place[0, index]],
                    far_k[spot_one],
                    far_k2[spot_two],
                ],
                axis=0,
            )
            query = jnp.concatenate([read_tile(queries, r, c), hosted_q[spot_one]], axis=0)
            dots = lax.dot_general(query, keys_here, NT_DIMS, preferred_element_type=jnp.float32)
            norms = key_norms(keys_here)
            valid = (row_room > r * TS) & (col_room > c * TS)
            norms = jnp.where(valid, norms, MASKED)
            own_reach = (
                jnp.int32(1),
                (inner & (near_reach >= 1)).astype(jnp.int32),
                (inner & (far_reach >= 1)).astype(jnp.int32),
                (inner & (far_reach >= 2)).astype(jnp.int32),
            )
            hosted_reach = (
                (far_reach >= 1).astype(jnp.int32),
                jnp.int32(1),
                (far_reach >= 2).astype(jnp.int32),
                (far_reach >= 3).astype(jnp.int32),
            )
            for half, allowed in enumerate((own_reach, hosted_reach)):
                bias = jnp.where(by_block(allowed) > 0, norms, MASKED)
                part = dots[half * AREA : (half + 1) * AREA].reshape(TS, 8, 4 * AREA)
                part = (part * SCALE + bias[None]).reshape(AREA, 4 * AREA)
                highest = jnp.max(part, axis=1, keepdims=True)
                weights[index, half * AREA : (half + 1) * AREA] = jnp.exp(part - highest).astype(
                    jnp.bfloat16
                )
        return carry

    lax.fori_loop(0, tile_rows, weigh_row, 0)


def mix_kernel(tile_rows, tile_cols, one, two, place, weights, own_s, near_s, far_s, far_s2, own_o, hosted_o):
    ones = jnp.ones((4 * AREA, DH), jnp.bfloat16)

    def mix_row(r, carry):
        for c in range(tile_cols):
            index = r * tile_cols + c
            spot = place[1, index]
            values_here = jnp.concatenate(
                [
                    own_s[place[0, index]],
                    near_s[place[0, index]],
                    far_s[jnp.minimum(spot, one - 1)],
                    far_s2[jnp.minimum(spot, two - 1)],
                ],
                axis=0,
            )
            total = jnp.dot(
                weights[index],
                jnp.concatenate([values_here, ones], axis=1),
                preferred_element_type=jnp.float32,
            )
            result = (total[:, :DH] / total[:, DH:]).astype(jnp.bfloat16)
            own_o[index] = result[:AREA]

            @pl.when(spot < one)
            def _():
                hosted_o[spot] = result[AREA:]

        return carry

    lax.fori_loop(0, tile_rows, mix_row, 0)


def combine_kernel(
    tile_rows, tile_cols, one, me, reach, place, rows_ok, cols_ok, own_s, own_o, returned, out
):
    mine = me[0]
    outer = (mine == 0) | (mine == 3)
    row_limit, col_limit = rows_ok[mine], cols_ok[mine]

    def combine_row(r, carry):
        for c in range(tile_cols):
            index = r * tile_cols + c
            spot = jnp.minimum(place[1, index], one - 1)
            remote = outer & (reach[1, index] >= 1)
            temporal = jnp.where(remote, returned[spot], own_o[index])
            spatial = own_s[place[0, index]].astype(jnp.float32)
            valid = row_valid(r, c, row_limit, col_limit)
            tile = jnp.where(valid, spatial + temporal.astype(jnp.float32), 0.0)
            out[pl.ds(r * TS, TS), c] = tile.astype(jnp.bfloat16).reshape(TS, TS, DH)
        return carry

    lax.fori_loop(0, tile_rows, combine_row, 0)


def run_kernel(kernel, out_shape, scalars, arrays, scratch=(), scalar_outs=0, micros=4):
    outs = list(out_shape)
    specs = [vector_spec()] * (len(outs) - scalar_outs) + [scalar_spec()] * scalar_outs
    return pl.pallas_call(
        kernel,
        out_shape=outs,
        in_specs=[scalar_spec()] * len(scalars) + [vector_spec()] * len(arrays),
        out_specs=specs,
        scratch_shapes=list(scratch),
        compiler_params=pltpu.CompilerParams(vmem_limit_bytes=VMEM_LIMIT),
        cost_estimate=pl.CostEstimate(
            flops=int(micros * 1e9), bytes_accessed=int(micros * 1e6), transcendentals=0
        ),
    )(*scalars, *arrays)


def four_frames(queries, keys, values, back_reach, fwd_reach, valid_rows, valid_cols):
    _, token_rows, token_cols, _ = queries.shape
    tile_rows, tile_cols = token_rows // TS, token_cols // TS
    count = tile_rows * tile_cols
    shape = (token_rows, tile_cols, TS, DH)
    queries, keys, values = queries.reshape(shape), keys.reshape(shape), values.reshape(shape)
    me = lax.axis_index("frame").reshape(1).astype(jnp.int32)
    inward, across, outward = [(0, 1), (3, 2)], [(1, 2), (2, 1)], [(1, 0), (2, 3)]
    levels = [(count, count)]

    def tiles(number):
        return jax.ShapeDtypeStruct((number, AREA, DH), jnp.bfloat16)

    def send(array, pairs):
        return lax.ppermute(array, "frame", pairs)

    packed_k, reach, place, level = run_kernel(
        functools.partial(pack_kernel, tile_rows, tile_cols, levels),
        (
            tiles(count),
            jax.ShapeDtypeStruct((2, count), jnp.int32),
            jax.ShapeDtypeStruct((2, count), jnp.int32),
            jax.ShapeDtypeStruct((1,), jnp.int32),
        ),
        (me, back_reach, fwd_reach),
        (keys,),
        scalar_outs=3,
        micros=2,
    )

    def with_room(one, two):
        def run(queries, keys, values, packed_k, reach, place):
            near_k = send(packed_k, inward)
            far_k = send(packed_k[:one], across)
            own_s, packed_q = run_kernel(
                functools.partial(spatial_kernel, tile_rows, tile_cols),
                (tiles(count), tiles(count)),
                (me, place, valid_rows, valid_cols),
                (queries, keys, values),
                scratch=(
                    pltpu.VMEM((count * AREA, DH), jnp.bfloat16),
                    pltpu.VMEM((count * AREA, DH), jnp.bfloat16),
                    pltpu.VMEM((count * AREA, 2 * DH), jnp.bfloat16),
                    pltpu.VMEM((tile_rows, 8, tile_cols * AREA), jnp.float32),
                    pltpu.VMEM((tile_rows, 8, (tile_cols - 2) * AREA), jnp.float32),
                ),
                micros=10,
            )
            near_s = send(own_s, inward)
            far_s = send(own_s[:one], across)
            far_k2 = send(near_k[:two], across)
            hosted_q = send(packed_q[:one], inward)
            far_s2 = send(near_s[:two], across)
            (weights,) = run_kernel(
                functools.partial(weights_kernel, tile_rows, tile_cols, one, two),
                (jax.ShapeDtypeStruct((count, 2 * AREA, 4 * AREA), jnp.bfloat16),),
                (me, reach, place, valid_rows, valid_cols),
                (queries, keys, near_k, far_k, far_k2, hosted_q),
                micros=5,
            )
            own_o, hosted_o = run_kernel(
                functools.partial(mix_kernel, tile_rows, tile_cols, one, two),
                (tiles(count), tiles(one)),
                (place,),
                (weights, own_s, near_s, far_s, far_s2),
                micros=4,
            )
            returned = send(hosted_o, outward)
            (out,) = run_kernel(
                functools.partial(combine_kernel, tile_rows, tile_cols, one),
                (jax.ShapeDtypeStruct(shape, jnp.bfloat16),),
                (me, reach, place, valid_rows, valid_cols),
                (own_s, own_o, returned),
                micros=2,
            )
            return out

        return run

    branches = [with_room(one, two) for one, two in levels]
    operands = (queries, keys, values, packed_k, reach, place)
    if len(branches) == 1:
        out = branches[0](*operands)
    else:
        out = lax.switch(level[0], branches, *operands)
    return out.reshape(1, token_rows, token_cols, DH)


def solution(mesh):
    in_specs = (
        P(("dp", "frame"), None, None, "row"),
        P(("dp", "frame"), None, None, "row"),
        P(("dp", "frame"), None, None, "row"),
        P("dp", None),
        P("dp", None),
        P("dp"),
        P("dp"),
    )
    out_specs = P(("dp", "frame"), None, None, "row")

    def block(*args):
        frames, _, token_cols, channels = args[0].shape
        line = mesh.shape["frame"] == 4 and frames == 1 and channels == DH
        if line and token_cols % (2 * TS) == 0 and token_cols // TS >= 4:
            return four_frames(*args)
        return per_device(*args)

    return jax.shard_map(
        block, mesh=mesh, in_specs=in_specs, out_specs=out_specs, check_vma=False
    )
```

```python
import functools
import math

import jax
import jax.numpy as jnp
from jax import lax
from jax.experimental import pallas as pl
from jax.experimental.pallas import tpu as pltpu
from jax.sharding import PartitionSpec as P

DH = 128
TS = 8


def group_size(item_count, row_count):
    size = 1
    for option in range(1, item_count + 1):
        if item_count % option == 0 and option * row_count <= 1024:
            size = option
    return size


def attend_group(group_parts):
    query_rows, key_rows, value_rows, allowed = group_parts
    dot_terms = jnp.einsum("gmd,gnd->gmn", query_rows, key_rows, preferred_element_type=jnp.float32)
    query_sq = jnp.einsum("gmd,gmd->gm", query_rows, query_rows, preferred_element_type=jnp.float32)
    key_sq = jnp.einsum("gnd,gnd->gn", key_rows, key_rows, preferred_element_type=jnp.float32)
    distance = query_sq[:, :, None] + key_sq[:, None, :] - 2.0 * dot_terms
    scores = jnp.where(allowed, -distance * (0.5 / math.sqrt(query_rows.shape[2])), -jnp.inf)
    highest = jnp.max(scores, axis=2, keepdims=True)
    weights = jnp.exp(scores - highest)
    totals = jnp.sum(weights, axis=2, keepdims=True)
    mixed = jnp.einsum(
        "gmn,gnd->gmd", weights.astype(jnp.bfloat16), value_rows, preferred_element_type=jnp.float32
    )
    return mixed / totals


def attend_items(query_items, key_items, value_items, masks):
    item_count = query_items.shape[0]
    per_group = group_size(item_count, query_items.shape[1])
    groups = item_count // per_group

    def regroup(array):
        return array.reshape((groups, per_group) + array.shape[1:])

    mixed = lax.map(
        attend_group,
        (regroup(query_items), regroup(key_items), regroup(value_items), regroup(masks)),
    )
    return mixed.reshape((item_count,) + mixed.shape[2:])


def tile_split(block):
    frames, token_rows, token_cols, channels = block.shape
    heads = channels // DH
    return (
        block.reshape(frames, token_rows // TS, TS, token_cols // TS, TS, heads, DH)
        .transpose(5, 0, 1, 3, 2, 4, 6)
        .reshape(heads, frames, token_rows // TS * (token_cols // TS), TS * TS, DH)
    )


def neighbours(tiles, tile_rows, tile_cols):
    heads, frames, count_tiles, area, depth = tiles.shape
    grid = tiles.reshape(heads * frames, tile_rows, tile_cols, area, depth)
    padded = jnp.pad(grid, ((0, 0), (1, 1), (1, 1), (0, 0), (0, 0)))
    views = [
        padded[:, dy : dy + tile_rows, dx : dx + tile_cols] for dy in range(3) for dx in range(3)
    ]
    stacked = jnp.stack(views, axis=3)
    return stacked.reshape(heads * frames * count_tiles, 9 * area, depth)


def pad_tiles(tiles, total):
    return jnp.pad(tiles, ((0, 0), (0, 0), (0, total - tiles.shape[2]), (0, 0), (0, 0)))


def per_device(queries, keys, values, back_reach, fwd_reach, valid_rows, valid_cols):
    frames, token_rows, token_cols, channels = queries.shape
    heads = channels // DH
    tile_rows = token_rows // TS
    tile_cols = token_cols // TS
    count_tiles = tile_rows * tile_cols
    area = TS * TS
    frame_count = lax.axis_size("frame")
    frame_index = lax.axis_index("frame")
    padded_count = (count_tiles + frame_count - 1) // frame_count * frame_count
    tiles_here = padded_count // frame_count
    all_frames = frames * frame_count
    row_ids = jnp.arange(token_rows, dtype=jnp.int32)
    col_ids = jnp.arange(token_cols, dtype=jnp.int32)
    row_ok = row_ids[None, :] < valid_rows[:, None]
    col_ok = col_ids[None, :] < valid_cols[:, None]
    token_valid = row_ok[:, :, None] & col_ok[:, None, :]
    tile_valid_all = (
        token_valid.reshape(all_frames, tile_rows, TS, tile_cols, TS)
        .transpose(0, 1, 3, 2, 4)
        .reshape(all_frames, tile_rows, tile_cols, area)
    )
    tile_valid = lax.dynamic_slice_in_dim(tile_valid_all, frame_index * frames, frames, 0)
    padded_valid = jnp.pad(tile_valid, ((0, 0), (1, 1), (1, 1), (0, 0)))
    near_valid = jnp.stack(
        [
            padded_valid[:, dy : dy + tile_rows, dx : dx + tile_cols]
            for dy in range(3)
            for dx in range(3)
        ],
        axis=3,
    )
    near_valid = near_valid.reshape(frames, count_tiles, 1, 9 * area)
    query_factor = tile_valid.reshape(frames, count_tiles, area).astype(jnp.float32)
    query_t = tile_split(queries)
    key_t = tile_split(keys)
    masks = near_valid[None].reshape(heads * frames * count_tiles, 1, 9 * area)
    spatial = attend_items(
        query_t.reshape(heads * frames * count_tiles, area, DH),
        neighbours(key_t, tile_rows, tile_cols),
        neighbours(tile_split(values), tile_rows, tile_cols),
        masks,
    )
    spatial = spatial.reshape(heads, frames, count_tiles, area, DH)
    spatial_t = (spatial * query_factor[None, :, :, :, None]).astype(jnp.bfloat16)
    triple = jnp.stack(
        [
            pad_tiles(query_t, padded_count),
            pad_tiles(key_t, padded_count),
            pad_tiles(spatial_t, padded_count),
        ]
    )
    sent = lax.all_to_all(triple, "frame", split_axis=3, concat_axis=2, tiled=True)
    query_here, key_here, value_here = (sent[0], sent[1], sent[2])
    start = frame_index * tiles_here
    length = all_frames * area
    frame_of = jnp.arange(length, dtype=jnp.int32) // area
    frame_gap = frame_of[None, :] - frame_of[:, None]
    valid_flat = tile_valid_all.reshape(all_frames, count_tiles, area).transpose(1, 0, 2)
    valid_flat = jnp.pad(
        valid_flat, ((0, padded_count - count_tiles), (0, 0), (0, 0)), constant_values=True
    )
    valid_here = lax.dynamic_slice_in_dim(valid_flat, start, tiles_here, 0)
    back_here = lax.dynamic_slice_in_dim(
        jnp.pad(back_reach.reshape(count_tiles), (0, padded_count - count_tiles)),
        start,
        tiles_here,
        0,
    )
    fwd_here = lax.dynamic_slice_in_dim(
        jnp.pad(fwd_reach.reshape(count_tiles), (0, padded_count - count_tiles)),
        start,
        tiles_here,
        0,
    )
    key_ok = valid_here.reshape(tiles_here, length)
    allowed = (
        (frame_gap[None] >= -back_here[:, None, None])
        & (frame_gap[None] <= fwd_here[:, None, None])
        & key_ok[:, None, :]
    )
    time_masks = allowed[None].reshape(heads * tiles_here, length, length)

    def by_tile(array):
        return array.transpose(0, 2, 1, 3, 4).reshape(heads * tiles_here, length, DH)

    temporal = attend_items(
        by_tile(query_here), by_tile(key_here), by_tile(value_here), time_masks
    ).astype(jnp.bfloat16)
    temporal = temporal.reshape(heads, tiles_here, all_frames, area, DH).transpose(0, 2, 1, 3, 4)
    returned = lax.all_to_all(temporal, "frame", split_axis=1, concat_axis=2, tiled=True)[
        :, :, :count_tiles
    ]
    combined = (spatial_t.astype(jnp.float32) + returned.astype(jnp.float32)) * query_factor[
        None, :, :, :, None
    ]
    combined = combined.astype(jnp.bfloat16).reshape(
        heads, frames, tile_rows, tile_cols, TS, TS, DH
    )
    return combined.transpose(1, 2, 4, 3, 5, 0, 6).reshape(frames, token_rows, token_cols, channels)


SCALE = 1.0 / math.sqrt(DH)
MASKED = -1e30
AREA = TS * TS
VMEM_LIMIT = 48 * 1024 * 1024
NT_DIMS = (((1,), (1,)), ((), ()))


def scalar_spec():
    return pl.BlockSpec(memory_space=pltpu.SMEM)


def vector_spec():
    return pl.BlockSpec(memory_space=pltpu.VMEM)


def read_tile(ref, row, col):
    return ref[pl.ds(row * TS, TS), col].reshape(AREA, DH)


def key_norms(keys):
    wide = keys.astype(jnp.float32)
    square = wide * wide
    high = square.astype(jnp.bfloat16)
    low = (square - high.astype(jnp.float32)).astype(jnp.bfloat16)
    ones = jnp.ones((8, DH), jnp.bfloat16)
    total = lax.dot_general(ones, high, NT_DIMS, preferred_element_type=jnp.float32)
    total += lax.dot_general(ones, low, NT_DIMS, preferred_element_type=jnp.float32)
    return total * (-0.5 * SCALE)


def row_valid(row, col, row_limit, col_limit):
    token = lax.broadcasted_iota(jnp.int32, (AREA, DH), 0)
    return (row * TS + (token >> 3) < row_limit) & (col * TS + (token & 7) < col_limit)


def pack_kernel(
    tile_rows, tile_cols, levels, me, back, fwd, keys, packed, reach, place, order, level, held, sem
):
    load = pltpu.make_async_copy(keys, held, sem)
    load.start()
    left = me[0] < 2
    most = [None] * 4
    tiles = [(r, c) for r in range(tile_rows) for c in range(tile_cols)]
    for way in range(2):
        counts = [jnp.int32(0)] * 4
        for index, (r, c) in enumerate(tiles):
            toward, away = back[r, c], fwd[r, c]
            value = jnp.where(left, toward, away) if way == 0 else jnp.where(left, away, toward)
            reach[way, index] = value
            counts = [counts[v] + (value >= v).astype(jnp.int32) for v in range(4)]
        for v in (1, 2, 3):
            most[v] = counts[v] if way == 0 else jnp.maximum(most[v], counts[v])
        spots = [counts[1], counts[2], counts[3], jnp.int32(0)]
        for index in range(len(tiles)):
            value = jnp.minimum(reach[way, index], 3)
            spot = spots[0]
            for v in (1, 2, 3):
                spot = jnp.where(value == v, spots[v], spot)
            spots = [spots[v] + (value == v).astype(jnp.int32) for v in range(4)]
            place[way, index] = spot
            if way == 1:
                order[spot] = index
    chosen = jnp.int32(0)
    for one, two, three in levels[:-1]:
        over = (most[1] > one) | (most[2] > two) | (most[3] > three)
        chosen += over.astype(jnp.int32)
    level[0] = chosen
    load.wait()

    def pack_row(r, carry):
        for c in range(tile_cols):
            packed[place[0, r * tile_cols + c]] = read_tile(held, r, c)
        return carry

    lax.fori_loop(0, tile_rows, pack_row, 0)


def spatial_kernel(
    tile_rows, tile_cols, me, place, rows_ok, cols_ok, queries, keys, values, mixed, packed_q,
    query_t, key_t, value_t, bias_even, bias_odd,
):
    row_limit, col_limit = rows_ok[me[0]], cols_ok[me[0]]
    wide = tile_cols * AREA
    value_t[:, DH:] = jnp.ones((value_t.shape[0], DH), jnp.bfloat16)

    def lane_bias(r, first, count):
        start = pl.multiple_of((r * tile_cols + first) * AREA, AREA)
        norms = key_norms(key_t[pl.ds(start, count * AREA)])
        lane = lax.broadcasted_iota(jnp.int32, (8, count * AREA), 1) + first * AREA
        valid = (r * TS + ((lane >> 3) & 7) < row_limit) & (
            (lane >> 6) * TS + (lane & 7) < col_limit
        )
        return jnp.where(valid, norms, MASKED)

    def retile_row(r, carry):
        for c in range(tile_cols):
            index = r * tile_cols + c
            span = pl.ds(pl.multiple_of(index * AREA, AREA), AREA)
            tile_q = read_tile(queries, r, c)
            query_t[span] = tile_q
            packed_q[place[1, index]] = tile_q
            key_t[span] = read_tile(keys, r, c)
            value_t[span, :DH] = read_tile(values, r, c)
        bias_even[r] = lane_bias(r, 0, tile_cols)
        bias_odd[r] = lane_bias(r, 1, tile_cols - 2)
        return carry

    lax.fori_loop(0, tile_rows, retile_row, 0)
    lane_tile = lax.broadcasted_iota(jnp.int32, (8, 4 * AREA), 1) >> 6

    def attend_row(r, carry):
        first_row = jnp.clip(r - 1, 0, tile_rows - 3)
        for pair in range(tile_cols // 2):
            first_col = min(max(2 * pair - 1, 0), tile_cols - 4)
            index = r * tile_cols + 2 * pair
            query = query_t[pl.ds(pl.multiple_of(index * AREA, AREA), 2 * AREA)]
            scores, spans = [], []
            for step in range(3):
                key_row = first_row + step
                start = (key_row * tile_cols + first_col) * AREA
                span = pl.ds(pl.multiple_of(start, AREA), 4 * AREA)
                spans.append(span)
                dots = lax.dot_general(
                    query, key_t[span], NT_DIMS, preferred_element_type=jnp.float32
                )
                if first_col % 2:
                    lane_start = (first_col - 1) * AREA
                    bias = bias_odd[key_row, :, lane_start : lane_start + 4 * AREA]
                else:
                    lane_start = first_col * AREA
                    bias = bias_even[key_row, :, lane_start : lane_start + 4 * AREA]
                near_row = jnp.abs(key_row - r) <= 1
                both = []
                for half in range(2):
                    gap = lane_tile + (first_col - 2 * pair - half)
                    near = (gap >= -1) & (gap <= 1) & near_row
                    part = dots[half * AREA : (half + 1) * AREA].reshape(TS, 8, 4 * AREA)
                    part = part * SCALE + jnp.where(near, bias, MASKED)[None]
                    both.append(part.reshape(AREA, 4 * AREA))
                scores.append(jnp.concatenate(both, axis=0))
            highest = jnp.maximum(jnp.maximum(scores[0], scores[1]), scores[2])
            highest = jnp.max(highest, axis=1, keepdims=True)
            total = None
            for step in range(3):
                weights = jnp.exp(scores[step] - highest).astype(jnp.bfloat16)
                part = jnp.dot(weights, value_t[spans[step]], preferred_element_type=jnp.float32)
                total = part if total is None else total + part
            result = total[:, :DH] / total[:, DH:]
            for half in range(2):
                valid = row_valid(r, 2 * pair + half, row_limit, col_limit)
                tile = jnp.where(valid, result[half * AREA : (half + 1) * AREA], 0.0)
                mixed[place[0, index + half]] = tile.astype(jnp.bfloat16)
        return carry

    lax.fori_loop(0, tile_rows, attend_row, 0)


def frames_of(mine):
    left = mine < 2
    return mine, jnp.where(left, 0, 3), jnp.where(left, 2, 1), jnp.where(left, 3, 0)


def by_block(picks, lanes):
    block = lax.broadcasted_iota(jnp.int32, (8, lanes), 1) >> 6
    chosen = jnp.full((8, lanes), picks[0], jnp.int32)
    for number in range(1, lanes // AREA):
        chosen = jnp.where(block == number, picks[number], chosen)
    return chosen


def room_left(frames, rows_ok, cols_ok, lanes):
    lane = lax.broadcasted_iota(jnp.int32, (8, lanes), 1)
    row_room = by_block([rows_ok[frame] for frame in frames], lanes) - ((lane >> 3) & 7)
    col_room = by_block([cols_ok[frame] for frame in frames], lanes) - (lane & 7)
    return row_room, col_room


def weigh(query, keys_here, allowed, room, row, col):
    lanes = keys_here.shape[0]
    dots = lax.dot_general(query, keys_here, NT_DIMS, preferred_element_type=jnp.float32)
    valid = (room[0] > row * TS) & (room[1] > col * TS) & (by_block(allowed, lanes) > 0)
    bias = jnp.where(valid, key_norms(keys_here), MASKED)
    part = (dots.reshape(TS, 8, lanes) * SCALE + bias[None]).reshape(AREA, lanes)
    highest = jnp.max(part, axis=1, keepdims=True)
    return jnp.exp(part - highest), highest


def mix(weights, values_here):
    ones = jnp.ones(values_here.shape, jnp.bfloat16)
    total = jnp.dot(
        weights,
        jnp.concatenate([values_here, ones], axis=1),
        preferred_element_type=jnp.float32,
    )
    return total[:, :DH], total[:, DH:]


def in_chunks(first, last, body, carry):
    size = max(option for option in (6, 5, 4, 3, 2, 1) if (last - first) % option == 0)

    def chunk(number, carry):
        for step in range(size):
            carry = body(first + number * size + step, carry)
        return carry

    return lax.fori_loop(0, (last - first) // size, chunk, carry)


def hosted_kernel(
    tile_cols, one, two, three, me, reach, place, order, rows_ok, cols_ok, hosted_q, packed_k,
    far_k, far_k2, own_s, far_s, mixed, weights,
):
    own, _, far, far2 = frames_of(me[0])
    short = room_left((own, far), rows_ok, cols_ok, 2 * AREA)
    full = room_left((own, far, far2, own), rows_ok, cols_ok, 4 * AREA)
    lane = lax.broadcasted_iota(jnp.int32, (AREA, DH), 1)
    no = jnp.int32(0)

    def reached(index, least):
        return (reach[1, index] >= least).astype(jnp.int32)

    def near_ones(spot, sums):
        index = order[spot]
        row = lax.div(index, tile_cols)
        home = place[0, index]
        keys_here = jnp.concatenate([packed_k[home], far_k[spot]], axis=0)
        allowed = (reached(index, 1), reached(index, 2))
        part, highest = weigh(
            hosted_q[spot], keys_here, allowed, short, row, index - row * tile_cols
        )
        values_here = jnp.concatenate([own_s[home], far_s[spot]], axis=0)
        total, sum_here = mix(part.astype(jnp.bfloat16), values_here)
        mixed[spot - three] = (total / sum_here).astype(jnp.bfloat16)
        return jnp.where(lane == spot, highest + jnp.log(sum_here), sums)

    def far_ones(spot, sums):
        index = order[spot]
        row = lax.div(index, tile_cols)
        home = packed_k[place[0, index]]
        keys_here = jnp.concatenate([home, far_k[spot], far_k2[spot], home], axis=0)
        allowed = (reached(index, 1), reached(index, 2), reached(index, 3), no)
        part, highest = weigh(
            hosted_q[spot], keys_here, allowed, full, row, index - row * tile_cols
        )
        weights[spot] = part.astype(jnp.bfloat16)
        sum_here = jnp.sum(part, axis=1, keepdims=True)
        return jnp.where(lane == spot, highest + jnp.log(sum_here), sums)

    sums = jnp.zeros((AREA, DH), jnp.float32)
    if one > three:
        sums = in_chunks(three, one, near_ones, sums)
    sums = in_chunks(0, three, far_ones, sums)
    for step in range(3):
        piece = sums.astype(jnp.bfloat16)
        mixed[one - three + step] = piece
        sums = sums - piece.astype(jnp.float32)


def far_mix_kernel(three, place, order, weights, own_s, far_s, far_s2, mixed):
    def far_ones(spot, carry):
        home = own_s[place[0, order[spot]]]
        values_here = jnp.concatenate([home, far_s[spot], far_s2[spot], home], axis=0)
        total, sum_here = mix(weights[spot], values_here)
        mixed[spot] = (total / sum_here).astype(jnp.bfloat16)
        return carry

    in_chunks(0, three, far_ones, 0)


def own_kernel(
    tile_rows, tile_cols, one, two, me, reach, place, rows_ok, cols_ok, queries, keys, near_k,
    far_k, far_k2, own_s, near_s, far_s, far_s2, mixed, sums_out,
):
    mine = me[0]
    inner = (mine == 1) | (mine == 2)
    room = room_left(frames_of(mine), rows_ok, cols_ok, 4 * AREA)
    lane = lax.broadcasted_iota(jnp.int32, (AREA, DH), 1)

    def own_row(r, sums):
        for c in range(tile_cols):
            index = r * tile_cols + c
            home = place[0, index]
            near = jnp.minimum(home, one - 1)
            far = jnp.minimum(place[1, index], one - 1)
            far2 = jnp.minimum(place[1, index], two - 1)
            near_reach, far_reach = reach[0, index], reach[1, index]
            allowed = (
                jnp.int32(1),
                (inner & (near_reach >= 1)).astype(jnp.int32),
                (inner & (far_reach >= 1)).astype(jnp.int32),
                (inner & (far_reach >= 2)).astype(jnp.int32),
            )
            keys_here = jnp.concatenate(
                [read_tile(keys, r, c), near_k[near], far_k[far], far_k2[far2]], axis=0
            )
            part, highest = weigh(read_tile(queries, r, c), keys_here, allowed, room, r, c)
            values_here = jnp.concatenate(
                [own_s[home], near_s[near], far_s[far], far_s2[far2]], axis=0
            )
            total, sum_here = mix(part.astype(jnp.bfloat16), values_here)
            mixed[index] = (total / sum_here).astype(jnp.bfloat16)
            sums = jnp.where(lane == index, highest + jnp.log(sum_here), sums)
        return sums

    sums_out[...] = lax.fori_loop(0, tile_rows, own_row, jnp.zeros((AREA, DH), jnp.float32))


def combine_kernel(
    tile_rows, tile_cols, one, three, me, reach, place, rows_ok, cols_ok, own_s, own_o, own_sums,
    near_ones, far_ones, out,
):
    mine = me[0]
    outer = (mine == 0) | (mine == 3)
    row_limit, col_limit = rows_ok[mine], cols_ok[mine]
    lane = lax.broadcasted_iota(jnp.int32, (AREA, DH), 1)
    their_sums = near_ones[one - three].astype(jnp.float32)
    their_sums += near_ones[one - three + 1].astype(jnp.float32)
    their_sums += near_ones[one - three + 2].astype(jnp.float32)
    my_sums = own_sums[...]

    def combine_row(r, carry):
        for c in range(tile_cols):
            index = r * tile_cols + c
            spot = jnp.minimum(place[1, index], one - 1)
            remote = outer & (reach[1, index] >= 1)
            gap = jnp.where(lane == spot, their_sums, 0.0) - jnp.where(lane == index, my_sums, 0.0)
            gap = jnp.sum(gap, axis=1, keepdims=True)
            share = 1.0 / (1.0 + jnp.exp(gap))
            share = jnp.where(remote, share, 1.0)
            theirs = far_ones[jnp.minimum(spot, three - 1)].astype(jnp.float32)
            if one > three:
                other = near_ones[jnp.maximum(spot - three, 0)].astype(jnp.float32)
                theirs = jnp.where(spot < three, theirs, other)
            mine_o = own_o[index].astype(jnp.float32)
            temporal = jnp.where(remote, share * mine_o + (1.0 - share) * theirs, mine_o)
            temporal = temporal.astype(jnp.bfloat16).astype(jnp.float32)
            spatial = own_s[place[0, index]].astype(jnp.float32)
            valid = row_valid(r, c, row_limit, col_limit)
            tile = jnp.where(valid, spatial + temporal, 0.0)
            out[pl.ds(r * TS, TS), c] = tile.astype(jnp.bfloat16).reshape(TS, TS, DH)
        return carry

    lax.fori_loop(0, tile_rows, combine_row, 0)


def run_kernel(
    kernel, out_shape, scalars, arrays, scratch=(), scalar_outs=0, micros=4, in_place=False
):
    outs = list(out_shape)
    specs = [vector_spec()] * (len(outs) - scalar_outs) + [scalar_spec()] * scalar_outs
    array_spec = pl.BlockSpec(memory_space=pl.ANY) if in_place else vector_spec()
    return pl.pallas_call(
        kernel,
        out_shape=outs,
        in_specs=[scalar_spec()] * len(scalars) + [array_spec] * len(arrays),
        out_specs=specs,
        scratch_shapes=list(scratch),
        compiler_params=pltpu.CompilerParams(vmem_limit_bytes=VMEM_LIMIT),
        cost_estimate=pl.CostEstimate(
            flops=int(micros * 1e9), bytes_accessed=int(micros * 1e6), transcendentals=0
        ),
    )(*scalars, *arrays)


def room_levels(count):
    shares = ((45, 30, 15), (48, 33, 18), (51, 36, 21), (54, 39, 24), (57, 45, 30))
    levels = [tuple(max(count * share // 60, 1) for share in level) for level in shares]
    return levels + [(count, count, count)]


def four_frames(queries, keys, values, back_reach, fwd_reach, valid_rows, valid_cols):
    _, token_rows, token_cols, _ = queries.shape
    tile_rows, tile_cols = token_rows // TS, token_cols // TS
    count = tile_rows * tile_cols
    shape = (token_rows, tile_cols, TS, DH)
    queries, keys, values = queries.reshape(shape), keys.reshape(shape), values.reshape(shape)
    me = lax.axis_index("frame").reshape(1).astype(jnp.int32)
    inward, across, outward = [(0, 1), (3, 2)], [(1, 2), (2, 1)], [(1, 0), (2, 3)]
    levels = room_levels(count)

    def tiles(number):
        return jax.ShapeDtypeStruct((number, AREA, DH), jnp.bfloat16)

    def ints(*sizes):
        return jax.ShapeDtypeStruct(sizes, jnp.int32)

    def send(array, pairs):
        return lax.ppermute(array, "frame", pairs)

    packed_k, reach, place, order, level = run_kernel(
        functools.partial(pack_kernel, tile_rows, tile_cols, levels),
        (tiles(count), ints(2, count), ints(2, count), ints(count), ints(1)),
        (me, back_reach, fwd_reach),
        (keys,),
        scratch=(pltpu.VMEM(shape, jnp.bfloat16), pltpu.SemaphoreType.DMA),
        scalar_outs=4,
        micros=2,
        in_place=True,
    )

    def with_room(one, two, three):
        def run(queries, keys, values, packed_k, reach, place, order):
            near_k = send(packed_k[:one], inward)
            far_k = send(packed_k[:one], across)
            own_s, packed_q = run_kernel(
                functools.partial(spatial_kernel, tile_rows, tile_cols),
                (tiles(count), tiles(count)),
                (me, place, valid_rows, valid_cols),
                (queries, keys, values),
                scratch=(
                    pltpu.VMEM((count * AREA, DH), jnp.bfloat16),
                    pltpu.VMEM((count * AREA, DH), jnp.bfloat16),
                    pltpu.VMEM((count * AREA, 2 * DH), jnp.bfloat16),
                    pltpu.VMEM((tile_rows, 8, tile_cols * AREA), jnp.float32),
                    pltpu.VMEM((tile_rows, 8, (tile_cols - 2) * AREA), jnp.float32),
                ),
                micros=10,
            )
            near_s = send(own_s[:one], inward)
            far_s = send(own_s[:one], across)
            packed_q, far_k = lax.optimization_barrier((packed_q, far_k))
            hosted_q = send(packed_q[:one], inward)
            far_k2 = send(near_k[:two], across)
            far_s2 = send(near_s[:two], across)
            hosted_a, hosted_w = run_kernel(
                functools.partial(hosted_kernel, tile_cols, one, two, three),
                (
                    tiles(one - three + 3),
                    jax.ShapeDtypeStruct((three, AREA, 4 * AREA), jnp.bfloat16),
                ),
                (me, reach, place, order, valid_rows, valid_cols),
                (hosted_q, packed_k, far_k, far_k2, own_s, far_s),
                micros=5,
            )
            returned_a = send(hosted_a, outward)
            (hosted_b,) = run_kernel(
                functools.partial(far_mix_kernel, three),
                (tiles(three),),
                (place, order),
                (hosted_w, own_s, far_s, far_s2),
                micros=2,
            )
            returned_b = send(hosted_b, outward)
            own_o, own_sums = run_kernel(
                functools.partial(own_kernel, tile_rows, tile_cols, one, two),
                (tiles(count), jax.ShapeDtypeStruct((AREA, DH), jnp.float32)),
                (me, reach, place, valid_rows, valid_cols),
                (queries, keys, near_k, far_k, far_k2, own_s, near_s, far_s, far_s2),
                micros=7,
            )
            (out,) = run_kernel(
                functools.partial(combine_kernel, tile_rows, tile_cols, one, three),
                (jax.ShapeDtypeStruct(shape, jnp.bfloat16),),
                (me, reach, place, valid_rows, valid_cols),
                (own_s, own_o, own_sums, returned_a, returned_b),
                micros=2,
            )
            return out

        return run

    branches = [with_room(*level) for level in levels]
    operands = (queries, keys, values, packed_k, reach, place, order)
    out = lax.switch(level[0], branches, *operands)
    return out.reshape(1, token_rows, token_cols, DH)


def solution(mesh):
    in_specs = (
        P(("dp", "frame"), None, None, "row"),
        P(("dp", "frame"), None, None, "row"),
        P(("dp", "frame"), None, None, "row"),
        P("dp", None),
        P("dp", None),
        P("dp"),
        P("dp"),
    )
    out_specs = P(("dp", "frame"), None, None, "row")

    def block(*args):
        frames, _, token_cols, channels = args[0].shape
        line = mesh.shape["frame"] == 4 and frames == 1 and channels == DH
        if line and token_cols % (2 * TS) == 0 and 4 <= token_cols // TS:
            return four_frames(*args)
        return per_device(*args)

    return jax.shard_map(
        block, mesh=mesh, in_specs=in_specs, out_specs=out_specs, check_vma=False
    )
```

```python
import functools
import math

import jax
import jax.numpy as jnp
from jax import lax
from jax.experimental import pallas as pl
from jax.experimental.pallas import tpu as pltpu
from jax.sharding import PartitionSpec as P

DH = 128
TS = 8


def group_size(item_count, row_count):
    size = 1
    for option in range(1, item_count + 1):
        if item_count % option == 0 and option * row_count <= 1024:
            size = option
    return size


def attend_group(group_parts):
    query_rows, key_rows, value_rows, allowed = group_parts
    dot_terms = jnp.einsum("gmd,gnd->gmn", query_rows, key_rows, preferred_element_type=jnp.float32)
    query_sq = jnp.einsum("gmd,gmd->gm", query_rows, query_rows, preferred_element_type=jnp.float32)
    key_sq = jnp.einsum("gnd,gnd->gn", key_rows, key_rows, preferred_element_type=jnp.float32)
    distance = query_sq[:, :, None] + key_sq[:, None, :] - 2.0 * dot_terms
    scores = jnp.where(allowed, -distance * (0.5 / math.sqrt(query_rows.shape[2])), -jnp.inf)
    highest = jnp.max(scores, axis=2, keepdims=True)
    weights = jnp.exp(scores - highest)
    totals = jnp.sum(weights, axis=2, keepdims=True)
    mixed = jnp.einsum(
        "gmn,gnd->gmd", weights.astype(jnp.bfloat16), value_rows, preferred_element_type=jnp.float32
    )
    return mixed / totals


def attend_items(query_items, key_items, value_items, masks):
    item_count = query_items.shape[0]
    per_group = group_size(item_count, query_items.shape[1])
    groups = item_count // per_group

    def regroup(array):
        return array.reshape((groups, per_group) + array.shape[1:])

    mixed = lax.map(
        attend_group,
        (regroup(query_items), regroup(key_items), regroup(value_items), regroup(masks)),
    )
    return mixed.reshape((item_count,) + mixed.shape[2:])


def tile_split(block):
    frames, token_rows, token_cols, channels = block.shape
    heads = channels // DH
    return (
        block.reshape(frames, token_rows // TS, TS, token_cols // TS, TS, heads, DH)
        .transpose(5, 0, 1, 3, 2, 4, 6)
        .reshape(heads, frames, token_rows // TS * (token_cols // TS), TS * TS, DH)
    )


def neighbours(tiles, tile_rows, tile_cols):
    heads, frames, count_tiles, area, depth = tiles.shape
    grid = tiles.reshape(heads * frames, tile_rows, tile_cols, area, depth)
    padded = jnp.pad(grid, ((0, 0), (1, 1), (1, 1), (0, 0), (0, 0)))
    views = [
        padded[:, dy : dy + tile_rows, dx : dx + tile_cols] for dy in range(3) for dx in range(3)
    ]
    stacked = jnp.stack(views, axis=3)
    return stacked.reshape(heads * frames * count_tiles, 9 * area, depth)


def pad_tiles(tiles, total):
    return jnp.pad(tiles, ((0, 0), (0, 0), (0, total - tiles.shape[2]), (0, 0), (0, 0)))


def per_device(queries, keys, values, back_reach, fwd_reach, valid_rows, valid_cols):
    frames, token_rows, token_cols, channels = queries.shape
    heads = channels // DH
    tile_rows = token_rows // TS
    tile_cols = token_cols // TS
    count_tiles = tile_rows * tile_cols
    area = TS * TS
    frame_count = lax.axis_size("frame")
    frame_index = lax.axis_index("frame")
    padded_count = (count_tiles + frame_count - 1) // frame_count * frame_count
    tiles_here = padded_count // frame_count
    all_frames = frames * frame_count
    row_ids = jnp.arange(token_rows, dtype=jnp.int32)
    col_ids = jnp.arange(token_cols, dtype=jnp.int32)
    row_ok = row_ids[None, :] < valid_rows[:, None]
    col_ok = col_ids[None, :] < valid_cols[:, None]
    token_valid = row_ok[:, :, None] & col_ok[:, None, :]
    tile_valid_all = (
        token_valid.reshape(all_frames, tile_rows, TS, tile_cols, TS)
        .transpose(0, 1, 3, 2, 4)
        .reshape(all_frames, tile_rows, tile_cols, area)
    )
    tile_valid = lax.dynamic_slice_in_dim(tile_valid_all, frame_index * frames, frames, 0)
    padded_valid = jnp.pad(tile_valid, ((0, 0), (1, 1), (1, 1), (0, 0)))
    near_valid = jnp.stack(
        [
            padded_valid[:, dy : dy + tile_rows, dx : dx + tile_cols]
            for dy in range(3)
            for dx in range(3)
        ],
        axis=3,
    )
    near_valid = near_valid.reshape(frames, count_tiles, 1, 9 * area)
    query_factor = tile_valid.reshape(frames, count_tiles, area).astype(jnp.float32)
    query_t = tile_split(queries)
    key_t = tile_split(keys)
    masks = near_valid[None].reshape(heads * frames * count_tiles, 1, 9 * area)
    spatial = attend_items(
        query_t.reshape(heads * frames * count_tiles, area, DH),
        neighbours(key_t, tile_rows, tile_cols),
        neighbours(tile_split(values), tile_rows, tile_cols),
        masks,
    )
    spatial = spatial.reshape(heads, frames, count_tiles, area, DH)
    spatial_t = (spatial * query_factor[None, :, :, :, None]).astype(jnp.bfloat16)
    triple = jnp.stack(
        [
            pad_tiles(query_t, padded_count),
            pad_tiles(key_t, padded_count),
            pad_tiles(spatial_t, padded_count),
        ]
    )
    sent = lax.all_to_all(triple, "frame", split_axis=3, concat_axis=2, tiled=True)
    query_here, key_here, value_here = (sent[0], sent[1], sent[2])
    start = frame_index * tiles_here
    length = all_frames * area
    frame_of = jnp.arange(length, dtype=jnp.int32) // area
    frame_gap = frame_of[None, :] - frame_of[:, None]
    valid_flat = tile_valid_all.reshape(all_frames, count_tiles, area).transpose(1, 0, 2)
    valid_flat = jnp.pad(
        valid_flat, ((0, padded_count - count_tiles), (0, 0), (0, 0)), constant_values=True
    )
    valid_here = lax.dynamic_slice_in_dim(valid_flat, start, tiles_here, 0)
    back_here = lax.dynamic_slice_in_dim(
        jnp.pad(back_reach.reshape(count_tiles), (0, padded_count - count_tiles)),
        start,
        tiles_here,
        0,
    )
    fwd_here = lax.dynamic_slice_in_dim(
        jnp.pad(fwd_reach.reshape(count_tiles), (0, padded_count - count_tiles)),
        start,
        tiles_here,
        0,
    )
    key_ok = valid_here.reshape(tiles_here, length)
    allowed = (
        (frame_gap[None] >= -back_here[:, None, None])
        & (frame_gap[None] <= fwd_here[:, None, None])
        & key_ok[:, None, :]
    )
    time_masks = allowed[None].reshape(heads * tiles_here, length, length)

    def by_tile(array):
        return array.transpose(0, 2, 1, 3, 4).reshape(heads * tiles_here, length, DH)

    temporal = attend_items(
        by_tile(query_here), by_tile(key_here), by_tile(value_here), time_masks
    ).astype(jnp.bfloat16)
    temporal = temporal.reshape(heads, tiles_here, all_frames, area, DH).transpose(0, 2, 1, 3, 4)
    returned = lax.all_to_all(temporal, "frame", split_axis=1, concat_axis=2, tiled=True)[
        :, :, :count_tiles
    ]
    combined = (spatial_t.astype(jnp.float32) + returned.astype(jnp.float32)) * query_factor[
        None, :, :, :, None
    ]
    combined = combined.astype(jnp.bfloat16).reshape(
        heads, frames, tile_rows, tile_cols, TS, TS, DH
    )
    return combined.transpose(1, 2, 4, 3, 5, 0, 6).reshape(frames, token_rows, token_cols, channels)


SCALE = 1.0 / math.sqrt(DH)
MASKED = -1e30
AREA = TS * TS
GROUP = 15
VMEM_LIMIT = 48 * 1024 * 1024
NT_DIMS = (((1,), (1,)), ((), ()))


def scalar_spec():
    return pl.BlockSpec(memory_space=pltpu.SMEM)


def vector_spec():
    return pl.BlockSpec(memory_space=pltpu.VMEM)


def read_tile(ref, row, col):
    return ref[pl.ds(row * TS, TS), col].reshape(AREA, DH)


def key_norms(keys):
    wide = keys.astype(jnp.float32)
    square = wide * wide
    high = square.astype(jnp.bfloat16)
    low = (square - high.astype(jnp.float32)).astype(jnp.bfloat16)
    ones = jnp.ones((8, 2 * DH), jnp.bfloat16)
    both = jnp.concatenate([high, low], axis=1)
    total = lax.dot_general(ones, both, NT_DIMS, preferred_element_type=jnp.float32)
    return total * (-0.5 * SCALE)


def row_valid(row, col, row_limit, col_limit):
    token = lax.broadcasted_iota(jnp.int32, (AREA, DH), 0)
    return (row * TS + (token >> 3) < row_limit) & (col * TS + (token & 7) < col_limit)


def pack_kernel(
    tile_rows, tile_cols, levels, me, back_in, fwd_in, keys, packed, reach, place, order, level,
    back, fwd, held, sems,
):
    load = pltpu.make_async_copy(keys, held, sems.at[0])
    loads = [
        pltpu.make_async_copy(back_in, back, sems.at[1]),
        pltpu.make_async_copy(fwd_in, fwd, sems.at[2]),
    ]
    for one in loads:
        one.start()
    load.start()
    for one in loads:
        one.wait()
    left = me[0] < 2
    most = [None] * 4
    tiles = [(r, c) for r in range(tile_rows) for c in range(tile_cols)]
    for way in range(2):
        counts = [jnp.int32(0)] * 4
        for index, (r, c) in enumerate(tiles):
            toward, away = back[r, c], fwd[r, c]
            value = jnp.where(left, toward, away) if way == 0 else jnp.where(left, away, toward)
            reach[way, index] = value
            counts = [counts[v] + (value >= v).astype(jnp.int32) for v in range(4)]
        for v in (1, 2, 3):
            most[v] = counts[v] if way == 0 else jnp.maximum(most[v], counts[v])
        spots = [counts[1], counts[2], counts[3], jnp.int32(0)]
        for index in range(len(tiles)):
            value = jnp.minimum(reach[way, index], 3)
            spot = spots[0]
            for v in (1, 2, 3):
                spot = jnp.where(value == v, spots[v], spot)
            spots = [spots[v] + (value == v).astype(jnp.int32) for v in range(4)]
            place[way, index] = spot
            if way == 1:
                order[spot] = index
    chosen = jnp.int32(0)
    for one, two, three in levels[:-1]:
        over = (most[1] > one) | (most[2] > two) | (most[3] > three)
        chosen += over.astype(jnp.int32)
    level[0] = chosen
    load.wait()

    def pack_row(r, carry):
        for c in range(tile_cols):
            packed[place[0, r * tile_cols + c]] = read_tile(held, r, c)
        return carry

    lax.fori_loop(0, tile_rows, pack_row, 0)


def spatial_kernel(
    tile_rows, tile_cols, me, place, rows_ok, cols_ok, queries, keys, values, mixed, packed_q,
    query_t, key_t, value_t, bias_even, bias_odd,
):
    row_limit, col_limit = rows_ok[me[0]], cols_ok[me[0]]
    wide = tile_cols * AREA
    value_t[:, DH:] = jnp.ones((value_t.shape[0], DH), jnp.bfloat16)

    def lane_bias(r, first, count):
        start = pl.multiple_of((r * tile_cols + first) * AREA, AREA)
        norms = key_norms(key_t[pl.ds(start, count * AREA)])
        lane = lax.broadcasted_iota(jnp.int32, (8, count * AREA), 1) + first * AREA
        valid = (r * TS + ((lane >> 3) & 7) < row_limit) & (
            (lane >> 6) * TS + (lane & 7) < col_limit
        )
        return jnp.where(valid, norms, MASKED)

    def retile_row(r, carry):
        for c in range(tile_cols):
            index = r * tile_cols + c
            span = pl.ds(pl.multiple_of(index * AREA, AREA), AREA)
            tile_q = read_tile(queries, r, c)
            query_t[span] = tile_q
            packed_q[place[1, index]] = tile_q
            key_t[span] = read_tile(keys, r, c)
            value_t[span, :DH] = read_tile(values, r, c)
        bias_even[r] = lane_bias(r, 0, tile_cols)
        bias_odd[r] = lane_bias(r, 1, tile_cols - 2)
        return carry

    lax.fori_loop(0, tile_rows, retile_row, 0)
    lane_tile = lax.broadcasted_iota(jnp.int32, (8, 4 * AREA), 1) >> 6

    def attend_row(r, carry):
        first_row = jnp.clip(r - 1, 0, tile_rows - 3)
        for pair in range(tile_cols // 2):
            first_col = min(max(2 * pair - 1, 0), tile_cols - 4)
            index = r * tile_cols + 2 * pair
            query = query_t[pl.ds(pl.multiple_of(index * AREA, AREA), 2 * AREA)]
            scores, spans = [], []
            for step in range(3):
                key_row = first_row + step
                start = (key_row * tile_cols + first_col) * AREA
                span = pl.ds(pl.multiple_of(start, AREA), 4 * AREA)
                spans.append(span)
                dots = lax.dot_general(
                    query, key_t[span], NT_DIMS, preferred_element_type=jnp.float32
                )
                if first_col % 2:
                    lane_start = (first_col - 1) * AREA
                    bias = bias_odd[key_row, :, lane_start : lane_start + 4 * AREA]
                else:
                    lane_start = first_col * AREA
                    bias = bias_even[key_row, :, lane_start : lane_start + 4 * AREA]
                near_row = jnp.abs(key_row - r) <= 1
                both = []
                for half in range(2):
                    gap = lane_tile + (first_col - 2 * pair - half)
                    near = (gap >= -1) & (gap <= 1) & near_row
                    part = dots[half * AREA : (half + 1) * AREA].reshape(TS, 8, 4 * AREA)
                    part = part * SCALE + jnp.where(near, bias, MASKED)[None]
                    both.append(part.reshape(AREA, 4 * AREA))
                scores.append(jnp.concatenate(both, axis=0))
            highest = jnp.maximum(jnp.maximum(scores[0], scores[1]), scores[2])
            highest = jnp.max(highest, axis=1, keepdims=True)
            total = None
            for step in range(3):
                weights = jnp.exp(scores[step] - highest).astype(jnp.bfloat16)
                part = jnp.dot(weights, value_t[spans[step]], preferred_element_type=jnp.float32)
                total = part if total is None else total + part
            result = total[:, :DH] / total[:, DH:]
            for half in range(2):
                valid = row_valid(r, 2 * pair + half, row_limit, col_limit)
                tile = jnp.where(valid, result[half * AREA : (half + 1) * AREA], 0.0)
                mixed[place[0, index + half]] = tile.astype(jnp.bfloat16)
        return carry

    lax.fori_loop(0, tile_rows, attend_row, 0)


def frames_of(mine):
    left = mine < 2
    return mine, jnp.where(left, 0, 3), jnp.where(left, 2, 1), jnp.where(left, 3, 0)


def by_block(picks, lanes):
    block = lax.broadcasted_iota(jnp.int32, (8, lanes), 1) >> 6
    chosen = jnp.full((8, lanes), picks[0], jnp.int32)
    for number in range(1, lanes // AREA):
        chosen = jnp.where(block == number, picks[number], chosen)
    return chosen


def room_left(frames, rows_ok, cols_ok, lanes):
    lane = lax.broadcasted_iota(jnp.int32, (8, lanes), 1)
    row_room = by_block([rows_ok[frame] for frame in frames], lanes) - ((lane >> 3) & 7)
    col_room = by_block([cols_ok[frame] for frame in frames], lanes) - (lane & 7)
    return row_room, col_room


def weigh(queries, keys_here, biases):
    parts, highest = [], []
    dots = [
        lax.dot_general(query, key, NT_DIMS, preferred_element_type=jnp.float32)
        for query, key in zip(queries, keys_here)
    ]
    norms = [key_norms(key) for key in keys_here]
    for dot, norm, bias in zip(dots, norms, biases):
        lanes = dot.shape[1]
        part = dot.reshape(TS, 8, lanes) * SCALE + (norm + bias)[None]
        parts.append(part.reshape(AREA, lanes))
    highest = [jnp.max(part, axis=1, keepdims=True) for part in parts]
    return [jnp.exp(part - top) for part, top in zip(parts, highest)], highest


def mask_bias(allowed, room, row, col, lanes):
    valid = (room[0] > row * TS) & (room[1] > col * TS) & (by_block(allowed, lanes) > 0)
    return jnp.where(valid, 0.0, MASKED)


def mix(weights, values_here):
    ones = jnp.ones(values_here.shape, jnp.bfloat16)
    total = jnp.dot(
        weights,
        jnp.concatenate([values_here, ones], axis=1),
        preferred_element_type=jnp.float32,
    )
    return total[:, :DH], total[:, DH:]


def in_chunks(first, last, body, carry):
    size = max(option for option in range(1, 19) if (last - first) % option == 0)

    def chunk(number, carry):
        return body([first + number * size + step for step in range(size)], carry)

    return lax.fori_loop(0, (last - first) // size, chunk, carry)


def hosted_kernel(
    tile_cols, one, two, three, me, reach, place, order, rows_ok, cols_ok, hosted_q, packed_k,
    far_k, far_k2, own_s, far_s, mixed, weights,
):
    own, _, far, far2 = frames_of(me[0])
    short = room_left((own, far), rows_ok, cols_ok, 2 * AREA)
    full = room_left((own, far, far2, own), rows_ok, cols_ok, 4 * AREA)
    lane = lax.broadcasted_iota(jnp.int32, (AREA, DH), 1)
    no = jnp.int32(0)

    def reached(index, least):
        return (reach[1, index] >= least).astype(jnp.int32)

    def near_ones(spots, sums):
        indices = [order[spot] for spot in spots]
        rows = [lax.div(index, tile_cols) for index in indices]
        homes = [place[0, index] for index in indices]
        keys_here = [
            jnp.concatenate([packed_k[home], far_k[spot]], axis=0)
            for home, spot in zip(homes, spots)
        ]
        values_here = [
            jnp.concatenate([own_s[home], far_s[spot]], axis=0)
            for home, spot in zip(homes, spots)
        ]
        biases = [
            mask_bias(
                (reached(index, 1), reached(index, 2)),
                short, row, index - row * tile_cols, 2 * AREA,
            )
            for index, row in zip(indices, rows)
        ]
        parts, highest = weigh([hosted_q[spot] for spot in spots], keys_here, biases)
        totals = [mix(part.astype(jnp.bfloat16), v) for part, v in zip(parts, values_here)]
        for spot, (total, sum_here), top in zip(spots, totals, highest):
            mixed[spot - three] = (total / sum_here).astype(jnp.bfloat16)
            sums = jnp.where(lane == spot, top + jnp.log(sum_here), sums)
        return sums

    def far_ones(spots, sums):
        indices = [order[spot] for spot in spots]
        rows = [lax.div(index, tile_cols) for index in indices]
        homes = [packed_k[place[0, index]] for index in indices]
        keys_here = [
            jnp.concatenate([home, far_k[spot], far_k2[spot], home], axis=0)
            for home, spot in zip(homes, spots)
        ]
        biases = [
            mask_bias(
                (reached(index, 1), reached(index, 2), reached(index, 3), no),
                full, row, index - row * tile_cols, 4 * AREA,
            )
            for index, row in zip(indices, rows)
        ]
        parts, highest = weigh([hosted_q[spot] for spot in spots], keys_here, biases)
        for spot, part, top in zip(spots, parts, highest):
            weights[spot] = part.astype(jnp.bfloat16)
            sum_here = jnp.sum(part, axis=1, keepdims=True)
            sums = jnp.where(lane == spot, top + jnp.log(sum_here), sums)
        return sums

    sums = jnp.zeros((AREA, DH), jnp.float32)
    if one > three:
        sums = in_chunks(three, one, near_ones, sums)
    sums = in_chunks(0, three, far_ones, sums)
    for step in range(3):
        piece = sums.astype(jnp.bfloat16)
        mixed[one - three + step] = piece
        sums = sums - piece.astype(jnp.float32)


def far_mix_kernel(three, place, order, weights, own_s, far_s, far_s2, mixed):
    def far_ones(spots, carry):
        homes = [own_s[place[0, order[spot]]] for spot in spots]
        totals = [
            mix(weights[spot], jnp.concatenate([home, far_s[spot], far_s2[spot], home], axis=0))
            for spot, home in zip(spots, homes)
        ]
        for spot, (total, sum_here) in zip(spots, totals):
            mixed[spot] = (total / sum_here).astype(jnp.bfloat16)
        return carry

    in_chunks(0, three, far_ones, 0)


def tile_groups(tile_rows, tile_cols, body, carry):
    rows = max(option for option in (1, 2, 3) if tile_rows % option == 0)

    def step(number, carry):
        here = [(number * rows + r, c) for r in range(rows) for c in range(tile_cols)]
        for first in range(0, len(here), GROUP):
            carry = body(here[first : first + GROUP], carry)
        return carry

    return lax.fori_loop(0, tile_rows // rows, step, carry)


def own_weights_kernel(
    tile_rows, tile_cols, one, two, me, reach, place, rows_ok, cols_ok, queries, keys, near_k,
    far_k, far_k2, weights, sums_out,
):
    mine = me[0]
    inner = (mine == 1) | (mine == 2)
    room = room_left(frames_of(mine), rows_ok, cols_ok, 4 * AREA)
    lane = lax.broadcasted_iota(jnp.int32, (AREA, DH), 1)

    def weigh_tiles(here, sums):
        query_list, key_list, biases = [], [], []
        for r, c in here:
            index = r * tile_cols + c
            near = jnp.minimum(place[0, index], one - 1)
            far = jnp.minimum(place[1, index], one - 1)
            far2 = jnp.minimum(place[1, index], two - 1)
            near_reach, far_reach = reach[0, index], reach[1, index]
            allowed = (
                jnp.int32(1),
                (inner & (near_reach >= 1)).astype(jnp.int32),
                (inner & (far_reach >= 1)).astype(jnp.int32),
                (inner & (far_reach >= 2)).astype(jnp.int32),
            )
            biases.append(mask_bias(allowed, room, r, c, 4 * AREA))
            query_list.append(read_tile(queries, r, c))
            key_list.append(
                jnp.concatenate(
                    [read_tile(keys, r, c), near_k[near], far_k[far], far_k2[far2]], axis=0
                )
            )
        parts, highest = weigh(query_list, key_list, biases)
        totals = [jnp.sum(part, axis=1, keepdims=True) for part in parts]
        for (r, c), part, sum_here, top in zip(here, parts, totals, highest):
            index = r * tile_cols + c
            weights[index] = part.astype(jnp.bfloat16)
            sums = jnp.where(lane == index, top + jnp.log(sum_here), sums)
        return sums

    sums_out[...] = tile_groups(
        tile_rows, tile_cols, weigh_tiles, jnp.zeros((AREA, DH), jnp.float32)
    )


def own_mix_kernel(
    tile_rows, tile_cols, one, two, place, weights, own_s, near_s, near_rest, far_s, far_s2, mixed
):
    def mix_tiles(here, carry):
        totals = []
        for r, c in here:
            index = r * tile_cols + c
            home = place[0, index]
            near = near_s[jnp.minimum(home, two - 1)]
            if one > two:
                rest = near_rest[jnp.clip(home - two, 0, one - two - 1)]
                near = jnp.where(home < two, near, rest)
            far = far_s[jnp.minimum(place[1, index], one - 1)]
            far2 = far_s2[jnp.minimum(place[1, index], two - 1)]
            values_here = jnp.concatenate([own_s[home], near, far, far2], axis=0)
            totals.append(mix(weights[index], values_here))
        for (r, c), (total, sum_here) in zip(here, totals):
            mixed[r * tile_cols + c] = (total / sum_here).astype(jnp.bfloat16)
        return carry

    tile_groups(tile_rows, tile_cols, mix_tiles, 0)


def combine_kernel(
    tile_rows, tile_cols, one, three, me, reach, place, rows_ok, cols_ok, own_s, own_o, own_sums,
    near_ones, far_ones, out, held, sems,
):
    mine = me[0]
    outer = (mine == 0) | (mine == 3)
    row_limit, col_limit = rows_ok[mine], cols_ok[mine]
    lane = lax.broadcasted_iota(jnp.int32, (AREA, DH), 1)
    their_sums = near_ones[one - three].astype(jnp.float32)
    their_sums += near_ones[one - three + 1].astype(jnp.float32)
    their_sums += near_ones[one - three + 2].astype(jnp.float32)
    my_sums = own_sums[...]

    def store_row(r):
        rows = pl.ds(r * TS, TS)
        return pltpu.make_async_copy(held.at[rows], out.at[rows], sems.at[r])

    def combine_row(r, carry):
        for c in range(tile_cols):
            index = r * tile_cols + c
            spot = jnp.minimum(place[1, index], one - 1)
            remote = outer & (reach[1, index] >= 1)
            gap = jnp.where(lane == spot, their_sums, 0.0) - jnp.where(lane == index, my_sums, 0.0)
            gap = jnp.sum(gap, axis=1, keepdims=True)
            share = 1.0 / (1.0 + jnp.exp(gap))
            share = jnp.where(remote, share, 1.0)
            theirs = far_ones[jnp.minimum(spot, three - 1)].astype(jnp.float32)
            if one > three:
                other = near_ones[jnp.maximum(spot - three, 0)].astype(jnp.float32)
                theirs = jnp.where(spot < three, theirs, other)
            mine_o = own_o[index].astype(jnp.float32)
            temporal = jnp.where(remote, share * mine_o + (1.0 - share) * theirs, mine_o)
            temporal = temporal.astype(jnp.bfloat16).astype(jnp.float32)
            spatial = own_s[place[0, index]].astype(jnp.float32)
            valid = row_valid(r, c, row_limit, col_limit)
            tile = jnp.where(valid, spatial + temporal, 0.0)
            held[pl.ds(r * TS, TS), c] = tile.astype(jnp.bfloat16).reshape(TS, TS, DH)
        store_row(r).start()
        return carry

    lax.fori_loop(0, tile_rows, combine_row, 0)
    for r in range(tile_rows):
        store_row(r).wait()


def run_kernel(
    kernel, out_shape, scalars, arrays, scratch=(), scalar_outs=0, micros=4, from_hbm=0,
    to_hbm=False,
):
    outs = list(out_shape)
    in_hbm = pl.BlockSpec(memory_space=pltpu.HBM)
    out_specs = [vector_spec()] * (len(outs) - scalar_outs) + [scalar_spec()] * scalar_outs
    in_specs = [in_hbm] * from_hbm + [vector_spec()] * (len(arrays) - from_hbm)
    return pl.pallas_call(
        kernel,
        out_shape=outs,
        in_specs=[scalar_spec()] * len(scalars) + in_specs,
        out_specs=[in_hbm] if to_hbm else out_specs,
        scratch_shapes=list(scratch),
        compiler_params=pltpu.CompilerParams(vmem_limit_bytes=VMEM_LIMIT),
        cost_estimate=pl.CostEstimate(
            flops=int(micros * 1e9), bytes_accessed=int(micros * 1e6), transcendentals=0
        ),
    )(*scalars, *arrays)


def room_levels(count):
    shares = ((45, 30, 15), (48, 33, 18), (51, 36, 21), (54, 39, 24), (57, 45, 30))
    levels = [tuple(max(count * share // 60, 1) for share in level) for level in shares]
    return levels + [(count, count, count)]


def four_frames(queries, keys, values, back_reach, fwd_reach, valid_rows, valid_cols):
    _, token_rows, token_cols, _ = queries.shape
    tile_rows, tile_cols = token_rows // TS, token_cols // TS
    count = tile_rows * tile_cols
    shape = (token_rows, tile_cols, TS, DH)
    queries, keys, values = queries.reshape(shape), keys.reshape(shape), values.reshape(shape)
    me = lax.axis_index("frame").reshape(1).astype(jnp.int32)
    inward, across, outward = [(0, 1), (3, 2)], [(1, 2), (2, 1)], [(1, 0), (2, 3)]
    levels = room_levels(count)

    def tiles(number):
        return jax.ShapeDtypeStruct((number, AREA, DH), jnp.bfloat16)

    def ints(*sizes):
        return jax.ShapeDtypeStruct(sizes, jnp.int32)

    def send(array, pairs):
        return lax.ppermute(array, "frame", pairs)

    packed_k, reach, place, order, level = run_kernel(
        functools.partial(pack_kernel, tile_rows, tile_cols, levels),
        (tiles(count), ints(2, count), ints(2, count), ints(count), ints(1)),
        (me,),
        (back_reach, fwd_reach, keys),
        scratch=(
            pltpu.SMEM((tile_rows, tile_cols), jnp.int32),
            pltpu.SMEM((tile_rows, tile_cols), jnp.int32),
            pltpu.VMEM(shape, jnp.bfloat16),
            pltpu.SemaphoreType.DMA((3,)),
        ),
        scalar_outs=4,
        micros=2,
        from_hbm=3,
    )

    def with_room(one, two, three):
        def run(queries, keys, values, packed_k, reach, place, order):
            near_k = send(packed_k[:one], inward)
            far_k = send(packed_k[:one], across)
            own_s, packed_q = run_kernel(
                functools.partial(spatial_kernel, tile_rows, tile_cols),
                (tiles(count), tiles(count)),
                (me, place, valid_rows, valid_cols),
                (queries, keys, values),
                scratch=(
                    pltpu.VMEM((count * AREA, DH), jnp.bfloat16),
                    pltpu.VMEM((count * AREA, DH), jnp.bfloat16),
                    pltpu.VMEM((count * AREA, 2 * DH), jnp.bfloat16),
                    pltpu.VMEM((tile_rows, 8, tile_cols * AREA), jnp.float32),
                    pltpu.VMEM((tile_rows, 8, (tile_cols - 2) * AREA), jnp.float32),
                ),
                micros=10,
            )
            packed_q, far_k = lax.optimization_barrier((packed_q, far_k))
            hosted_q = send(packed_q[:one], inward)
            far_s = send(own_s[:one], across)
            near_s = send(own_s[:two], inward)
            near_rest = send(own_s[two:one], inward) if one > two else near_s
            far_k2 = send(near_k[:two], across)
            far_s2 = send(near_s[:two], across)
            hosted_a, hosted_w = run_kernel(
                functools.partial(hosted_kernel, tile_cols, one, two, three),
                (
                    tiles(one - three + 3),
                    jax.ShapeDtypeStruct((three, AREA, 4 * AREA), jnp.bfloat16),
                ),
                (me, reach, place, order, valid_rows, valid_cols),
                (hosted_q, packed_k, far_k, far_k2, own_s, far_s),
                micros=5,
            )
            returned_a = send(hosted_a, outward)
            hosted_w, near_k = lax.optimization_barrier((hosted_w, near_k))
            own_w, own_sums = run_kernel(
                functools.partial(own_weights_kernel, tile_rows, tile_cols, one, two),
                (
                    jax.ShapeDtypeStruct((count, AREA, 4 * AREA), jnp.bfloat16),
                    jax.ShapeDtypeStruct((AREA, DH), jnp.float32),
                ),
                (me, reach, place, valid_rows, valid_cols),
                (queries, keys, near_k, far_k, far_k2),
                micros=5,
            )
            hosted_w, own_w = lax.optimization_barrier((hosted_w, own_w))
            (hosted_b,) = run_kernel(
                functools.partial(far_mix_kernel, three),
                (tiles(three),),
                (place, order),
                (hosted_w, own_s, far_s, far_s2),
                micros=0.5,
            )
            returned_b = send(hosted_b, outward)
            (own_o,) = run_kernel(
                functools.partial(own_mix_kernel, tile_rows, tile_cols, one, two),
                (tiles(count),),
                (place,),
                (own_w, own_s, near_s, near_rest, far_s, far_s2),
                micros=1,
            )
            (out,) = run_kernel(
                functools.partial(combine_kernel, tile_rows, tile_cols, one, three),
                (jax.ShapeDtypeStruct(shape, jnp.bfloat16),),
                (me, reach, place, valid_rows, valid_cols),
                (own_s, own_o, own_sums, returned_a, returned_b),
                scratch=(pltpu.VMEM(shape, jnp.bfloat16), pltpu.SemaphoreType.DMA((tile_rows,))),
                micros=2,
                to_hbm=True,
            )
            return out

        return run

    branches = [with_room(*level) for level in levels]
    operands = (queries, keys, values, packed_k, reach, place, order)
    out = lax.switch(level[0], branches, *operands)
    return out.reshape(1, token_rows, token_cols, DH)


def solution(mesh):
    in_specs = (
        P(("dp", "frame"), None, None, "row"),
        P(("dp", "frame"), None, None, "row"),
        P(("dp", "frame"), None, None, "row"),
        P("dp", None),
        P("dp", None),
        P("dp"),
        P("dp"),
    )
    out_specs = P(("dp", "frame"), None, None, "row")

    def block(*args):
        frames, _, token_cols, channels = args[0].shape
        line = mesh.shape["frame"] == 4 and frames == 1 and channels == DH
        if line and token_cols % (2 * TS) == 0 and 4 <= token_cols // TS:
            return four_frames(*args)
        return per_device(*args)

    return jax.shard_map(
        block, mesh=mesh, in_specs=in_specs, out_specs=out_specs, check_vma=False
    )
```

```python
import functools
import math

import jax
import jax.numpy as jnp
from jax import lax
from jax.experimental import pallas as pl
from jax.experimental.pallas import tpu as pltpu
from jax.sharding import PartitionSpec as P

DH = 128
TS = 8


def group_size(item_count, row_count):
    size = 1
    for option in range(1, item_count + 1):
        if item_count % option == 0 and option * row_count <= 1024:
            size = option
    return size


def attend_group(group_parts):
    query_rows, key_rows, value_rows, allowed = group_parts
    dot_terms = jnp.einsum("gmd,gnd->gmn", query_rows, key_rows, preferred_element_type=jnp.float32)
    query_sq = jnp.einsum("gmd,gmd->gm", query_rows, query_rows, preferred_element_type=jnp.float32)
    key_sq = jnp.einsum("gnd,gnd->gn", key_rows, key_rows, preferred_element_type=jnp.float32)
    distance = query_sq[:, :, None] + key_sq[:, None, :] - 2.0 * dot_terms
    scores = jnp.where(allowed, -distance * (0.5 / math.sqrt(query_rows.shape[2])), -jnp.inf)
    highest = jnp.max(scores, axis=2, keepdims=True)
    weights = jnp.exp(scores - highest)
    totals = jnp.sum(weights, axis=2, keepdims=True)
    mixed = jnp.einsum(
        "gmn,gnd->gmd", weights.astype(jnp.bfloat16), value_rows, preferred_element_type=jnp.float32
    )
    return mixed / totals


def attend_items(query_items, key_items, value_items, masks):
    item_count = query_items.shape[0]
    per_group = group_size(item_count, query_items.shape[1])
    groups = item_count // per_group

    def regroup(array):
        return array.reshape((groups, per_group) + array.shape[1:])

    mixed = lax.map(
        attend_group,
        (regroup(query_items), regroup(key_items), regroup(value_items), regroup(masks)),
    )
    return mixed.reshape((item_count,) + mixed.shape[2:])


def tile_split(block):
    frames, token_rows, token_cols, channels = block.shape
    heads = channels // DH
    return (
        block.reshape(frames, token_rows // TS, TS, token_cols // TS, TS, heads, DH)
        .transpose(5, 0, 1, 3, 2, 4, 6)
        .reshape(heads, frames, token_rows // TS * (token_cols // TS), TS * TS, DH)
    )


def neighbours(tiles, tile_rows, tile_cols):
    heads, frames, count_tiles, area, depth = tiles.shape
    grid = tiles.reshape(heads * frames, tile_rows, tile_cols, area, depth)
    padded = jnp.pad(grid, ((0, 0), (1, 1), (1, 1), (0, 0), (0, 0)))
    views = [
        padded[:, dy : dy + tile_rows, dx : dx + tile_cols] for dy in range(3) for dx in range(3)
    ]
    stacked = jnp.stack(views, axis=3)
    return stacked.reshape(heads * frames * count_tiles, 9 * area, depth)


def pad_tiles(tiles, total):
    return jnp.pad(tiles, ((0, 0), (0, 0), (0, total - tiles.shape[2]), (0, 0), (0, 0)))


def per_device(queries, keys, values, back_reach, fwd_reach, valid_rows, valid_cols):
    frames, token_rows, token_cols, channels = queries.shape
    heads = channels // DH
    tile_rows = token_rows // TS
    tile_cols = token_cols // TS
    count_tiles = tile_rows * tile_cols
    area = TS * TS
    frame_count = lax.axis_size("frame")
    frame_index = lax.axis_index("frame")
    padded_count = (count_tiles + frame_count - 1) // frame_count * frame_count
    tiles_here = padded_count // frame_count
    all_frames = frames * frame_count
    row_ids = jnp.arange(token_rows, dtype=jnp.int32)
    col_ids = jnp.arange(token_cols, dtype=jnp.int32)
    row_ok = row_ids[None, :] < valid_rows[:, None]
    col_ok = col_ids[None, :] < valid_cols[:, None]
    token_valid = row_ok[:, :, None] & col_ok[:, None, :]
    tile_valid_all = (
        token_valid.reshape(all_frames, tile_rows, TS, tile_cols, TS)
        .transpose(0, 1, 3, 2, 4)
        .reshape(all_frames, tile_rows, tile_cols, area)
    )
    tile_valid = lax.dynamic_slice_in_dim(tile_valid_all, frame_index * frames, frames, 0)
    padded_valid = jnp.pad(tile_valid, ((0, 0), (1, 1), (1, 1), (0, 0)))
    near_valid = jnp.stack(
        [
            padded_valid[:, dy : dy + tile_rows, dx : dx + tile_cols]
            for dy in range(3)
            for dx in range(3)
        ],
        axis=3,
    )
    near_valid = near_valid.reshape(frames, count_tiles, 1, 9 * area)
    query_factor = tile_valid.reshape(frames, count_tiles, area).astype(jnp.float32)
    query_t = tile_split(queries)
    key_t = tile_split(keys)
    masks = near_valid[None].reshape(heads * frames * count_tiles, 1, 9 * area)
    spatial = attend_items(
        query_t.reshape(heads * frames * count_tiles, area, DH),
        neighbours(key_t, tile_rows, tile_cols),
        neighbours(tile_split(values), tile_rows, tile_cols),
        masks,
    )
    spatial = spatial.reshape(heads, frames, count_tiles, area, DH)
    spatial_t = (spatial * query_factor[None, :, :, :, None]).astype(jnp.bfloat16)
    triple = jnp.stack(
        [
            pad_tiles(query_t, padded_count),
            pad_tiles(key_t, padded_count),
            pad_tiles(spatial_t, padded_count),
        ]
    )
    sent = lax.all_to_all(triple, "frame", split_axis=3, concat_axis=2, tiled=True)
    query_here, key_here, value_here = (sent[0], sent[1], sent[2])
    start = frame_index * tiles_here
    length = all_frames * area
    frame_of = jnp.arange(length, dtype=jnp.int32) // area
    frame_gap = frame_of[None, :] - frame_of[:, None]
    valid_flat = tile_valid_all.reshape(all_frames, count_tiles, area).transpose(1, 0, 2)
    valid_flat = jnp.pad(
        valid_flat, ((0, padded_count - count_tiles), (0, 0), (0, 0)), constant_values=True
    )
    valid_here = lax.dynamic_slice_in_dim(valid_flat, start, tiles_here, 0)
    back_here = lax.dynamic_slice_in_dim(
        jnp.pad(back_reach.reshape(count_tiles), (0, padded_count - count_tiles)),
        start,
        tiles_here,
        0,
    )
    fwd_here = lax.dynamic_slice_in_dim(
        jnp.pad(fwd_reach.reshape(count_tiles), (0, padded_count - count_tiles)),
        start,
        tiles_here,
        0,
    )
    key_ok = valid_here.reshape(tiles_here, length)
    allowed = (
        (frame_gap[None] >= -back_here[:, None, None])
        & (frame_gap[None] <= fwd_here[:, None, None])
        & key_ok[:, None, :]
    )
    time_masks = allowed[None].reshape(heads * tiles_here, length, length)

    def by_tile(array):
        return array.transpose(0, 2, 1, 3, 4).reshape(heads * tiles_here, length, DH)

    temporal = attend_items(
        by_tile(query_here), by_tile(key_here), by_tile(value_here), time_masks
    ).astype(jnp.bfloat16)
    temporal = temporal.reshape(heads, tiles_here, all_frames, area, DH).transpose(0, 2, 1, 3, 4)
    returned = lax.all_to_all(temporal, "frame", split_axis=1, concat_axis=2, tiled=True)[
        :, :, :count_tiles
    ]
    combined = (spatial_t.astype(jnp.float32) + returned.astype(jnp.float32)) * query_factor[
        None, :, :, :, None
    ]
    combined = combined.astype(jnp.bfloat16).reshape(
        heads, frames, tile_rows, tile_cols, TS, TS, DH
    )
    return combined.transpose(1, 2, 4, 3, 5, 0, 6).reshape(frames, token_rows, token_cols, channels)


SCALE = 1.0 / math.sqrt(DH)
MASKED = -1e30
AREA = TS * TS
GROUP = 10
VMEM_LIMIT = 24 * 1024 * 1024
NT_DIMS = (((1,), (1,)), ((), ()))


def scalar_spec():
    return pl.BlockSpec(memory_space=pltpu.SMEM)


def vector_spec():
    return pl.BlockSpec(memory_space=pltpu.VMEM)


def read_tile(ref, row, col):
    return ref[pl.ds(row * TS, TS), col].reshape(AREA, DH)


def key_norms(keys):
    wide = keys.astype(jnp.float32)
    square = wide * wide
    high = square.astype(jnp.bfloat16)
    low = (square - high.astype(jnp.float32)).astype(jnp.bfloat16)
    ones = jnp.ones((8, 2 * DH), jnp.bfloat16)
    both = jnp.concatenate([high, low], axis=1)
    total = lax.dot_general(ones, both, NT_DIMS, preferred_element_type=jnp.float32)
    return total * (-0.5 * SCALE)


def row_valid(row, col, row_limit, col_limit):
    token = lax.broadcasted_iota(jnp.int32, (AREA, DH), 0)
    return (row * TS + (token >> 3) < row_limit) & (col * TS + (token & 7) < col_limit)


def pack_kernel(
    tile_rows, tile_cols, levels, me, back_in, fwd_in, keys, packed, reach, place, order, level,
    back, fwd, held, sems,
):
    load = pltpu.make_async_copy(keys, held, sems.at[0])
    loads = [
        pltpu.make_async_copy(back_in, back, sems.at[1]),
        pltpu.make_async_copy(fwd_in, fwd, sems.at[2]),
    ]
    for one in loads:
        one.start()
    load.start()
    for one in loads:
        one.wait()
    left = me[0] < 2
    most = [None] * 4
    tiles = [(r, c) for r in range(tile_rows) for c in range(tile_cols)]
    for way in range(2):
        counts = [jnp.int32(0)] * 4
        for index, (r, c) in enumerate(tiles):
            toward, away = back[r, c], fwd[r, c]
            value = jnp.where(left, toward, away) if way == 0 else jnp.where(left, away, toward)
            reach[way, index] = value
            counts = [counts[v] + (value >= v).astype(jnp.int32) for v in range(4)]
        for v in (1, 2, 3):
            most[v] = counts[v] if way == 0 else jnp.maximum(most[v], counts[v])
        spots = [counts[1], counts[2], counts[3], jnp.int32(0)]
        for index in range(len(tiles)):
            value = jnp.minimum(reach[way, index], 3)
            spot = spots[0]
            for v in (1, 2, 3):
                spot = jnp.where(value == v, spots[v], spot)
            spots = [spots[v] + (value == v).astype(jnp.int32) for v in range(4)]
            place[way, index] = spot
            if way == 1:
                order[spot] = index
    chosen = jnp.int32(0)
    for one, two, three in levels[:-1]:
        over = (most[1] > one) | (most[2] > two) | (most[3] > three)
        chosen += over.astype(jnp.int32)
    level[0] = chosen
    load.wait()

    def pack_row(r, carry):
        for c in range(tile_cols):
            packed[place[0, r * tile_cols + c]] = read_tile(held, r, c)
        return carry

    lax.fori_loop(0, tile_rows, pack_row, 0)


def spatial_kernel(
    tile_rows, tile_cols, me, place, rows_ok, cols_ok, queries, keys, values, mixed, packed_q,
    query_t, key_t, value_t, bias_even, bias_odd,
):
    row_limit, col_limit = rows_ok[me[0]], cols_ok[me[0]]
    wide = tile_cols * AREA
    value_t[:, DH:] = jnp.ones((value_t.shape[0], DH), jnp.bfloat16)

    def lane_bias(r, first, count):
        start = pl.multiple_of((r * tile_cols + first) * AREA, AREA)
        norms = key_norms(key_t[pl.ds(start, count * AREA)])
        lane = lax.broadcasted_iota(jnp.int32, (8, count * AREA), 1) + first * AREA
        valid = (r * TS + ((lane >> 3) & 7) < row_limit) & (
            (lane >> 6) * TS + (lane & 7) < col_limit
        )
        return jnp.where(valid, norms, MASKED)

    def retile_row(r, carry):
        for c in range(tile_cols):
            index = r * tile_cols + c
            span = pl.ds(pl.multiple_of(index * AREA, AREA), AREA)
            tile_q = read_tile(queries, r, c)
            query_t[span] = tile_q
            packed_q[place[1, index]] = tile_q
            key_t[span] = read_tile(keys, r, c)
            value_t[span, :DH] = read_tile(values, r, c)
        bias_even[r] = lane_bias(r, 0, tile_cols)
        bias_odd[r] = lane_bias(r, 1, tile_cols - 2)
        return carry

    lax.fori_loop(0, tile_rows, retile_row, 0)
    lane_tile = lax.broadcasted_iota(jnp.int32, (8, 4 * AREA), 1) >> 6

    def attend_row(r, carry):
        first_row = jnp.clip(r - 1, 0, tile_rows - 3)
        for pair in range(tile_cols // 2):
            first_col = min(max(2 * pair - 1, 0), tile_cols - 4)
            index = r * tile_cols + 2 * pair
            query = query_t[pl.ds(pl.multiple_of(index * AREA, AREA), 2 * AREA)]
            scores, spans = [], []
            for step in range(3):
                key_row = first_row + step
                start = (key_row * tile_cols + first_col) * AREA
                span = pl.ds(pl.multiple_of(start, AREA), 4 * AREA)
                spans.append(span)
                dots = lax.dot_general(
                    query, key_t[span], NT_DIMS, preferred_element_type=jnp.float32
                )
                if first_col % 2:
                    lane_start = (first_col - 1) * AREA
                    bias = bias_odd[key_row, :, lane_start : lane_start + 4 * AREA]
                else:
                    lane_start = first_col * AREA
                    bias = bias_even[key_row, :, lane_start : lane_start + 4 * AREA]
                near_row = jnp.abs(key_row - r) <= 1
                both = []
                for half in range(2):
                    gap = lane_tile + (first_col - 2 * pair - half)
                    near = (gap >= -1) & (gap <= 1) & near_row
                    part = dots[half * AREA : (half + 1) * AREA].reshape(TS, 8, 4 * AREA)
                    part = part * SCALE + jnp.where(near, bias, MASKED)[None]
                    both.append(part.reshape(AREA, 4 * AREA))
                scores.append(jnp.concatenate(both, axis=0))
            highest = jnp.maximum(jnp.maximum(scores[0], scores[1]), scores[2])
            highest = jnp.max(highest, axis=1, keepdims=True)
            total = None
            for step in range(3):
                weights = jnp.exp(scores[step] - highest).astype(jnp.bfloat16)
                part = jnp.dot(weights, value_t[spans[step]], preferred_element_type=jnp.float32)
                total = part if total is None else total + part
            result = total[:, :DH] / total[:, DH:]
            for half in range(2):
                valid = row_valid(r, 2 * pair + half, row_limit, col_limit)
                tile = jnp.where(valid, result[half * AREA : (half + 1) * AREA], 0.0)
                mixed[place[0, index + half]] = tile.astype(jnp.bfloat16)
        return carry

    lax.fori_loop(0, tile_rows, attend_row, 0)


def frames_of(mine):
    left = mine < 2
    return mine, jnp.where(left, 0, 3), jnp.where(left, 2, 1), jnp.where(left, 3, 0)


def by_block(picks, lanes):
    block = lax.broadcasted_iota(jnp.int32, (8, lanes), 1) >> 6
    chosen = jnp.full((8, lanes), picks[0], jnp.int32)
    for number in range(1, lanes // AREA):
        chosen = jnp.where(block == number, picks[number], chosen)
    return chosen


def room_left(frames, rows_ok, cols_ok, lanes):
    lane = lax.broadcasted_iota(jnp.int32, (8, lanes), 1)
    row_room = by_block([rows_ok[frame] for frame in frames], lanes) - ((lane >> 3) & 7)
    col_room = by_block([cols_ok[frame] for frame in frames], lanes) - (lane & 7)
    return row_room, col_room


def weigh(queries, keys_here, biases):
    parts, highest = [], []
    dots = [
        lax.dot_general(query, key, NT_DIMS, preferred_element_type=jnp.float32)
        for query, key in zip(queries, keys_here)
    ]
    norms = [key_norms(key) for key in keys_here]
    for dot, norm, bias in zip(dots, norms, biases):
        lanes = dot.shape[1]
        part = dot.reshape(TS, 8, lanes) * SCALE + (norm + bias)[None]
        parts.append(part.reshape(AREA, lanes))
    highest = [jnp.max(part, axis=1, keepdims=True) for part in parts]
    return [jnp.exp(part - top) for part, top in zip(parts, highest)], highest


def mask_bias(allowed, room, row, col, lanes):
    valid = (room[0] > row * TS) & (room[1] > col * TS) & (by_block(allowed, lanes) > 0)
    return jnp.where(valid, 0.0, MASKED)


def mix(weights, values_here):
    ones = jnp.ones(values_here.shape, jnp.bfloat16)
    total = jnp.dot(
        weights,
        jnp.concatenate([values_here, ones], axis=1),
        preferred_element_type=jnp.float32,
    )
    return total[:, :DH], total[:, DH:]


def in_chunks(first, last, body, carry):
    size = max(option for option in range(1, 11) if (last - first) % option == 0)

    def chunk(number, carry):
        return body([first + number * size + step for step in range(size)], carry)

    return lax.fori_loop(0, (last - first) // size, chunk, carry)


def reached(reach, index, least):
    return (reach[1, index] >= least).astype(jnp.int32)


def near_hosted_kernel(
    tile_cols, one, two, three, me, reach, place, order, rows_ok, cols_ok, hosted_q, packed_k,
    far_k, own_s, far_s, mixed, sums_out,
):
    own, _, far, _ = frames_of(me[0])
    room = room_left((own, far), rows_ok, cols_ok, 2 * AREA)
    lane = lax.broadcasted_iota(jnp.int32, (AREA, DH), 1)

    def near_ones(spots, sums):
        indices = [order[spot] for spot in spots]
        rows = [lax.div(index, tile_cols) for index in indices]
        homes = [place[0, index] for index in indices]
        keys_here = [
            jnp.concatenate([packed_k[home], far_k[spot]], axis=0)
            for home, spot in zip(homes, spots)
        ]
        values_here = [
            jnp.concatenate([own_s[home], far_s[jnp.minimum(spot, two - 1)]], axis=0)
            for home, spot in zip(homes, spots)
        ]
        biases = [
            mask_bias(
                (reached(reach, index, 1), reached(reach, index, 2)),
                room, row, index - row * tile_cols, 2 * AREA,
            )
            for index, row in zip(indices, rows)
        ]
        parts, highest = weigh([hosted_q[spot - three] for spot in spots], keys_here, biases)
        totals = [mix(part.astype(jnp.bfloat16), v) for part, v in zip(parts, values_here)]
        for spot, (total, sum_here), top in zip(spots, totals, highest):
            mixed[spot - three] = (total / sum_here).astype(jnp.bfloat16)
            sums = jnp.where(lane == spot, top + jnp.log(sum_here), sums)
        return sums

    sums = jnp.zeros((AREA, DH), jnp.float32)
    sums_out[...] = in_chunks(three, one, near_ones, sums)


def far_hosted_kernel(
    tile_cols, three, me, reach, place, order, rows_ok, cols_ok, hosted_q, packed_k, far_k,
    far_k2, near_sums, weights, sums_out,
):
    own, _, far, far2 = frames_of(me[0])
    room = room_left((own, far, far2, own), rows_ok, cols_ok, 4 * AREA)
    lane = lax.broadcasted_iota(jnp.int32, (AREA, DH), 1)
    no = jnp.int32(0)

    def far_ones(spots, sums):
        indices = [order[spot] for spot in spots]
        rows = [lax.div(index, tile_cols) for index in indices]
        homes = [packed_k[place[0, index]] for index in indices]
        keys_here = [
            jnp.concatenate([home, far_k[spot], far_k2[spot], home], axis=0)
            for home, spot in zip(homes, spots)
        ]
        biases = [
            mask_bias(
                tuple(reached(reach, index, least) for least in (1, 2, 3)) + (no,),
                room, row, index - row * tile_cols, 4 * AREA,
            )
            for index, row in zip(indices, rows)
        ]
        parts, highest = weigh([hosted_q[spot] for spot in spots], keys_here, biases)
        for spot, part, top in zip(spots, parts, highest):
            weights[spot] = part.astype(jnp.bfloat16)
            sum_here = jnp.sum(part, axis=1, keepdims=True)
            sums = jnp.where(lane == spot, top + jnp.log(sum_here), sums)
        return sums

    sums = in_chunks(0, three, far_ones, near_sums[...])
    for step in range(3):
        piece = sums.astype(jnp.bfloat16)
        sums_out[step] = piece
        sums = sums - piece.astype(jnp.float32)


def far_mix_kernel(three, place, order, weights, own_s, far_s, far_s2, sums, mixed):
    def far_ones(spots, carry):
        homes = [own_s[place[0, order[spot]]] for spot in spots]
        totals = [
            mix(weights[spot], jnp.concatenate([home, far_s[spot], far_s2[spot], home], axis=0))
            for spot, home in zip(spots, homes)
        ]
        for spot, (total, sum_here) in zip(spots, totals):
            mixed[spot] = (total / sum_here).astype(jnp.bfloat16)
        return carry

    in_chunks(0, three, far_ones, 0)
    mixed[three : three + 3] = sums[...]


def tile_groups(tile_rows, tile_cols, body, carry):
    rows = 1

    def step(number, carry):
        here = [(number * rows + r, c) for r in range(rows) for c in range(tile_cols)]
        for first in range(0, len(here), GROUP):
            carry = body(here[first : first + GROUP], carry)
        return carry

    return lax.fori_loop(0, tile_rows // rows, step, carry)


def two_part(first, rest, spot, one, two):
    tile = first[jnp.minimum(spot, two - 1)]
    if one > two:
        tile = jnp.where(spot < two, tile, rest[jnp.clip(spot - two, 0, one - two - 1)])
    return tile


def own_weights_kernel(
    tile_rows, tile_cols, one, two, me, reach, place, rows_ok, cols_ok, queries, keys, near_k,
    near_rest, far_k, far_k2, weights, sums_out,
):
    mine = me[0]
    inner = (mine == 1) | (mine == 2)
    room = room_left(frames_of(mine), rows_ok, cols_ok, 4 * AREA)
    lane = lax.broadcasted_iota(jnp.int32, (AREA, DH), 1)

    def weigh_tiles(here, sums):
        query_list, key_list, biases = [], [], []
        for r, c in here:
            index = r * tile_cols + c
            near = two_part(near_k, near_rest, place[0, index], one, two)
            far = jnp.minimum(place[1, index], one - 1)
            far2 = jnp.minimum(place[1, index], two - 1)
            near_reach, far_reach = reach[0, index], reach[1, index]
            allowed = (
                jnp.int32(1),
                (inner & (near_reach >= 1)).astype(jnp.int32),
                (inner & (far_reach >= 1)).astype(jnp.int32),
                (inner & (far_reach >= 2)).astype(jnp.int32),
            )
            biases.append(mask_bias(allowed, room, r, c, 4 * AREA))
            query_list.append(read_tile(queries, r, c))
            key_list.append(
                jnp.concatenate(
                    [read_tile(keys, r, c), near, far_k[far], far_k2[far2]], axis=0
                )
            )
        parts, highest = weigh(query_list, key_list, biases)
        totals = [jnp.sum(part, axis=1, keepdims=True) for part in parts]
        for (r, c), part, sum_here, top in zip(here, parts, totals, highest):
            index = r * tile_cols + c
            weights[index] = part.astype(jnp.bfloat16)
            sums = jnp.where(lane == index, top + jnp.log(sum_here), sums)
        return sums

    sums_out[...] = tile_groups(
        tile_rows, tile_cols, weigh_tiles, jnp.zeros((AREA, DH), jnp.float32)
    )


def own_mix_kernel(
    tile_rows, tile_cols, one, two, place, weights, own_s, near_s, near_rest, far_s, far_rest,
    far_s2, mixed,
):
    def mix_tiles(here, carry):
        totals = []
        for r, c in here:
            index = r * tile_cols + c
            home = place[0, index]
            near = two_part(near_s, near_rest, home, one, two)
            far = two_part(far_s, far_rest, place[1, index], one, two)
            far2 = far_s2[jnp.minimum(place[1, index], two - 1)]
            values_here = jnp.concatenate([own_s[home], near, far, far2], axis=0)
            totals.append(mix(weights[index], values_here))
        for (r, c), (total, sum_here) in zip(here, totals):
            mixed[r * tile_cols + c] = (total / sum_here).astype(jnp.bfloat16)
        return carry

    tile_groups(tile_rows, tile_cols, mix_tiles, 0)


def combine_kernel(
    tile_rows, tile_cols, one, three, me, reach, place, rows_ok, cols_ok, own_s, own_o, own_sums,
    near_ones, far_ones, out, held, sems,
):
    mine = me[0]
    outer = (mine == 0) | (mine == 3)
    row_limit, col_limit = rows_ok[mine], cols_ok[mine]
    lane = lax.broadcasted_iota(jnp.int32, (AREA, DH), 1)
    their_sums = far_ones[three].astype(jnp.float32)
    their_sums += far_ones[three + 1].astype(jnp.float32)
    their_sums += far_ones[three + 2].astype(jnp.float32)
    my_sums = own_sums[...]

    def store_row(r):
        rows = pl.ds(r * TS, TS)
        return pltpu.make_async_copy(held.at[rows], out.at[rows], sems.at[r])

    def combine_row(r, carry):
        for c in range(tile_cols):
            index = r * tile_cols + c
            spot = jnp.minimum(place[1, index], one - 1)
            remote = outer & (reach[1, index] >= 1)
            gap = jnp.where(lane == spot, their_sums, 0.0) - jnp.where(lane == index, my_sums, 0.0)
            gap = jnp.sum(gap, axis=1, keepdims=True)
            share = 1.0 / (1.0 + jnp.exp(gap))
            share = jnp.where(remote, share, 1.0)
            theirs = far_ones[jnp.minimum(spot, three - 1)].astype(jnp.float32)
            if one > three:
                other = near_ones[jnp.maximum(spot - three, 0)].astype(jnp.float32)
                theirs = jnp.where(spot < three, theirs, other)
            mine_o = own_o[index].astype(jnp.float32)
            temporal = jnp.where(remote, share * mine_o + (1.0 - share) * theirs, mine_o)
            temporal = temporal.astype(jnp.bfloat16).astype(jnp.float32)
            spatial = own_s[place[0, index]].astype(jnp.float32)
            valid = row_valid(r, c, row_limit, col_limit)
            tile = jnp.where(valid, spatial + temporal, 0.0)
            held[pl.ds(r * TS, TS), c] = tile.astype(jnp.bfloat16).reshape(TS, TS, DH)
        store_row(r).start()
        return carry

    lax.fori_loop(0, tile_rows, combine_row, 0)
    for r in range(tile_rows):
        store_row(r).wait()


def run_kernel(
    kernel, out_shape, scalars, arrays, scratch=(), scalar_outs=0, micros=4, from_hbm=0,
    to_hbm=False,
):
    outs = list(out_shape)
    arrays = [
        pltpu.with_memory_space_constraint(array, pltpu.HBM) if number < from_hbm else array
        for number, array in enumerate(arrays)
    ]
    in_hbm = pl.BlockSpec(memory_space=pltpu.HBM)
    out_specs = [vector_spec()] * (len(outs) - scalar_outs) + [scalar_spec()] * scalar_outs
    in_specs = [in_hbm] * from_hbm + [vector_spec()] * (len(arrays) - from_hbm)
    return pl.pallas_call(
        kernel,
        out_shape=outs,
        in_specs=[scalar_spec()] * len(scalars) + in_specs,
        out_specs=[in_hbm] if to_hbm else out_specs,
        scratch_shapes=list(scratch),
        compiler_params=pltpu.CompilerParams(vmem_limit_bytes=VMEM_LIMIT),
        cost_estimate=pl.CostEstimate(
            flops=int(micros * 1e9), bytes_accessed=int(micros * 1e6), transcendentals=0
        ),
    )(*scalars, *arrays)


def room_levels(count):
    shares = ((49, 34, 21), (51, 37, 24), (54, 41, 27))
    levels = [tuple(max(count * share // 60, 1) for share in level) for level in shares]
    return levels + [(count, count, count)]


def four_frames(queries, keys, values, back_reach, fwd_reach, valid_rows, valid_cols):
    _, token_rows, token_cols, _ = queries.shape
    tile_rows, tile_cols = token_rows // TS, token_cols // TS
    count = tile_rows * tile_cols
    shape = (token_rows, tile_cols, TS, DH)
    queries, keys, values = queries.reshape(shape), keys.reshape(shape), values.reshape(shape)
    me = lax.axis_index("frame").reshape(1).astype(jnp.int32)
    inward, across, outward = [(0, 1), (3, 2)], [(1, 2), (2, 1)], [(1, 0), (2, 3)]
    levels = room_levels(count)

    def tiles(number):
        return jax.ShapeDtypeStruct((number, AREA, DH), jnp.bfloat16)

    def ints(*sizes):
        return jax.ShapeDtypeStruct(sizes, jnp.int32)

    def send(array, pairs):
        return lax.ppermute(array, "frame", pairs)

    packed_k, reach, place, order, level = run_kernel(
        functools.partial(pack_kernel, tile_rows, tile_cols, levels),
        (tiles(count), ints(2, count), ints(2, count), ints(count), ints(1)),
        (me,),
        (back_reach, fwd_reach, keys),
        scratch=(
            pltpu.SMEM((tile_rows, tile_cols), jnp.int32),
            pltpu.SMEM((tile_rows, tile_cols), jnp.int32),
            pltpu.VMEM(shape, jnp.bfloat16),
            pltpu.SemaphoreType.DMA((3,)),
        ),
        scalar_outs=4,
        micros=2,
        from_hbm=3,
    )

    def with_room(one, two, three):
        def run(queries, keys, values, packed_k, reach, place, order):
            far_k = send(packed_k[:one], across)
            near_k = send(packed_k[:two], inward)
            own_s, packed_q = run_kernel(
                functools.partial(spatial_kernel, tile_rows, tile_cols),
                (tiles(count), tiles(count)),
                (me, place, valid_rows, valid_cols),
                (queries, keys, values),
                scratch=(
                    pltpu.VMEM((count * AREA, DH), jnp.bfloat16),
                    pltpu.VMEM((count * AREA, DH), jnp.bfloat16),
                    pltpu.VMEM((count * AREA, 2 * DH), jnp.bfloat16),
                    pltpu.VMEM((tile_rows, 8, tile_cols * AREA), jnp.float32),
                    pltpu.VMEM((tile_rows, 8, (tile_cols - 2) * AREA), jnp.float32),
                ),
                micros=10,
            )
            far_s = send(own_s[:two], across)
            near_s = send(own_s[:two], inward)
            hosted_qa = send(packed_q[three:one], inward) if one > three else None
            hosted_qb = send(packed_q[:three], inward)
            far_k2 = send(near_k, across)
            far_s2 = send(near_s, across)
            near_rest_k, near_rest_s, far_rest_s = near_k, near_s, far_s
            if one > two:
                rest_k, rest_s, far_k, _ = lax.optimization_barrier(
                    (packed_k[two:one], own_s[two:one], far_k, near_s)
                )
                near_rest_k = send(rest_k, inward)
                near_rest_s = send(rest_s, inward)
                far_rest_s = send(rest_s, across)
            sums = jnp.zeros((AREA, DH), jnp.float32)
            returned_a = near_k
            if one > three:
                hosted_a, sums = run_kernel(
                    functools.partial(near_hosted_kernel, tile_cols, one, two, three),
                    (tiles(one - three), jax.ShapeDtypeStruct((AREA, DH), jnp.float32)),
                    (me, reach, place, order, valid_rows, valid_cols),
                    (hosted_qa, packed_k, far_k, own_s, far_s),
                    micros=3,
                )
                returned_a = send(hosted_a, outward)
            hosted_w, sums = run_kernel(
                functools.partial(far_hosted_kernel, tile_cols, three),
                (jax.ShapeDtypeStruct((three, AREA, 4 * AREA), jnp.bfloat16), tiles(3)),
                (me, reach, place, order, valid_rows, valid_cols),
                (hosted_qb, packed_k, far_k, far_k2, sums),
                micros=3,
            )
            hosted_w, near_k = lax.optimization_barrier((hosted_w, near_k))
            own_w, own_sums = run_kernel(
                functools.partial(own_weights_kernel, tile_rows, tile_cols, one, two),
                (
                    jax.ShapeDtypeStruct((count, AREA, 4 * AREA), jnp.bfloat16),
                    jax.ShapeDtypeStruct((AREA, DH), jnp.float32),
                ),
                (me, reach, place, valid_rows, valid_cols),
                (queries, keys, near_k, near_rest_k, far_k, far_k2),
                micros=5,
            )
            hosted_w, own_w = lax.optimization_barrier((hosted_w, own_w))
            (hosted_b,) = run_kernel(
                functools.partial(far_mix_kernel, three),
                (tiles(three + 3),),
                (place, order),
                (hosted_w, own_s, far_s, far_s2, sums),
                micros=0.5,
            )
            returned_b = send(hosted_b, outward)
            (own_o,) = run_kernel(
                functools.partial(own_mix_kernel, tile_rows, tile_cols, one, two),
                (tiles(count),),
                (place,),
                (own_w, own_s, near_s, near_rest_s, far_s, far_rest_s, far_s2),
                micros=1,
            )
            (out,) = run_kernel(
                functools.partial(combine_kernel, tile_rows, tile_cols, one, three),
                (pltpu.HBM(shape, jnp.bfloat16),),
                (me, reach, place, valid_rows, valid_cols),
                (own_s, own_o, own_sums, returned_a, returned_b),
                scratch=(pltpu.VMEM(shape, jnp.bfloat16), pltpu.SemaphoreType.DMA((tile_rows,))),
                micros=2,
                to_hbm=True,
            )
            return out

        return run

    branches = [with_room(*level) for level in levels]
    operands = (queries, keys, values, packed_k, reach, place, order)
    out = lax.switch(level[0], branches, *operands)
    return out.reshape(1, token_rows, token_cols, DH)


def solution(mesh):
    in_specs = (
        P(("dp", "frame"), None, None, "row"),
        P(("dp", "frame"), None, None, "row"),
        P(("dp", "frame"), None, None, "row"),
        P("dp", None),
        P("dp", None),
        P("dp"),
        P("dp"),
    )
    out_specs = P(("dp", "frame"), None, None, "row")

    def block(*args):
        frames, _, token_cols, channels = args[0].shape
        line = mesh.shape["frame"] == 4 and frames == 1 and channels == DH
        if line and token_cols % (2 * TS) == 0 and 4 <= token_cols // TS:
            return four_frames(*args)
        return per_device(*args)

    return jax.shard_map(
        block, mesh=mesh, in_specs=in_specs, out_specs=out_specs, check_vma=False
    )
```

```python
import functools
import math

import jax
import jax.numpy as jnp
from jax import lax
from jax.experimental import pallas as pl
from jax.experimental.pallas import tpu as pltpu
from jax.sharding import PartitionSpec as P

DH = 128
TS = 8


def group_size(item_count, row_count):
    size = 1
    for option in range(1, item_count + 1):
        if item_count % option == 0 and option * row_count <= 1024:
            size = option
    return size


def attend_group(group_parts):
    query_rows, key_rows, value_rows, allowed = group_parts
    dot_terms = jnp.einsum("gmd,gnd->gmn", query_rows, key_rows, preferred_element_type=jnp.float32)
    query_sq = jnp.einsum("gmd,gmd->gm", query_rows, query_rows, preferred_element_type=jnp.float32)
    key_sq = jnp.einsum("gnd,gnd->gn", key_rows, key_rows, preferred_element_type=jnp.float32)
    distance = query_sq[:, :, None] + key_sq[:, None, :] - 2.0 * dot_terms
    scores = jnp.where(allowed, -distance * (0.5 / math.sqrt(query_rows.shape[2])), -jnp.inf)
    highest = jnp.max(scores, axis=2, keepdims=True)
    weights = jnp.exp(scores - highest)
    totals = jnp.sum(weights, axis=2, keepdims=True)
    mixed = jnp.einsum(
        "gmn,gnd->gmd", weights.astype(jnp.bfloat16), value_rows, preferred_element_type=jnp.float32
    )
    return mixed / totals


def attend_items(query_items, key_items, value_items, masks):
    item_count = query_items.shape[0]
    per_group = group_size(item_count, query_items.shape[1])
    groups = item_count // per_group

    def regroup(array):
        return array.reshape((groups, per_group) + array.shape[1:])

    mixed = lax.map(
        attend_group,
        (regroup(query_items), regroup(key_items), regroup(value_items), regroup(masks)),
    )
    return mixed.reshape((item_count,) + mixed.shape[2:])


def tile_split(block):
    frames, token_rows, token_cols, channels = block.shape
    heads = channels // DH
    return (
        block.reshape(frames, token_rows // TS, TS, token_cols // TS, TS, heads, DH)
        .transpose(5, 0, 1, 3, 2, 4, 6)
        .reshape(heads, frames, token_rows // TS * (token_cols // TS), TS * TS, DH)
    )


def neighbours(tiles, tile_rows, tile_cols):
    heads, frames, count_tiles, area, depth = tiles.shape
    grid = tiles.reshape(heads * frames, tile_rows, tile_cols, area, depth)
    padded = jnp.pad(grid, ((0, 0), (1, 1), (1, 1), (0, 0), (0, 0)))
    views = [
        padded[:, dy : dy + tile_rows, dx : dx + tile_cols] for dy in range(3) for dx in range(3)
    ]
    stacked = jnp.stack(views, axis=3)
    return stacked.reshape(heads * frames * count_tiles, 9 * area, depth)


def pad_tiles(tiles, total):
    return jnp.pad(tiles, ((0, 0), (0, 0), (0, total - tiles.shape[2]), (0, 0), (0, 0)))


def per_device(queries, keys, values, back_reach, fwd_reach, valid_rows, valid_cols):
    frames, token_rows, token_cols, channels = queries.shape
    heads = channels // DH
    tile_rows = token_rows // TS
    tile_cols = token_cols // TS
    count_tiles = tile_rows * tile_cols
    area = TS * TS
    frame_count = lax.axis_size("frame")
    frame_index = lax.axis_index("frame")
    padded_count = (count_tiles + frame_count - 1) // frame_count * frame_count
    tiles_here = padded_count // frame_count
    all_frames = frames * frame_count
    row_ids = jnp.arange(token_rows, dtype=jnp.int32)
    col_ids = jnp.arange(token_cols, dtype=jnp.int32)
    row_ok = row_ids[None, :] < valid_rows[:, None]
    col_ok = col_ids[None, :] < valid_cols[:, None]
    token_valid = row_ok[:, :, None] & col_ok[:, None, :]
    tile_valid_all = (
        token_valid.reshape(all_frames, tile_rows, TS, tile_cols, TS)
        .transpose(0, 1, 3, 2, 4)
        .reshape(all_frames, tile_rows, tile_cols, area)
    )
    tile_valid = lax.dynamic_slice_in_dim(tile_valid_all, frame_index * frames, frames, 0)
    padded_valid = jnp.pad(tile_valid, ((0, 0), (1, 1), (1, 1), (0, 0)))
    near_valid = jnp.stack(
        [
            padded_valid[:, dy : dy + tile_rows, dx : dx + tile_cols]
            for dy in range(3)
            for dx in range(3)
        ],
        axis=3,
    )
    near_valid = near_valid.reshape(frames, count_tiles, 1, 9 * area)
    query_factor = tile_valid.reshape(frames, count_tiles, area).astype(jnp.float32)
    query_t = tile_split(queries)
    key_t = tile_split(keys)
    masks = near_valid[None].reshape(heads * frames * count_tiles, 1, 9 * area)
    spatial = attend_items(
        query_t.reshape(heads * frames * count_tiles, area, DH),
        neighbours(key_t, tile_rows, tile_cols),
        neighbours(tile_split(values), tile_rows, tile_cols),
        masks,
    )
    spatial = spatial.reshape(heads, frames, count_tiles, area, DH)
    spatial_t = (spatial * query_factor[None, :, :, :, None]).astype(jnp.bfloat16)
    triple = jnp.stack(
        [
            pad_tiles(query_t, padded_count),
            pad_tiles(key_t, padded_count),
            pad_tiles(spatial_t, padded_count),
        ]
    )
    sent = lax.all_to_all(triple, "frame", split_axis=3, concat_axis=2, tiled=True)
    query_here, key_here, value_here = (sent[0], sent[1], sent[2])
    start = frame_index * tiles_here
    length = all_frames * area
    frame_of = jnp.arange(length, dtype=jnp.int32) // area
    frame_gap = frame_of[None, :] - frame_of[:, None]
    valid_flat = tile_valid_all.reshape(all_frames, count_tiles, area).transpose(1, 0, 2)
    valid_flat = jnp.pad(
        valid_flat, ((0, padded_count - count_tiles), (0, 0), (0, 0)), constant_values=True
    )
    valid_here = lax.dynamic_slice_in_dim(valid_flat, start, tiles_here, 0)
    back_here = lax.dynamic_slice_in_dim(
        jnp.pad(back_reach.reshape(count_tiles), (0, padded_count - count_tiles)),
        start,
        tiles_here,
        0,
    )
    fwd_here = lax.dynamic_slice_in_dim(
        jnp.pad(fwd_reach.reshape(count_tiles), (0, padded_count - count_tiles)),
        start,
        tiles_here,
        0,
    )
    key_ok = valid_here.reshape(tiles_here, length)
    allowed = (
        (frame_gap[None] >= -back_here[:, None, None])
        & (frame_gap[None] <= fwd_here[:, None, None])
        & key_ok[:, None, :]
    )
    time_masks = allowed[None].reshape(heads * tiles_here, length, length)

    def by_tile(array):
        return array.transpose(0, 2, 1, 3, 4).reshape(heads * tiles_here, length, DH)

    temporal = attend_items(
        by_tile(query_here), by_tile(key_here), by_tile(value_here), time_masks
    ).astype(jnp.bfloat16)
    temporal = temporal.reshape(heads, tiles_here, all_frames, area, DH).transpose(0, 2, 1, 3, 4)
    returned = lax.all_to_all(temporal, "frame", split_axis=1, concat_axis=2, tiled=True)[
        :, :, :count_tiles
    ]
    combined = (spatial_t.astype(jnp.float32) + returned.astype(jnp.float32)) * query_factor[
        None, :, :, :, None
    ]
    combined = combined.astype(jnp.bfloat16).reshape(
        heads, frames, tile_rows, tile_cols, TS, TS, DH
    )
    return combined.transpose(1, 2, 4, 3, 5, 0, 6).reshape(frames, token_rows, token_cols, channels)


SCALE = 1.0 / math.sqrt(DH)
MASKED = -1e30
AREA = TS * TS
GROUP = 10
VMEM_LIMIT = 24 * 1024 * 1024
NT_DIMS = (((1,), (1,)), ((), ()))


def scalar_spec():
    return pl.BlockSpec(memory_space=pltpu.SMEM)


def vector_spec():
    return pl.BlockSpec(memory_space=pltpu.VMEM)


def read_tile(ref, row, col):
    return ref[pl.ds(row * TS, TS), col].reshape(AREA, DH)


def key_norms(keys):
    wide = keys.astype(jnp.float32)
    square = wide * wide
    high = square.astype(jnp.bfloat16)
    low = (square - high.astype(jnp.float32)).astype(jnp.bfloat16)
    ones = jnp.ones((8, 2 * DH), jnp.bfloat16)
    both = jnp.concatenate([high, low], axis=1)
    total = lax.dot_general(ones, both, NT_DIMS, preferred_element_type=jnp.float32)
    return total * (-0.5 * SCALE)


def row_valid(row, col, row_limit, col_limit):
    token = lax.broadcasted_iota(jnp.int32, (AREA, DH), 0)
    return (row * TS + (token >> 3) < row_limit) & (col * TS + (token & 7) < col_limit)


def pack_kernel(
    tile_rows, tile_cols, levels, me, back_in, fwd_in, keys, packed, reach, place, order, level,
    back, fwd, held, sems,
):
    load = pltpu.make_async_copy(keys, held, sems.at[0])
    loads = [
        pltpu.make_async_copy(back_in, back, sems.at[1]),
        pltpu.make_async_copy(fwd_in, fwd, sems.at[2]),
    ]
    for one in loads:
        one.start()
    load.start()
    for one in loads:
        one.wait()
    left = me[0] < 2
    most = [None] * 4
    tiles = [(r, c) for r in range(tile_rows) for c in range(tile_cols)]
    for way in range(2):
        counts = [jnp.int32(0)] * 4
        for index, (r, c) in enumerate(tiles):
            toward, away = back[r, c], fwd[r, c]
            value = jnp.where(left, toward, away) if way == 0 else jnp.where(left, away, toward)
            reach[way, index] = value
            counts = [counts[v] + (value >= v).astype(jnp.int32) for v in range(4)]
        for v in (1, 2, 3):
            most[v] = counts[v] if way == 0 else jnp.maximum(most[v], counts[v])
        spots = [counts[1], counts[2], counts[3], jnp.int32(0)]
        for index in range(len(tiles)):
            value = jnp.minimum(reach[way, index], 3)
            spot = spots[0]
            for v in (1, 2, 3):
                spot = jnp.where(value == v, spots[v], spot)
            spots = [spots[v] + (value == v).astype(jnp.int32) for v in range(4)]
            place[way, index] = spot
            if way == 1:
                order[spot] = index
    chosen = jnp.int32(0)
    for one, two, three in levels[:-1]:
        over = (most[1] > one) | (most[2] > two) | (most[3] > three)
        chosen += over.astype(jnp.int32)
    level[0] = chosen
    load.wait()

    def pack_row(r, carry):
        for c in range(tile_cols):
            packed[place[0, r * tile_cols + c]] = read_tile(held, r, c)
        return carry

    lax.fori_loop(0, tile_rows, pack_row, 0)


def spatial_kernel(
    tile_rows, tile_cols, me, place, rows_ok, cols_ok, queries, keys, values, mixed, packed_q,
    query_t, key_t, value_t, bias_even, bias_odd,
):
    row_limit, col_limit = rows_ok[me[0]], cols_ok[me[0]]
    wide = tile_cols * AREA
    value_t[:, DH:] = jnp.ones((value_t.shape[0], DH), jnp.bfloat16)

    def lane_bias(r, first, count):
        start = pl.multiple_of((r * tile_cols + first) * AREA, AREA)
        norms = key_norms(key_t[pl.ds(start, count * AREA)])
        lane = lax.broadcasted_iota(jnp.int32, (8, count * AREA), 1) + first * AREA
        valid = (r * TS + ((lane >> 3) & 7) < row_limit) & (
            (lane >> 6) * TS + (lane & 7) < col_limit
        )
        return jnp.where(valid, norms, MASKED)

    def retile_row(r, carry):
        for c in range(tile_cols):
            index = r * tile_cols + c
            span = pl.ds(pl.multiple_of(index * AREA, AREA), AREA)
            tile_q = read_tile(queries, r, c)
            query_t[span] = tile_q
            packed_q[place[1, index]] = tile_q
            key_t[span] = read_tile(keys, r, c)
            value_t[span, :DH] = read_tile(values, r, c)
        bias_even[r] = lane_bias(r, 0, tile_cols)
        bias_odd[r] = lane_bias(r, 1, tile_cols - 2)
        return carry

    lax.fori_loop(0, tile_rows, retile_row, 0)
    lane_tile = lax.broadcasted_iota(jnp.int32, (8, 4 * AREA), 1) >> 6

    def attend_row(r, carry):
        first_row = jnp.clip(r - 1, 0, tile_rows - 3)
        for pair in range(tile_cols // 2):
            first_col = min(max(2 * pair - 1, 0), tile_cols - 4)
            index = r * tile_cols + 2 * pair
            query = query_t[pl.ds(pl.multiple_of(index * AREA, AREA), 2 * AREA)]
            scores, spans = [], []
            for step in range(3):
                key_row = first_row + step
                start = (key_row * tile_cols + first_col) * AREA
                span = pl.ds(pl.multiple_of(start, AREA), 4 * AREA)
                spans.append(span)
                dots = lax.dot_general(
                    query, key_t[span], NT_DIMS, preferred_element_type=jnp.float32
                )
                if first_col % 2:
                    lane_start = (first_col - 1) * AREA
                    bias = bias_odd[key_row, :, lane_start : lane_start + 4 * AREA]
                else:
                    lane_start = first_col * AREA
                    bias = bias_even[key_row, :, lane_start : lane_start + 4 * AREA]
                near_row = jnp.abs(key_row - r) <= 1
                both = []
                for half in range(2):
                    gap = lane_tile + (first_col - 2 * pair - half)
                    near = (gap >= -1) & (gap <= 1) & near_row
                    part = dots[half * AREA : (half + 1) * AREA].reshape(TS, 8, 4 * AREA)
                    part = part * SCALE + jnp.where(near, bias, MASKED)[None]
                    both.append(part.reshape(AREA, 4 * AREA))
                scores.append(jnp.concatenate(both, axis=0))
            highest = jnp.maximum(jnp.maximum(scores[0], scores[1]), scores[2])
            highest = jnp.max(highest, axis=1, keepdims=True)
            total = None
            for step in range(3):
                weights = jnp.exp(scores[step] - highest).astype(jnp.bfloat16)
                part = jnp.dot(weights, value_t[spans[step]], preferred_element_type=jnp.float32)
                total = part if total is None else total + part
            result = total[:, :DH] / total[:, DH:]
            for half in range(2):
                valid = row_valid(r, 2 * pair + half, row_limit, col_limit)
                tile = jnp.where(valid, result[half * AREA : (half + 1) * AREA], 0.0)
                mixed[place[0, index + half]] = tile.astype(jnp.bfloat16)
        return carry

    lax.fori_loop(0, tile_rows, attend_row, 0)


def frames_of(mine):
    left = mine < 2
    return mine, jnp.where(left, 0, 3), jnp.where(left, 2, 1), jnp.where(left, 3, 0)


def by_block(picks, lanes):
    block = lax.broadcasted_iota(jnp.int32, (8, lanes), 1) >> 6
    chosen = jnp.full((8, lanes), picks[0], jnp.int32)
    for number in range(1, lanes // AREA):
        chosen = jnp.where(block == number, picks[number], chosen)
    return chosen


def room_left(frames, rows_ok, cols_ok, lanes):
    lane = lax.broadcasted_iota(jnp.int32, (8, lanes), 1)
    row_room = by_block([rows_ok[frame] for frame in frames], lanes) - ((lane >> 3) & 7)
    col_room = by_block([cols_ok[frame] for frame in frames], lanes) - (lane & 7)
    return row_room, col_room


def weigh(queries, keys_here, biases):
    parts, highest = [], []
    dots = [
        lax.dot_general(query, key, NT_DIMS, preferred_element_type=jnp.float32)
        for query, key in zip(queries, keys_here)
    ]
    norms = [key_norms(key) for key in keys_here]
    for dot, norm, bias in zip(dots, norms, biases):
        lanes = dot.shape[1]
        part = dot.reshape(TS, 8, lanes) * SCALE + (norm + bias)[None]
        parts.append(part.reshape(AREA, lanes))
    highest = [jnp.max(part, axis=1, keepdims=True) for part in parts]
    return [jnp.exp(part - top) for part, top in zip(parts, highest)], highest


def mask_bias(allowed, room, row, col, lanes):
    valid = (room[0] > row * TS) & (room[1] > col * TS) & (by_block(allowed, lanes) > 0)
    return jnp.where(valid, 0.0, MASKED)


def mix(weights, values_here):
    ones = jnp.ones(values_here.shape, jnp.bfloat16)
    total = jnp.dot(
        weights,
        jnp.concatenate([values_here, ones], axis=1),
        preferred_element_type=jnp.float32,
    )
    return total[:, :DH], total[:, DH:]


def in_chunks(first, last, body, carry):
    size = max(option for option in range(1, 11) if (last - first) % option == 0)

    def chunk(number, carry):
        return body([first + number * size + step for step in range(size)], carry)

    return lax.fori_loop(0, (last - first) // size, chunk, carry)


def is_inner(mine):
    return (mine == 1) | (mine == 2)


def store_sums(ref, first, sums):
    for step in range(3):
        piece = sums.astype(jnp.bfloat16)
        ref[first + step] = piece
        sums = sums - piece.astype(jnp.float32)


def load_sums(ref, first):
    pieces = [ref[first + step].astype(jnp.float32) for step in range(3)]
    return (pieces[0] + pieces[1]) + pieces[2]


def reached(reach, index, least):
    return (reach[1, index] >= least).astype(jnp.int32)


def near_hosted_kernel(
    tile_cols, one, two, three, me, reach, place, order, rows_ok, cols_ok, hosted_q, packed_k,
    far_k, own_s, far_s, mixed,
):
    own, _, far, _ = frames_of(me[0])
    room = room_left((own, far), rows_ok, cols_ok, 2 * AREA)
    lane = lax.broadcasted_iota(jnp.int32, (AREA, DH), 1)

    def near_ones(spots, sums):
        indices = [order[spot] for spot in spots]
        rows = [lax.div(index, tile_cols) for index in indices]
        homes = [place[0, index] for index in indices]
        keys_here = [
            jnp.concatenate([packed_k[home], far_k[spot]], axis=0)
            for home, spot in zip(homes, spots)
        ]
        values_here = [
            jnp.concatenate([own_s[home], far_s[jnp.minimum(spot, two - 1)]], axis=0)
            for home, spot in zip(homes, spots)
        ]
        biases = [
            mask_bias(
                (reached(reach, index, 1), reached(reach, index, 2)),
                room, row, index - row * tile_cols, 2 * AREA,
            )
            for index, row in zip(indices, rows)
        ]
        parts, highest = weigh([hosted_q[spot - three] for spot in spots], keys_here, biases)
        totals = [mix(part.astype(jnp.bfloat16), v) for part, v in zip(parts, values_here)]
        for spot, (total, sum_here), top in zip(spots, totals, highest):
            mixed[spot - three] = (total / sum_here).astype(jnp.bfloat16)
            sums = jnp.where(lane == spot, top + jnp.log(sum_here), sums)
        return sums

    @pl.when(is_inner(me[0]))
    def _():
        sums = in_chunks(three, one, near_ones, jnp.zeros((AREA, DH), jnp.float32))
        store_sums(mixed, one - three, sums)


def far_hosted_kernel(
    tile_cols, three, me, reach, place, order, rows_ok, cols_ok, hosted_q, packed_k, far_k,
    far_k2, weights, sums_out,
):
    own, _, far, far2 = frames_of(me[0])
    room = room_left((own, far, far2, own), rows_ok, cols_ok, 4 * AREA)
    lane = lax.broadcasted_iota(jnp.int32, (AREA, DH), 1)
    no = jnp.int32(0)

    def far_ones(spots, sums):
        indices = [order[spot] for spot in spots]
        rows = [lax.div(index, tile_cols) for index in indices]
        homes = [packed_k[place[0, index]] for index in indices]
        keys_here = [
            jnp.concatenate([home, far_k[spot], far_k2[spot], home], axis=0)
            for home, spot in zip(homes, spots)
        ]
        biases = [
            mask_bias(
                tuple(reached(reach, index, least) for least in (1, 2, 3)) + (no,),
                room, row, index - row * tile_cols, 4 * AREA,
            )
            for index, row in zip(indices, rows)
        ]
        parts, highest = weigh([hosted_q[spot] for spot in spots], keys_here, biases)
        for spot, part, top in zip(spots, parts, highest):
            weights[spot] = part.astype(jnp.bfloat16)
            sum_here = jnp.sum(part, axis=1, keepdims=True)
            sums = jnp.where(lane == spot, top + jnp.log(sum_here), sums)
        return sums

    @pl.when(is_inner(me[0]))
    def _():
        sums = in_chunks(0, three, far_ones, jnp.zeros((AREA, DH), jnp.float32))
        store_sums(sums_out, 0, sums)


def far_mix_kernel(three, me, place, order, weights, own_s, far_s, far_s2, sums, mixed):
    def far_ones(spots, carry):
        homes = [own_s[place[0, order[spot]]] for spot in spots]
        totals = [
            mix(weights[spot], jnp.concatenate([home, far_s[spot], far_s2[spot], home], axis=0))
            for spot, home in zip(spots, homes)
        ]
        for spot, (total, sum_here) in zip(spots, totals):
            mixed[spot] = (total / sum_here).astype(jnp.bfloat16)
        return carry

    @pl.when(is_inner(me[0]))
    def _():
        in_chunks(0, three, far_ones, 0)
        mixed[three : three + 3] = sums[...]


def tile_groups(tile_rows, tile_cols, body, carry):
    rows = 1

    def step(number, carry):
        here = [(number * rows + r, c) for r in range(rows) for c in range(tile_cols)]
        for first in range(0, len(here), GROUP):
            carry = body(here[first : first + GROUP], carry)
        return carry

    return lax.fori_loop(0, tile_rows // rows, step, carry)


def two_part(first, rest, spot, split, last, start=0):
    tile = first[jnp.minimum(spot, split - 1)]
    if last > split:
        other = rest[start + jnp.clip(spot - split, 0, last - split - 1)]
        tile = jnp.where(spot < split, tile, other)
    return tile


def own_weights_kernel(
    tile_rows, tile_cols, one, two, me, reach, place, rows_ok, cols_ok, queries, keys, near_k,
    near_rest, far_k, far_k2, weights, sums_out,
):
    mine = me[0]
    inner = is_inner(mine)
    room = room_left(frames_of(mine), rows_ok, cols_ok, 4 * AREA)
    lane = lax.broadcasted_iota(jnp.int32, (AREA, DH), 1)

    def weigh_tiles(here, sums):
        query_list, key_list, biases = [], [], []
        for r, c in here:
            index = r * tile_cols + c
            near = two_part(near_k, near_rest, place[0, index], two, one)
            far = jnp.minimum(place[1, index], one - 1)
            far2 = jnp.minimum(place[1, index], two - 1)
            near_reach, far_reach = reach[0, index], reach[1, index]
            allowed = (
                jnp.int32(1),
                (inner & (near_reach >= 1)).astype(jnp.int32),
                (inner & (far_reach >= 1)).astype(jnp.int32),
                (inner & (far_reach >= 2)).astype(jnp.int32),
            )
            biases.append(mask_bias(allowed, room, r, c, 4 * AREA))
            query_list.append(read_tile(queries, r, c))
            key_list.append(
                jnp.concatenate(
                    [read_tile(keys, r, c), near, far_k[far], far_k2[far2]], axis=0
                )
            )
        parts, highest = weigh(query_list, key_list, biases)
        totals = [jnp.sum(part, axis=1, keepdims=True) for part in parts]
        for (r, c), part, sum_here, top in zip(here, parts, totals, highest):
            index = r * tile_cols + c
            weights[index] = part.astype(jnp.bfloat16)
            sums = jnp.where(lane == index, top + jnp.log(sum_here), sums)
        return sums

    sums_out[...] = tile_groups(
        tile_rows, tile_cols, weigh_tiles, jnp.zeros((AREA, DH), jnp.float32)
    )


def merged(own, own_sums, theirs, their_sums, index, spot):
    lane = lax.broadcasted_iota(jnp.int32, (AREA, DH), 1)
    gap = jnp.where(lane == spot, their_sums, 0.0) - jnp.where(lane == index, own_sums, 0.0)
    share = 1.0 / (1.0 + jnp.exp(jnp.sum(gap, axis=1, keepdims=True)))
    return share * own + (1.0 - share) * theirs.astype(jnp.float32)


def finished(spatial, temporal, valid):
    temporal = temporal.astype(jnp.bfloat16).astype(jnp.float32)
    tile = jnp.where(valid, spatial.astype(jnp.float32) + temporal, 0.0)
    return tile.astype(jnp.bfloat16).reshape(TS, TS, DH)


def own_mix_kernel(
    tile_rows, tile_cols, one, two, three, me, reach, place, rows_ok, cols_ok, weights, own_sums,
    own_s, near_s, near_rest, far_s, far_s2, late, near_ones, mixed, out, held, sems,
):
    mine = me[0]
    outer = jnp.logical_not(is_inner(mine))
    row_limit, col_limit = rows_ok[mine], cols_ok[mine]
    my_sums = own_sums[...]
    if one > three:
        their_sums = load_sums(near_ones, one - three)

    def store_row(r):
        rows = pl.ds(r * TS, TS)
        return pltpu.make_async_copy(held.at[rows], out.at[rows], sems.at[r])

    def mix_row(r, carry):
        totals = []
        for c in range(tile_cols):
            index = r * tile_cols + c
            home, spot = place[0, index], place[1, index]
            near = two_part(near_s, near_rest, home, two, one, one - two)
            far = two_part(far_s, late, spot, two, one, two - three)
            far2 = two_part(far_s2, late, spot, three, two)
            values_here = jnp.concatenate([own_s[home], near, far, far2], axis=0)
            totals.append(mix(weights[index], values_here))
        results = []
        for c, (total, sum_here) in enumerate(totals):
            index = r * tile_cols + c
            result = total / sum_here
            mixed[index] = result.astype(jnp.bfloat16)
            if one > three:
                spot = place[1, index]
                remote = outer & (reach[1, index] >= 1)
                theirs = near_ones[jnp.clip(spot - three, 0, one - three - 1)]
                both = merged(result, my_sums, theirs, their_sums, index, spot)
                result = jnp.where(remote, both, result)
            results.append(result)
        for c, result in enumerate(results):
            valid = row_valid(r, c, row_limit, col_limit)
            spatial = own_s[place[0, r * tile_cols + c]]
            held[pl.ds(r * TS, TS), c] = finished(spatial, result, valid)
        store_row(r).start()
        return carry

    lax.fori_loop(0, tile_rows, mix_row, 0)
    for r in range(tile_rows):
        store_row(r).wait()


def patch_kernel(
    tile_cols, three, me, reach, place, order, rows_ok, cols_ok, done, own_s, own_o, own_sums,
    far_ones, out, held, sem,
):
    mine = me[0]
    row_limit, col_limit = rows_ok[mine], cols_ok[mine]

    def store_tile(spot):
        index = order[spot]
        r = lax.div(index, tile_cols)
        target = out.at[pl.ds(r * TS, TS), index - r * tile_cols]
        return pltpu.make_async_copy(held.at[spot], target, sem.at[spot])

    @pl.when(jnp.logical_not(is_inner(mine)))
    def _():
        my_sums = own_sums[...]
        their_sums = load_sums(far_ones, three)

        def patch(spots, carry):
            tiles = []
            for spot in spots:
                index = order[spot]
                own = own_o[index].astype(jnp.float32)
                both = merged(own, my_sums, far_ones[spot], their_sums, index, spot)
                tiles.append(jnp.where(reach[1, index] >= 1, both, own))
            for spot, tile in zip(spots, tiles):
                index = order[spot]
                r = lax.div(index, tile_cols)
                valid = row_valid(r, index - r * tile_cols, row_limit, col_limit)
                held[spot] = finished(own_s[place[0, index]], tile, valid)
                store_tile(spot).start()
            return carry

        in_chunks(0, three, patch, 0)

        def wait(spot, carry):
            store_tile(spot).wait()
            return carry

        lax.fori_loop(0, three, wait, 0)


def run_kernel(
    kernel, out_shape, scalars, arrays, scratch=(), scalar_outs=0, micros=4, from_hbm=0,
    to_hbm=0, in_place=False,
):
    outs = list(out_shape)
    arrays = [
        pltpu.with_memory_space_constraint(array, pltpu.HBM) if number < from_hbm else array
        for number, array in enumerate(arrays)
    ]
    in_hbm = pl.BlockSpec(memory_space=pltpu.HBM)
    in_specs = [in_hbm] * from_hbm + [vector_spec()] * (len(arrays) - from_hbm)
    out_specs = [vector_spec()] * (len(outs) - scalar_outs - to_hbm)
    out_specs += [scalar_spec()] * scalar_outs + [in_hbm] * to_hbm
    return pl.pallas_call(
        kernel,
        out_shape=outs,
        in_specs=[scalar_spec()] * len(scalars) + in_specs,
        out_specs=out_specs,
        scratch_shapes=list(scratch),
        input_output_aliases={len(scalars): 0} if in_place else {},
        compiler_params=pltpu.CompilerParams(vmem_limit_bytes=VMEM_LIMIT),
        cost_estimate=pl.CostEstimate(
            flops=int(micros * 1e9), bytes_accessed=int(micros * 1e6), transcendentals=0
        ),
    )(*scalars, *arrays)


def room_levels(count):
    shares = ((49, 34, 21), (51, 37, 24), (54, 41, 27))
    levels = [tuple(max(count * share // 60, 1) for share in level) for level in shares]
    return levels + [(count, count, count)]


def four_frames(queries, keys, values, back_reach, fwd_reach, valid_rows, valid_cols):
    _, token_rows, token_cols, _ = queries.shape
    tile_rows, tile_cols = token_rows // TS, token_cols // TS
    count = tile_rows * tile_cols
    shape = (token_rows, tile_cols, TS, DH)
    queries, keys, values = queries.reshape(shape), keys.reshape(shape), values.reshape(shape)
    me = lax.axis_index("frame").reshape(1).astype(jnp.int32)
    inward, across, outward = [(0, 1), (3, 2)], [(1, 2), (2, 1)], [(1, 0), (2, 3)]
    levels = room_levels(count)

    def tiles(number):
        return jax.ShapeDtypeStruct((number, AREA, DH), jnp.bfloat16)

    def ints(*sizes):
        return jax.ShapeDtypeStruct(sizes, jnp.int32)

    def send(array, pairs):
        return lax.ppermute(array, "frame", pairs)

    packed_k, reach, place, order, level = run_kernel(
        functools.partial(pack_kernel, tile_rows, tile_cols, levels),
        (tiles(count), ints(2, count), ints(2, count), ints(count), ints(1)),
        (me,),
        (back_reach, fwd_reach, keys),
        scratch=(
            pltpu.SMEM((tile_rows, tile_cols), jnp.int32),
            pltpu.SMEM((tile_rows, tile_cols), jnp.int32),
            pltpu.VMEM(shape, jnp.bfloat16),
            pltpu.SemaphoreType.DMA((3,)),
        ),
        scalar_outs=4,
        micros=2,
        from_hbm=3,
    )

    def with_room(one, two, three):
        def run(queries, keys, values, packed_k, reach, place, order):
            far_k = send(packed_k[:one], across)
            near_k = send(packed_k[:two], inward)
            own_s, packed_q = run_kernel(
                functools.partial(spatial_kernel, tile_rows, tile_cols),
                (tiles(count), tiles(count)),
                (me, place, valid_rows, valid_cols),
                (queries, keys, values),
                scratch=(
                    pltpu.VMEM((count * AREA, DH), jnp.bfloat16),
                    pltpu.VMEM((count * AREA, DH), jnp.bfloat16),
                    pltpu.VMEM((count * AREA, 2 * DH), jnp.bfloat16),
                    pltpu.VMEM((tile_rows, 8, tile_cols * AREA), jnp.float32),
                    pltpu.VMEM((tile_rows, 8, (tile_cols - 2) * AREA), jnp.float32),
                ),
                micros=10,
            )
            far_s = send(own_s[:two], across)
            near_s = send(own_s[:two], inward)
            hosted_qa = send(packed_q[three:one], inward) if one > three else None
            hosted_qb = send(packed_q[:three], inward)
            far_k2 = send(near_k, across)
            far_s2 = send(near_s[:three], across)
            near_rest, late = near_k, near_s
            if one > two:
                rest = jnp.concatenate([packed_k[two:one], own_s[two:one]])
                rest, far_k, _ = lax.optimization_barrier((rest, far_k, near_s))
                near_rest = send(rest, inward)
            if one > three:
                late = send(jnp.concatenate([near_s[three:two], own_s[two:one]]), across)
            returned_a = near_k
            if one > three:
                (hosted_a,) = run_kernel(
                    functools.partial(near_hosted_kernel, tile_cols, one, two, three),
                    (tiles(one - three + 3),),
                    (me, reach, place, order, valid_rows, valid_cols),
                    (hosted_qa, packed_k, far_k, own_s, far_s),
                    micros=3,
                )
                returned_a = send(hosted_a, outward)
            hosted_w, sums = run_kernel(
                functools.partial(far_hosted_kernel, tile_cols, three),
                (jax.ShapeDtypeStruct((three, AREA, 4 * AREA), jnp.bfloat16), tiles(3)),
                (me, reach, place, order, valid_rows, valid_cols),
                (hosted_qb, packed_k, far_k, far_k2),
                micros=3,
            )
            (hosted_b,) = run_kernel(
                functools.partial(far_mix_kernel, three),
                (tiles(three + 3),),
                (me, place, order),
                (hosted_w, own_s, far_s, far_s2, sums),
                micros=0.5,
            )
            returned_b = send(hosted_b, outward)
            hosted_b, near_k = lax.optimization_barrier((hosted_b, near_k))
            own_w, own_sums = run_kernel(
                functools.partial(own_weights_kernel, tile_rows, tile_cols, one, two),
                (
                    jax.ShapeDtypeStruct((count, AREA, 4 * AREA), jnp.bfloat16),
                    jax.ShapeDtypeStruct((AREA, DH), jnp.float32),
                ),
                (me, reach, place, valid_rows, valid_cols),
                (queries, keys, near_k, near_rest, far_k, far_k2),
                micros=1,
            )
            own_o, out = run_kernel(
                functools.partial(own_mix_kernel, tile_rows, tile_cols, one, two, three),
                (tiles(count), pltpu.HBM(shape, jnp.bfloat16)),
                (me, reach, place, valid_rows, valid_cols),
                (own_w, own_sums, own_s, near_s, near_rest, far_s, far_s2, late, returned_a),
                scratch=(pltpu.VMEM(shape, jnp.bfloat16), pltpu.SemaphoreType.DMA((tile_rows,))),
                micros=0.5,
                to_hbm=1,
            )
            (out,) = run_kernel(
                functools.partial(patch_kernel, tile_cols, three),
                (pltpu.HBM(shape, jnp.bfloat16),),
                (me, reach, place, order, valid_rows, valid_cols),
                (out, own_s, own_o, own_sums, returned_b),
                scratch=(
                    pltpu.VMEM((three, TS, TS, DH), jnp.bfloat16),
                    pltpu.SemaphoreType.DMA((three,)),
                ),
                micros=1,
                from_hbm=1,
                to_hbm=1,
                in_place=True,
            )
            return out

        return run

    branches = [with_room(*level) for level in levels]
    operands = (queries, keys, values, packed_k, reach, place, order)
    out = lax.switch(level[0], branches, *operands)
    return out.reshape(1, token_rows, token_cols, DH)


def solution(mesh):
    in_specs = (
        P(("dp", "frame"), None, None, "row"),
        P(("dp", "frame"), None, None, "row"),
        P(("dp", "frame"), None, None, "row"),
        P("dp", None),
        P("dp", None),
        P("dp"),
        P("dp"),
    )
    out_specs = P(("dp", "frame"), None, None, "row")

    def block(*args):
        frames, _, token_cols, channels = args[0].shape
        line = mesh.shape["frame"] == 4 and frames == 1 and channels == DH
        if line and token_cols % (2 * TS) == 0 and 4 <= token_cols // TS:
            return four_frames(*args)
        return per_device(*args)

    return jax.shard_map(
        block, mesh=mesh, in_specs=in_specs, out_specs=out_specs, check_vma=False
    )
```

```python
import functools
import math

import jax
import jax.numpy as jnp
from jax import lax
from jax.experimental import pallas as pl
from jax.experimental.pallas import tpu as pltpu
from jax.sharding import PartitionSpec as P

DH = 128
TS = 8


def group_size(item_count, row_count):
    size = 1
    for option in range(1, item_count + 1):
        if item_count % option == 0 and option * row_count <= 1024:
            size = option
    return size


def attend_group(group_parts):
    query_rows, key_rows, value_rows, allowed = group_parts
    dot_terms = jnp.einsum("gmd,gnd->gmn", query_rows, key_rows, preferred_element_type=jnp.float32)
    query_sq = jnp.einsum("gmd,gmd->gm", query_rows, query_rows, preferred_element_type=jnp.float32)
    key_sq = jnp.einsum("gnd,gnd->gn", key_rows, key_rows, preferred_element_type=jnp.float32)
    distance = query_sq[:, :, None] + key_sq[:, None, :] - 2.0 * dot_terms
    scores = jnp.where(allowed, -distance * (0.5 / math.sqrt(query_rows.shape[2])), -jnp.inf)
    highest = jnp.max(scores, axis=2, keepdims=True)
    weights = jnp.exp(scores - highest)
    totals = jnp.sum(weights, axis=2, keepdims=True)
    mixed = jnp.einsum(
        "gmn,gnd->gmd", weights.astype(jnp.bfloat16), value_rows, preferred_element_type=jnp.float32
    )
    return mixed / totals


def attend_items(query_items, key_items, value_items, masks):
    item_count = query_items.shape[0]
    per_group = group_size(item_count, query_items.shape[1])
    groups = item_count // per_group

    def regroup(array):
        return array.reshape((groups, per_group) + array.shape[1:])

    mixed = lax.map(
        attend_group,
        (regroup(query_items), regroup(key_items), regroup(value_items), regroup(masks)),
    )
    return mixed.reshape((item_count,) + mixed.shape[2:])


def tile_split(block):
    frames, token_rows, token_cols, channels = block.shape
    heads = channels // DH
    return (
        block.reshape(frames, token_rows // TS, TS, token_cols // TS, TS, heads, DH)
        .transpose(5, 0, 1, 3, 2, 4, 6)
        .reshape(heads, frames, token_rows // TS * (token_cols // TS), TS * TS, DH)
    )


def neighbours(tiles, tile_rows, tile_cols):
    heads, frames, count_tiles, area, depth = tiles.shape
    grid = tiles.reshape(heads * frames, tile_rows, tile_cols, area, depth)
    padded = jnp.pad(grid, ((0, 0), (1, 1), (1, 1), (0, 0), (0, 0)))
    views = [
        padded[:, dy : dy + tile_rows, dx : dx + tile_cols] for dy in range(3) for dx in range(3)
    ]
    stacked = jnp.stack(views, axis=3)
    return stacked.reshape(heads * frames * count_tiles, 9 * area, depth)


def pad_tiles(tiles, total):
    return jnp.pad(tiles, ((0, 0), (0, 0), (0, total - tiles.shape[2]), (0, 0), (0, 0)))


def per_device(queries, keys, values, back_reach, fwd_reach, valid_rows, valid_cols):
    frames, token_rows, token_cols, channels = queries.shape
    heads = channels // DH
    tile_rows = token_rows // TS
    tile_cols = token_cols // TS
    count_tiles = tile_rows * tile_cols
    area = TS * TS
    frame_count = lax.axis_size("frame")
    frame_index = lax.axis_index("frame")
    padded_count = (count_tiles + frame_count - 1) // frame_count * frame_count
    tiles_here = padded_count // frame_count
    all_frames = frames * frame_count
    row_ids = jnp.arange(token_rows, dtype=jnp.int32)
    col_ids = jnp.arange(token_cols, dtype=jnp.int32)
    row_ok = row_ids[None, :] < valid_rows[:, None]
    col_ok = col_ids[None, :] < valid_cols[:, None]
    token_valid = row_ok[:, :, None] & col_ok[:, None, :]
    tile_valid_all = (
        token_valid.reshape(all_frames, tile_rows, TS, tile_cols, TS)
        .transpose(0, 1, 3, 2, 4)
        .reshape(all_frames, tile_rows, tile_cols, area)
    )
    tile_valid = lax.dynamic_slice_in_dim(tile_valid_all, frame_index * frames, frames, 0)
    padded_valid = jnp.pad(tile_valid, ((0, 0), (1, 1), (1, 1), (0, 0)))
    near_valid = jnp.stack(
        [
            padded_valid[:, dy : dy + tile_rows, dx : dx + tile_cols]
            for dy in range(3)
            for dx in range(3)
        ],
        axis=3,
    )
    near_valid = near_valid.reshape(frames, count_tiles, 1, 9 * area)
    query_factor = tile_valid.reshape(frames, count_tiles, area).astype(jnp.float32)
    query_t = tile_split(queries)
    key_t = tile_split(keys)
    masks = near_valid[None].reshape(heads * frames * count_tiles, 1, 9 * area)
    spatial = attend_items(
        query_t.reshape(heads * frames * count_tiles, area, DH),
        neighbours(key_t, tile_rows, tile_cols),
        neighbours(tile_split(values), tile_rows, tile_cols),
        masks,
    )
    spatial = spatial.reshape(heads, frames, count_tiles, area, DH)
    spatial_t = (spatial * query_factor[None, :, :, :, None]).astype(jnp.bfloat16)
    triple = jnp.stack(
        [
            pad_tiles(query_t, padded_count),
            pad_tiles(key_t, padded_count),
            pad_tiles(spatial_t, padded_count),
        ]
    )
    sent = lax.all_to_all(triple, "frame", split_axis=3, concat_axis=2, tiled=True)
    query_here, key_here, value_here = (sent[0], sent[1], sent[2])
    start = frame_index * tiles_here
    length = all_frames * area
    frame_of = jnp.arange(length, dtype=jnp.int32) // area
    frame_gap = frame_of[None, :] - frame_of[:, None]
    valid_flat = tile_valid_all.reshape(all_frames, count_tiles, area).transpose(1, 0, 2)
    valid_flat = jnp.pad(
        valid_flat, ((0, padded_count - count_tiles), (0, 0), (0, 0)), constant_values=True
    )
    valid_here = lax.dynamic_slice_in_dim(valid_flat, start, tiles_here, 0)
    back_here = lax.dynamic_slice_in_dim(
        jnp.pad(back_reach.reshape(count_tiles), (0, padded_count - count_tiles)),
        start,
        tiles_here,
        0,
    )
    fwd_here = lax.dynamic_slice_in_dim(
        jnp.pad(fwd_reach.reshape(count_tiles), (0, padded_count - count_tiles)),
        start,
        tiles_here,
        0,
    )
    key_ok = valid_here.reshape(tiles_here, length)
    allowed = (
        (frame_gap[None] >= -back_here[:, None, None])
        & (frame_gap[None] <= fwd_here[:, None, None])
        & key_ok[:, None, :]
    )
    time_masks = allowed[None].reshape(heads * tiles_here, length, length)

    def by_tile(array):
        return array.transpose(0, 2, 1, 3, 4).reshape(heads * tiles_here, length, DH)

    temporal = attend_items(
        by_tile(query_here), by_tile(key_here), by_tile(value_here), time_masks
    ).astype(jnp.bfloat16)
    temporal = temporal.reshape(heads, tiles_here, all_frames, area, DH).transpose(0, 2, 1, 3, 4)
    returned = lax.all_to_all(temporal, "frame", split_axis=1, concat_axis=2, tiled=True)[
        :, :, :count_tiles
    ]
    combined = (spatial_t.astype(jnp.float32) + returned.astype(jnp.float32)) * query_factor[
        None, :, :, :, None
    ]
    combined = combined.astype(jnp.bfloat16).reshape(
        heads, frames, tile_rows, tile_cols, TS, TS, DH
    )
    return combined.transpose(1, 2, 4, 3, 5, 0, 6).reshape(frames, token_rows, token_cols, channels)


SCALE = 1.0 / math.sqrt(DH)
MASKED = -1e30
AREA = TS * TS
GROUP = 10
VMEM_LIMIT = 24 * 1024 * 1024
NT_DIMS = (((1,), (1,)), ((), ()))


def scalar_spec():
    return pl.BlockSpec(memory_space=pltpu.SMEM)


def vector_spec():
    return pl.BlockSpec(memory_space=pltpu.VMEM)


def read_tile(ref, row, col):
    return ref[pl.ds(row * TS, TS), col].reshape(AREA, DH)


def key_norms(keys):
    wide = keys.astype(jnp.float32)
    square = wide * wide
    high = square.astype(jnp.bfloat16)
    low = (square - high.astype(jnp.float32)).astype(jnp.bfloat16)
    ones = jnp.ones((8, 2 * DH), jnp.bfloat16)
    both = jnp.concatenate([high, low], axis=1)
    total = lax.dot_general(ones, both, NT_DIMS, preferred_element_type=jnp.float32)
    return total * (-0.5 * SCALE)


def row_valid(row, col, row_limit, col_limit):
    token = lax.broadcasted_iota(jnp.int32, (AREA, DH), 0)
    return (row * TS + (token >> 3) < row_limit) & (col * TS + (token & 7) < col_limit)


def pack_kernel(
    tile_rows, tile_cols, levels, me, back, fwd, keys, packed, reach, place, order, level, held,
    sem,
):
    load = pltpu.make_async_copy(keys, held, sem)
    load.start()
    left = me[0] < 2
    most = [None] * 4
    tiles = [(r, c) for r in range(tile_rows) for c in range(tile_cols)]
    for way in range(2):
        counts = [jnp.int32(0)] * 4
        for index, (r, c) in enumerate(tiles):
            toward, away = back[r, c], fwd[r, c]
            value = jnp.where(left, toward, away) if way == 0 else jnp.where(left, away, toward)
            reach[way, index] = value
            counts = [counts[v] + (value >= v).astype(jnp.int32) for v in range(4)]
        for v in (1, 2, 3):
            most[v] = counts[v] if way == 0 else jnp.maximum(most[v], counts[v])
        spots = [counts[1], counts[2], counts[3], jnp.int32(0)]
        for index in range(len(tiles)):
            value = jnp.minimum(reach[way, index], 3)
            spot = spots[0]
            for v in (1, 2, 3):
                spot = jnp.where(value == v, spots[v], spot)
            spots = [spots[v] + (value == v).astype(jnp.int32) for v in range(4)]
            place[way, index] = spot
            if way == 1:
                order[spot] = index
    chosen = jnp.int32(0)
    for one, two, three in levels[:-1]:
        over = (most[1] > one) | (most[2] > two) | (most[3] > three)
        chosen += over.astype(jnp.int32)
    level[0] = chosen
    load.wait()

    def pack_row(r, carry):
        for c in range(tile_cols):
            packed[place[0, r * tile_cols + c]] = read_tile(held, r, c)
        return carry

    lax.fori_loop(0, tile_rows, pack_row, 0)


def spatial_kernel(
    tile_rows, tile_cols, me, place, rows_ok, cols_ok, queries, keys, values, mixed, packed_q,
    query_t, key_t, value_t, bias_even, bias_odd,
):
    row_limit, col_limit = rows_ok[me[0]], cols_ok[me[0]]
    wide = tile_cols * AREA
    value_t[:, DH:] = jnp.ones((value_t.shape[0], DH), jnp.bfloat16)

    def lane_bias(r, first, count):
        start = pl.multiple_of((r * tile_cols + first) * AREA, AREA)
        norms = key_norms(key_t[pl.ds(start, count * AREA)])
        lane = lax.broadcasted_iota(jnp.int32, (8, count * AREA), 1) + first * AREA
        valid = (r * TS + ((lane >> 3) & 7) < row_limit) & (
            (lane >> 6) * TS + (lane & 7) < col_limit
        )
        return jnp.where(valid, norms, MASKED)

    def retile_row(r, carry):
        for c in range(tile_cols):
            index = r * tile_cols + c
            span = pl.ds(pl.multiple_of(index * AREA, AREA), AREA)
            tile_q = read_tile(queries, r, c)
            query_t[span] = tile_q
            packed_q[place[1, index]] = tile_q
            key_t[span] = read_tile(keys, r, c)
            value_t[span, :DH] = read_tile(values, r, c)
        bias_even[r] = lane_bias(r, 0, tile_cols)
        bias_odd[r] = lane_bias(r, 1, tile_cols - 2)
        return carry

    lax.fori_loop(0, tile_rows, retile_row, 0)
    lane_tile = lax.broadcasted_iota(jnp.int32, (8, 4 * AREA), 1) >> 6

    def attend_row(r, carry):
        first_row = jnp.clip(r - 1, 0, tile_rows - 3)
        for pair in range(tile_cols // 2):
            first_col = min(max(2 * pair - 1, 0), tile_cols - 4)
            index = r * tile_cols + 2 * pair
            query = query_t[pl.ds(pl.multiple_of(index * AREA, AREA), 2 * AREA)]
            scores, spans = [], []
            for step in range(3):
                key_row = first_row + step
                start = (key_row * tile_cols + first_col) * AREA
                span = pl.ds(pl.multiple_of(start, AREA), 4 * AREA)
                spans.append(span)
                dots = lax.dot_general(
                    query, key_t[span], NT_DIMS, preferred_element_type=jnp.float32
                )
                if first_col % 2:
                    lane_start = (first_col - 1) * AREA
                    bias = bias_odd[key_row, :, lane_start : lane_start + 4 * AREA]
                else:
                    lane_start = first_col * AREA
                    bias = bias_even[key_row, :, lane_start : lane_start + 4 * AREA]
                near_row = jnp.abs(key_row - r) <= 1
                both = []
                for half in range(2):
                    gap = lane_tile + (first_col - 2 * pair - half)
                    near = (gap >= -1) & (gap <= 1) & near_row
                    part = dots[half * AREA : (half + 1) * AREA].reshape(TS, 8, 4 * AREA)
                    part = part * SCALE + jnp.where(near, bias, MASKED)[None]
                    both.append(part.reshape(AREA, 4 * AREA))
                scores.append(jnp.concatenate(both, axis=0))
            highest = jnp.maximum(jnp.maximum(scores[0], scores[1]), scores[2])
            highest = jnp.max(highest, axis=1, keepdims=True)
            total = None
            for step in range(3):
                weights = jnp.exp(scores[step] - highest).astype(jnp.bfloat16)
                part = jnp.dot(weights, value_t[spans[step]], preferred_element_type=jnp.float32)
                total = part if total is None else total + part
            result = total[:, :DH] / total[:, DH:]
            for half in range(2):
                valid = row_valid(r, 2 * pair + half, row_limit, col_limit)
                tile = jnp.where(valid, result[half * AREA : (half + 1) * AREA], 0.0)
                mixed[place[0, index + half]] = tile.astype(jnp.bfloat16)
        return carry

    lax.fori_loop(0, tile_rows, attend_row, 0)


def frames_of(mine):
    left = mine < 2
    return mine, jnp.where(left, 0, 3), jnp.where(left, 2, 1), jnp.where(left, 3, 0)


def by_block(picks, lanes):
    block = lax.broadcasted_iota(jnp.int32, (8, lanes), 1) >> 6
    chosen = jnp.full((8, lanes), picks[0], jnp.int32)
    for number in range(1, lanes // AREA):
        chosen = jnp.where(block == number, picks[number], chosen)
    return chosen


def room_left(frames, rows_ok, cols_ok, lanes):
    lane = lax.broadcasted_iota(jnp.int32, (8, lanes), 1)
    row_room = by_block([rows_ok[frame] for frame in frames], lanes) - ((lane >> 3) & 7)
    col_room = by_block([cols_ok[frame] for frame in frames], lanes) - (lane & 7)
    return row_room, col_room


def weigh(queries, keys_here, biases):
    parts, highest = [], []
    dots = [
        lax.dot_general(query, key, NT_DIMS, preferred_element_type=jnp.float32)
        for query, key in zip(queries, keys_here)
    ]
    norms = [key_norms(key) for key in keys_here]
    for dot, norm, bias in zip(dots, norms, biases):
        lanes = dot.shape[1]
        part = dot.reshape(TS, 8, lanes) * SCALE + (norm + bias)[None]
        parts.append(part.reshape(AREA, lanes))
    highest = [jnp.max(part, axis=1, keepdims=True) for part in parts]
    return [jnp.exp(part - top) for part, top in zip(parts, highest)], highest


def mask_bias(allowed, room, row, col, lanes):
    valid = (room[0] > row * TS) & (room[1] > col * TS) & (by_block(allowed, lanes) > 0)
    return jnp.where(valid, 0.0, MASKED)


def mix(weights, values_here):
    ones = jnp.ones(values_here.shape, jnp.bfloat16)
    total = jnp.dot(
        weights,
        jnp.concatenate([values_here, ones], axis=1),
        preferred_element_type=jnp.float32,
    )
    return total[:, :DH], total[:, DH:]


def in_chunks(first, last, body, carry):
    size = max(option for option in range(1, 16) if (last - first) % option == 0)

    if size == last - first:
        return body(list(range(first, last)), carry)

    def chunk(number, carry):
        return body([first + number * size + step for step in range(size)], carry)

    return lax.fori_loop(0, (last - first) // size, chunk, carry)


def is_inner(mine):
    return (mine == 1) | (mine == 2)


def store_sums(ref, first, sums):
    for step in range(3):
        piece = sums.astype(jnp.bfloat16)
        ref[first + step] = piece
        sums = sums - piece.astype(jnp.float32)


def load_sums(ref, first):
    pieces = [ref[first + step].astype(jnp.float32) for step in range(3)]
    return (pieces[0] + pieces[1]) + pieces[2]


def reached(reach, index, least):
    return (reach[1, index] >= least).astype(jnp.int32)


def near_hosted_kernel(
    tile_cols, one, two, three, me, reach, place, order, rows_ok, cols_ok, hosted_q, packed_k,
    far_k, own_s, far_s, mixed,
):
    own, _, far, _ = frames_of(me[0])
    room = room_left((own, far), rows_ok, cols_ok, 2 * AREA)
    lane = lax.broadcasted_iota(jnp.int32, (AREA, DH), 1)

    def near_ones(spots, sums):
        indices = [order[spot] for spot in spots]
        rows = [lax.div(index, tile_cols) for index in indices]
        homes = [place[0, index] for index in indices]
        keys_here = [
            jnp.concatenate([packed_k[home], far_k[jnp.minimum(spot, two - 1)]], axis=0)
            for home, spot in zip(homes, spots)
        ]
        values_here = [
            jnp.concatenate([own_s[home], far_s[jnp.minimum(spot, two - 1)]], axis=0)
            for home, spot in zip(homes, spots)
        ]
        biases = [
            mask_bias(
                (reached(reach, index, 1), reached(reach, index, 2)),
                room, row, index - row * tile_cols, 2 * AREA,
            )
            for index, row in zip(indices, rows)
        ]
        parts, highest = weigh([hosted_q[spot - three] for spot in spots], keys_here, biases)
        totals = [mix(part.astype(jnp.bfloat16), v) for part, v in zip(parts, values_here)]
        for spot, (total, sum_here), top in zip(spots, totals, highest):
            mixed[spot - three] = (total / sum_here).astype(jnp.bfloat16)
            sums = jnp.where(lane == spot, top + jnp.log(sum_here), sums)
        return sums

    @pl.when(is_inner(me[0]))
    def _():
        sums = in_chunks(three, one, near_ones, jnp.zeros((AREA, DH), jnp.float32))
        store_sums(mixed, one - three, sums)


def far_hosted_kernel(
    tile_cols, three, me, reach, place, order, rows_ok, cols_ok, hosted_q, packed_k, far_k,
    far_k2, weights, sums_out,
):
    own, _, far, far2 = frames_of(me[0])
    room = room_left((own, far, far2, own), rows_ok, cols_ok, 4 * AREA)
    lane = lax.broadcasted_iota(jnp.int32, (AREA, DH), 1)
    no = jnp.int32(0)

    def far_ones(spots, sums):
        indices = [order[spot] for spot in spots]
        rows = [lax.div(index, tile_cols) for index in indices]
        homes = [packed_k[place[0, index]] for index in indices]
        keys_here = [
            jnp.concatenate([home, far_k[spot], far_k2[spot], home], axis=0)
            for home, spot in zip(homes, spots)
        ]
        biases = [
            mask_bias(
                tuple(reached(reach, index, least) for least in (1, 2, 3)) + (no,),
                room, row, index - row * tile_cols, 4 * AREA,
            )
            for index, row in zip(indices, rows)
        ]
        parts, highest = weigh([hosted_q[spot] for spot in spots], keys_here, biases)
        for spot, part, top in zip(spots, parts, highest):
            weights[spot] = part.astype(jnp.bfloat16)
            sum_here = jnp.sum(part, axis=1, keepdims=True)
            sums = jnp.where(lane == spot, top + jnp.log(sum_here), sums)
        return sums

    @pl.when(is_inner(me[0]))
    def _():
        sums = in_chunks(0, three, far_ones, jnp.zeros((AREA, DH), jnp.float32))
        store_sums(sums_out, 0, sums)


def far_mix_kernel(three, me, place, order, weights, own_s, far_s, far_s2, sums, mixed):
    def far_ones(spots, carry):
        homes = [own_s[place[0, order[spot]]] for spot in spots]
        totals = [
            mix(weights[spot], jnp.concatenate([home, far_s[spot], far_s2[spot], home], axis=0))
            for spot, home in zip(spots, homes)
        ]
        for spot, (total, sum_here) in zip(spots, totals):
            mixed[spot] = (total / sum_here).astype(jnp.bfloat16)
        return carry

    @pl.when(is_inner(me[0]))
    def _():
        in_chunks(0, three, far_ones, 0)
        mixed[three : three + 3] = sums[...]


def tile_groups(tile_rows, tile_cols, body, carry):
    rows = 1

    def step(number, carry):
        here = [(number * rows + r, c) for r in range(rows) for c in range(tile_cols)]
        for first in range(0, len(here), GROUP):
            carry = body(here[first : first + GROUP], carry)
        return carry

    return lax.fori_loop(0, tile_rows // rows, step, carry)


def two_part(first, rest, spot, split, last, start=0):
    tile = first[jnp.minimum(spot, split - 1)]
    if last > split:
        other = rest[start + jnp.clip(spot - split, 0, last - split - 1)]
        tile = jnp.where(spot < split, tile, other)
    return tile


def own_weights_kernel(
    tile_rows, tile_cols, one, two, me, reach, place, rows_ok, cols_ok, queries, keys, near_k,
    near_rest, far_k, far_k2, weights, sums_out,
):
    mine = me[0]
    inner = is_inner(mine)
    room = room_left(frames_of(mine), rows_ok, cols_ok, 4 * AREA)
    lane = lax.broadcasted_iota(jnp.int32, (AREA, DH), 1)

    def weigh_tiles(here, sums):
        query_list, key_list, biases = [], [], []
        for r, c in here:
            index = r * tile_cols + c
            near = two_part(near_k, near_rest, place[0, index], two, one)
            far = far_k[jnp.minimum(place[1, index], two - 1)]
            far2 = jnp.minimum(place[1, index], two - 1)
            near_reach, far_reach = reach[0, index], reach[1, index]
            allowed = (
                jnp.int32(1),
                (inner & (near_reach >= 1)).astype(jnp.int32),
                (inner & (far_reach >= 1)).astype(jnp.int32),
                (inner & (far_reach >= 2)).astype(jnp.int32),
            )
            biases.append(mask_bias(allowed, room, r, c, 4 * AREA))
            query_list.append(read_tile(queries, r, c))
            key_list.append(
                jnp.concatenate(
                    [read_tile(keys, r, c), near, far, far_k2[far2]], axis=0
                )
            )
        parts, highest = weigh(query_list, key_list, biases)
        totals = [jnp.sum(part, axis=1, keepdims=True) for part in parts]
        for (r, c), part, sum_here, top in zip(here, parts, totals, highest):
            index = r * tile_cols + c
            weights[index] = part.astype(jnp.bfloat16)
            sums = jnp.where(lane == index, top + jnp.log(sum_here), sums)
        return sums

    sums_out[...] = tile_groups(
        tile_rows, tile_cols, weigh_tiles, jnp.zeros((AREA, DH), jnp.float32)
    )


def merged(own, own_sums, theirs, their_sums, index, spot):
    lane = lax.broadcasted_iota(jnp.int32, (AREA, DH), 1)
    gap = jnp.where(lane == spot, their_sums, 0.0) - jnp.where(lane == index, own_sums, 0.0)
    share = 1.0 / (1.0 + jnp.exp(jnp.sum(gap, axis=1, keepdims=True)))
    return share * own + (1.0 - share) * theirs.astype(jnp.float32)


def finished(spatial, temporal, valid):
    temporal = temporal.astype(jnp.bfloat16).astype(jnp.float32)
    tile = jnp.where(valid, spatial.astype(jnp.float32) + temporal, 0.0)
    return tile.astype(jnp.bfloat16).reshape(TS, TS, DH)


def tile_store(tile_cols, order, held, out, sems, spot):
    index = order[spot]
    r = lax.div(index, tile_cols)
    target = out.at[pl.ds(r * TS, TS), index - r * tile_cols]
    return pltpu.make_async_copy(held.at[spot], target, sems.at[spot])


def wait_stores(first, last, store):
    def wait(spot, carry):
        store(spot).wait()
        return carry

    lax.fori_loop(first, last, wait, 0)


def own_mix_kernel(
    tile_cols, count, one, two, three, me, reach, place, order, rows_ok, cols_ok, weights,
    own_sums, own_s, near_s, near_rest, far_s, far_s2, near_ones, first_o, out, held, sems,
):
    mine = me[0]
    inner = is_inner(mine)
    row_limit, col_limit = rows_ok[mine], cols_ok[mine]
    my_sums = own_sums[...]
    store = functools.partial(tile_store, tile_cols, order, held, out, sems)

    def mix_tiles(spots, their_sums):
        indices = [order[spot] for spot in spots]
        homes = [place[0, index] for index in indices]
        totals = []
        for spot, index, home in zip(spots, indices, homes):
            near = two_part(near_s, near_rest, home, two, one, one - two)
            far = far_s[jnp.minimum(spot, two - 1)]
            far2 = far_s2[jnp.minimum(spot, three - 1)]
            values_here = jnp.concatenate([own_s[home], near, far, far2], axis=0)
            totals.append(mix(weights[index], values_here))
        results = [total / sum_here for total, sum_here in totals]
        if their_sums is not None:
            for number, (spot, index) in enumerate(zip(spots, indices)):
                theirs = near_ones[spot - three]
                both = merged(results[number], my_sums, theirs, their_sums, index, spot)
                results[number] = jnp.where(reach[1, index] >= 1, both, results[number])
        for spot, index, home, result in zip(spots, indices, homes, results):
            r = lax.div(index, tile_cols)
            valid = row_valid(r, index - r * tile_cols, row_limit, col_limit)
            held[spot] = finished(own_s[home], result, valid)
            store(spot).start()
        return results

    def first_tiles(spots, carry):
        for spot, result in zip(spots, mix_tiles(spots, None)):
            first_o[spot] = result.astype(jnp.bfloat16)
        return carry

    def other_tiles(spots, carry):
        mix_tiles(spots, carry)
        return carry

    in_chunks(0, three, first_tiles, 0)
    if count > one:
        in_chunks(one, count, other_tiles, None)
    if one > three:

        @pl.when(jnp.logical_not(inner))
        def _():
            in_chunks(three, one, other_tiles, load_sums(near_ones, one - three))
            wait_stores(three, one, store)

    wait_stores(0, three, store)
    wait_stores(one, count, store)


def last_kernel(
    tile_cols, one, two, three, me, reach, place, order, rows_ok, cols_ok, done, weights, queries,
    packed_k, near_k, own_s, near_s, near_rest, far_s, late, own_sums, first_o, far_ones, out,
    held, sems,
):
    mine = me[0]
    inner = is_inner(mine)
    row_limit, col_limit = rows_ok[mine], cols_ok[mine]
    store = functools.partial(tile_store, tile_cols, order, held, out, sems)

    def finish(spots, results):
        for spot, result in zip(spots, results):
            index = order[spot]
            r = lax.div(index, tile_cols)
            valid = row_valid(r, index - r * tile_cols, row_limit, col_limit)
            held[spot] = finished(own_s[place[0, index]], result, valid)
            store(spot).start()

    def near_part(first, rest_start, home):
        return two_part(first, near_rest, home, two, one, rest_start)

    def late_mix(spot):
        index = order[spot]
        home = place[0, index]
        near = near_part(near_s, one - two, home)
        values_here = jnp.concatenate(
            [own_s[home], near, far_s[spot], late[spot - three]], axis=0
        )
        return mix(weights[index], values_here)

    def weigh_last(spots):
        room = room_left(frames_of(mine), rows_ok, cols_ok, 4 * AREA)
        query_list, key_list, value_list, biases = [], [], [], []
        for spot in spots:
            index = order[spot]
            r = lax.div(index, tile_cols)
            c = index - r * tile_cols
            home = place[0, index]
            allowed = (
                jnp.int32(1),
                (reach[0, index] >= 1).astype(jnp.int32),
                (reach[1, index] >= 1).astype(jnp.int32),
                jnp.int32(0),
            )
            biases.append(mask_bias(allowed, room, r, c, 4 * AREA))
            query_list.append(read_tile(queries, r, c))
            own, far = packed_k[home], late[spot - three + one - two]
            near = near_part(near_k, 0, home)
            key_list.append(jnp.concatenate([own, near, far, own], axis=0))
            own, far = own_s[home], late[spot - three]
            near = near_part(near_s, one - two, home)
            value_list.append(jnp.concatenate([own, near, far, own], axis=0))
        parts, _ = weigh(query_list, key_list, biases)
        return [part.astype(jnp.bfloat16) for part in parts], value_list

    if one > three:

        @pl.when(inner)
        def _():
            parts, value_list = weigh_last(range(two, one)) if one > two else ([], [])
            totals = [late_mix(spot) for spot in range(three, two)]
            totals += [mix(part, v) for part, v in zip(parts, value_list)]
            finish(range(three, one), [total / sum_here for total, sum_here in totals])
            wait_stores(three, one, store)

    @pl.when(jnp.logical_not(inner))
    def _():
        my_sums = own_sums[...]
        their_sums = load_sums(far_ones, three)

        def far_tiles(spots, carry):
            results = []
            for spot in spots:
                index = order[spot]
                own = first_o[spot].astype(jnp.float32)
                both = merged(own, my_sums, far_ones[spot], their_sums, index, spot)
                results.append(jnp.where(reach[1, index] >= 1, both, own))
            finish(spots, results)
            return carry

        in_chunks(0, three, far_tiles, 0)
        wait_stores(0, three, store)


def run_kernel(
    kernel, out_shape, scalars, arrays, scratch=(), scalar_outs=0, micros=4, from_hbm=0,
    to_hbm=0, in_place=False,
):
    outs = list(out_shape)
    arrays = [
        pltpu.with_memory_space_constraint(array, pltpu.HBM) if number < from_hbm else array
        for number, array in enumerate(arrays)
    ]
    in_hbm = pl.BlockSpec(memory_space=pltpu.HBM)
    in_specs = [in_hbm] * from_hbm + [vector_spec()] * (len(arrays) - from_hbm)
    out_specs = [vector_spec()] * (len(outs) - scalar_outs - to_hbm)
    out_specs += [scalar_spec()] * scalar_outs + [in_hbm] * to_hbm
    return pl.pallas_call(
        kernel,
        out_shape=outs,
        in_specs=[scalar_spec()] * len(scalars) + in_specs,
        out_specs=out_specs,
        scratch_shapes=list(scratch),
        input_output_aliases={len(scalars): 0} if in_place else {},
        compiler_params=pltpu.CompilerParams(vmem_limit_bytes=VMEM_LIMIT),
        cost_estimate=pl.CostEstimate(
            flops=int(micros * 1e9), bytes_accessed=int(micros * 1e6), transcendentals=0
        ),
    )(*scalars, *arrays)


def room_levels(count):
    shares = ((49, 34, 21), (51, 37, 24), (54, 41, 27))
    levels = [tuple(max(count * share // 60, 1) for share in level) for level in shares]
    return levels + [(count, count, count)]


def four_frames(queries, keys, values, back_reach, fwd_reach, valid_rows, valid_cols):
    _, token_rows, token_cols, _ = queries.shape
    tile_rows, tile_cols = token_rows // TS, token_cols // TS
    count = tile_rows * tile_cols
    shape = (token_rows, tile_cols, TS, DH)
    queries, keys, values = queries.reshape(shape), keys.reshape(shape), values.reshape(shape)
    me = lax.axis_index("frame").reshape(1).astype(jnp.int32)
    inward, across, outward = [(0, 1), (3, 2)], [(1, 2), (2, 1)], [(1, 0), (2, 3)]
    levels = room_levels(count)

    def tiles(number):
        return jax.ShapeDtypeStruct((number, AREA, DH), jnp.bfloat16)

    def ints(*sizes):
        return jax.ShapeDtypeStruct(sizes, jnp.int32)

    def send(array, pairs):
        return lax.ppermute(array, "frame", pairs)

    packed_k, reach, place, order, level = run_kernel(
        functools.partial(pack_kernel, tile_rows, tile_cols, levels),
        (tiles(count), ints(2, count), ints(2, count), ints(count), ints(1)),
        (
            me,
            pltpu.with_memory_space_constraint(back_reach, pltpu.HBM),
            pltpu.with_memory_space_constraint(fwd_reach, pltpu.HBM),
        ),
        (keys,),
        scratch=(pltpu.VMEM(shape, jnp.bfloat16), pltpu.SemaphoreType.DMA),
        scalar_outs=4,
        micros=2,
        from_hbm=1,
    )

    def with_room(one, two, three):
        def run(queries, keys, values, packed_k, reach, place, order):
            far_k = send(packed_k[:two], across)
            near_k = send(packed_k[:two], inward)
            own_s, packed_q = run_kernel(
                functools.partial(spatial_kernel, tile_rows, tile_cols),
                (tiles(count), tiles(count)),
                (me, place, valid_rows, valid_cols),
                (queries, keys, values),
                scratch=(
                    pltpu.VMEM((count * AREA, DH), jnp.bfloat16),
                    pltpu.VMEM((count * AREA, DH), jnp.bfloat16),
                    pltpu.VMEM((count * AREA, 2 * DH), jnp.bfloat16),
                    pltpu.VMEM((tile_rows, 8, tile_cols * AREA), jnp.float32),
                    pltpu.VMEM((tile_rows, 8, (tile_cols - 2) * AREA), jnp.float32),
                ),
                micros=10,
            )
            far_s = send(own_s[:two], across)
            near_s = send(own_s[:two], inward)
            hosted_qa = send(packed_q[three:one], inward) if one > three else None
            first_q, far_k = lax.optimization_barrier((packed_q[:three], far_k))
            hosted_qb = send(first_q, inward)
            far_k2 = send(near_k, across)
            far_s2 = send(near_s[:three], across)
            returned_a = near_k
            if one > three:
                (hosted_a,) = run_kernel(
                    functools.partial(near_hosted_kernel, tile_cols, one, two, three),
                    (tiles(one - three + 3),),
                    (me, reach, place, order, valid_rows, valid_cols),
                    (hosted_qa, packed_k, far_k, own_s, far_s),
                    micros=0.6,
                )
                returned_a = send(hosted_a, outward)
            near_rest, late = near_k, near_s
            if one > two:
                rest_k, rest_s, late_s, _ = lax.optimization_barrier(
                    (packed_k[two:one], own_s[two:one], near_s[three:two], near_s)
                )
                near_rest = send(jnp.concatenate([rest_k, rest_s]), inward)
                late = send(jnp.concatenate([late_s, rest_s, rest_k]), across)
            hosted_w, sums = run_kernel(
                functools.partial(far_hosted_kernel, tile_cols, three),
                (jax.ShapeDtypeStruct((three, AREA, 4 * AREA), jnp.bfloat16), tiles(3)),
                (me, reach, place, order, valid_rows, valid_cols),
                (hosted_qb, packed_k, far_k, far_k2),
                micros=0.6,
            )
            (hosted_b,) = run_kernel(
                functools.partial(far_mix_kernel, three),
                (tiles(three + 3),),
                (me, place, order),
                (hosted_w, own_s, far_s, far_s2, sums),
                micros=2,
            )
            returned_b = send(hosted_b, outward)
            hosted_b, near_k = lax.optimization_barrier((hosted_b, near_k))
            own_w, own_sums = run_kernel(
                functools.partial(own_weights_kernel, tile_rows, tile_cols, one, two),
                (
                    jax.ShapeDtypeStruct((count, AREA, 4 * AREA), jnp.bfloat16),
                    jax.ShapeDtypeStruct((AREA, DH), jnp.float32),
                ),
                (me, reach, place, valid_rows, valid_cols),
                (queries, keys, near_k, near_rest, far_k, far_k2),
                micros=1,
            )
            staging = (
                pltpu.VMEM((count, TS, TS, DH), jnp.bfloat16),
                pltpu.SemaphoreType.DMA((count,)),
            )
            first_o, out = run_kernel(
                functools.partial(own_mix_kernel, tile_cols, count, one, two, three),
                (tiles(three), pltpu.HBM(shape, jnp.bfloat16)),
                (me, reach, place, order, valid_rows, valid_cols),
                (own_w, own_sums, own_s, near_s, near_rest, far_s, far_s2, returned_a),
                scratch=staging,
                micros=3,
                to_hbm=1,
            )
            (out,) = run_kernel(
                functools.partial(last_kernel, tile_cols, one, two, three),
                (pltpu.HBM(shape, jnp.bfloat16),),
                (me, reach, place, order, valid_rows, valid_cols),
                (
                    out, own_w, queries, packed_k, near_k, own_s, near_s, near_rest, far_s, late,
                    own_sums, first_o, returned_b,
                ),
                scratch=staging,
                micros=3,
                from_hbm=1,
                to_hbm=1,
                in_place=True,
            )
            return out

        return run

    branches = [with_room(*level) for level in levels]
    operands = (queries, keys, values, packed_k, reach, place, order)
    out = lax.switch(level[0], branches, *operands)
    return out.reshape(1, token_rows, token_cols, DH)


def solution(mesh):
    in_specs = (
        P(("dp", "frame"), None, None, "row"),
        P(("dp", "frame"), None, None, "row"),
        P(("dp", "frame"), None, None, "row"),
        P("dp", None),
        P("dp", None),
        P("dp"),
        P("dp"),
    )
    out_specs = P(("dp", "frame"), None, None, "row")

    def block(*args):
        frames, _, token_cols, channels = args[0].shape
        line = mesh.shape["frame"] == 4 and frames == 1 and channels == DH
        if line and token_cols % (2 * TS) == 0 and 4 <= token_cols // TS:
            return four_frames(*args)
        return per_device(*args)

    return jax.shard_map(
        block, mesh=mesh, in_specs=in_specs, out_specs=out_specs, check_vma=False
    )
```

```python
import functools
import math

import jax
import jax.numpy as jnp
from jax import lax
from jax.experimental import pallas as pl
from jax.experimental.pallas import tpu as pltpu
from jax.sharding import PartitionSpec as P

DH = 128
TS = 8


def group_size(item_count, row_count):
    size = 1
    for option in range(1, item_count + 1):
        if item_count % option == 0 and option * row_count <= 1024:
            size = option
    return size


def attend_group(group_parts):
    query_rows, key_rows, value_rows, allowed = group_parts
    dot_terms = jnp.einsum("gmd,gnd->gmn", query_rows, key_rows, preferred_element_type=jnp.float32)
    query_sq = jnp.einsum("gmd,gmd->gm", query_rows, query_rows, preferred_element_type=jnp.float32)
    key_sq = jnp.einsum("gnd,gnd->gn", key_rows, key_rows, preferred_element_type=jnp.float32)
    distance = query_sq[:, :, None] + key_sq[:, None, :] - 2.0 * dot_terms
    scores = jnp.where(allowed, -distance * (0.5 / math.sqrt(query_rows.shape[2])), -jnp.inf)
    highest = jnp.max(scores, axis=2, keepdims=True)
    weights = jnp.exp(scores - highest)
    totals = jnp.sum(weights, axis=2, keepdims=True)
    mixed = jnp.einsum(
        "gmn,gnd->gmd", weights.astype(jnp.bfloat16), value_rows, preferred_element_type=jnp.float32
    )
    return mixed / totals


def attend_items(query_items, key_items, value_items, masks):
    item_count = query_items.shape[0]
    per_group = group_size(item_count, query_items.shape[1])
    groups = item_count // per_group

    def regroup(array):
        return array.reshape((groups, per_group) + array.shape[1:])

    mixed = lax.map(
        attend_group,
        (regroup(query_items), regroup(key_items), regroup(value_items), regroup(masks)),
    )
    return mixed.reshape((item_count,) + mixed.shape[2:])


def tile_split(block):
    frames, token_rows, token_cols, channels = block.shape
    heads = channels // DH
    return (
        block.reshape(frames, token_rows // TS, TS, token_cols // TS, TS, heads, DH)
        .transpose(5, 0, 1, 3, 2, 4, 6)
        .reshape(heads, frames, token_rows // TS * (token_cols // TS), TS * TS, DH)
    )


def neighbours(tiles, tile_rows, tile_cols):
    heads, frames, count_tiles, area, depth = tiles.shape
    grid = tiles.reshape(heads * frames, tile_rows, tile_cols, area, depth)
    padded = jnp.pad(grid, ((0, 0), (1, 1), (1, 1), (0, 0), (0, 0)))
    views = [
        padded[:, dy : dy + tile_rows, dx : dx + tile_cols] for dy in range(3) for dx in range(3)
    ]
    stacked = jnp.stack(views, axis=3)
    return stacked.reshape(heads * frames * count_tiles, 9 * area, depth)


def pad_tiles(tiles, total):
    return jnp.pad(tiles, ((0, 0), (0, 0), (0, total - tiles.shape[2]), (0, 0), (0, 0)))


def per_device(queries, keys, values, back_reach, fwd_reach, valid_rows, valid_cols):
    frames, token_rows, token_cols, channels = queries.shape
    heads = channels // DH
    tile_rows = token_rows // TS
    tile_cols = token_cols // TS
    count_tiles = tile_rows * tile_cols
    area = TS * TS
    frame_count = lax.axis_size("frame")
    frame_index = lax.axis_index("frame")
    padded_count = (count_tiles + frame_count - 1) // frame_count * frame_count
    tiles_here = padded_count // frame_count
    all_frames = frames * frame_count
    row_ids = jnp.arange(token_rows, dtype=jnp.int32)
    col_ids = jnp.arange(token_cols, dtype=jnp.int32)
    row_ok = row_ids[None, :] < valid_rows[:, None]
    col_ok = col_ids[None, :] < valid_cols[:, None]
    token_valid = row_ok[:, :, None] & col_ok[:, None, :]
    tile_valid_all = (
        token_valid.reshape(all_frames, tile_rows, TS, tile_cols, TS)
        .transpose(0, 1, 3, 2, 4)
        .reshape(all_frames, tile_rows, tile_cols, area)
    )
    tile_valid = lax.dynamic_slice_in_dim(tile_valid_all, frame_index * frames, frames, 0)
    padded_valid = jnp.pad(tile_valid, ((0, 0), (1, 1), (1, 1), (0, 0)))
    near_valid = jnp.stack(
        [
            padded_valid[:, dy : dy + tile_rows, dx : dx + tile_cols]
            for dy in range(3)
            for dx in range(3)
        ],
        axis=3,
    )
    near_valid = near_valid.reshape(frames, count_tiles, 1, 9 * area)
    query_factor = tile_valid.reshape(frames, count_tiles, area).astype(jnp.float32)
    query_t = tile_split(queries)
    key_t = tile_split(keys)
    masks = near_valid[None].reshape(heads * frames * count_tiles, 1, 9 * area)
    spatial = attend_items(
        query_t.reshape(heads * frames * count_tiles, area, DH),
        neighbours(key_t, tile_rows, tile_cols),
        neighbours(tile_split(values), tile_rows, tile_cols),
        masks,
    )
    spatial = spatial.reshape(heads, frames, count_tiles, area, DH)
    spatial_t = (spatial * query_factor[None, :, :, :, None]).astype(jnp.bfloat16)
    triple = jnp.stack(
        [
            pad_tiles(query_t, padded_count),
            pad_tiles(key_t, padded_count),
            pad_tiles(spatial_t, padded_count),
        ]
    )
    sent = lax.all_to_all(triple, "frame", split_axis=3, concat_axis=2, tiled=True)
    query_here, key_here, value_here = (sent[0], sent[1], sent[2])
    start = frame_index * tiles_here
    length = all_frames * area
    frame_of = jnp.arange(length, dtype=jnp.int32) // area
    frame_gap = frame_of[None, :] - frame_of[:, None]
    valid_flat = tile_valid_all.reshape(all_frames, count_tiles, area).transpose(1, 0, 2)
    valid_flat = jnp.pad(
        valid_flat, ((0, padded_count - count_tiles), (0, 0), (0, 0)), constant_values=True
    )
    valid_here = lax.dynamic_slice_in_dim(valid_flat, start, tiles_here, 0)
    back_here = lax.dynamic_slice_in_dim(
        jnp.pad(back_reach.reshape(count_tiles), (0, padded_count - count_tiles)),
        start,
        tiles_here,
        0,
    )
    fwd_here = lax.dynamic_slice_in_dim(
        jnp.pad(fwd_reach.reshape(count_tiles), (0, padded_count - count_tiles)),
        start,
        tiles_here,
        0,
    )
    key_ok = valid_here.reshape(tiles_here, length)
    allowed = (
        (frame_gap[None] >= -back_here[:, None, None])
        & (frame_gap[None] <= fwd_here[:, None, None])
        & key_ok[:, None, :]
    )
    time_masks = allowed[None].reshape(heads * tiles_here, length, length)

    def by_tile(array):
        return array.transpose(0, 2, 1, 3, 4).reshape(heads * tiles_here, length, DH)

    temporal = attend_items(
        by_tile(query_here), by_tile(key_here), by_tile(value_here), time_masks
    ).astype(jnp.bfloat16)
    temporal = temporal.reshape(heads, tiles_here, all_frames, area, DH).transpose(0, 2, 1, 3, 4)
    returned = lax.all_to_all(temporal, "frame", split_axis=1, concat_axis=2, tiled=True)[
        :, :, :count_tiles
    ]
    combined = (spatial_t.astype(jnp.float32) + returned.astype(jnp.float32)) * query_factor[
        None, :, :, :, None
    ]
    combined = combined.astype(jnp.bfloat16).reshape(
        heads, frames, tile_rows, tile_cols, TS, TS, DH
    )
    return combined.transpose(1, 2, 4, 3, 5, 0, 6).reshape(frames, token_rows, token_cols, channels)


SCALE = 1.0 / math.sqrt(DH)
MASKED = -1e30
AREA = TS * TS
GROUP = 10
PAIRS = 5
VMEM_LIMIT = 24 * 1024 * 1024
NT_DIMS = (((1,), (1,)), ((), ()))


def scalar_spec():
    return pl.BlockSpec(memory_space=pltpu.SMEM)


def vector_spec():
    return pl.BlockSpec(memory_space=pltpu.VMEM)


def read_tile(ref, row, col):
    return ref[pl.ds(row * TS, TS), col].reshape(AREA, DH)


def key_norms(keys):
    wide = keys.astype(jnp.float32)
    square = wide * wide
    high = square.astype(jnp.bfloat16)
    low = (square - high.astype(jnp.float32)).astype(jnp.bfloat16)
    ones = jnp.ones((8, 2 * DH), jnp.bfloat16)
    both = jnp.concatenate([high, low], axis=1)
    total = lax.dot_general(ones, both, NT_DIMS, preferred_element_type=jnp.float32)
    return total * (-0.5 * SCALE)


def row_valid(row, col, row_limit, col_limit):
    token = lax.broadcasted_iota(jnp.int32, (AREA, DH), 0)
    return (row * TS + (token >> 3) < row_limit) & (col * TS + (token & 7) < col_limit)


def pack_kernel(
    tile_rows, tile_cols, levels, me, back, fwd, keys, packed, reach, place, order, level, held,
    sem,
):
    load = pltpu.make_async_copy(keys, held, sem)
    load.start()
    left = me[0] < 2
    most = [None] * 4
    tiles = [(r, c) for r in range(tile_rows) for c in range(tile_cols)]
    for way in range(2):
        counts = [jnp.int32(0)] * 4
        for index, (r, c) in enumerate(tiles):
            toward, away = back[r, c], fwd[r, c]
            value = jnp.where(left, toward, away) if way == 0 else jnp.where(left, away, toward)
            reach[way, index] = value
            counts = [counts[v] + (value >= v).astype(jnp.int32) for v in range(4)]
        for v in (1, 2, 3):
            most[v] = counts[v] if way == 0 else jnp.maximum(most[v], counts[v])
        spots = [counts[1], counts[2], counts[3], jnp.int32(0)]
        for index in range(len(tiles)):
            value = jnp.minimum(reach[way, index], 3)
            spot = spots[0]
            for v in (1, 2, 3):
                spot = jnp.where(value == v, spots[v], spot)
            spots = [spots[v] + (value == v).astype(jnp.int32) for v in range(4)]
            place[way, index] = spot
            if way == 1:
                order[spot] = index
    chosen = jnp.int32(0)
    for one, two, three in levels[:-1]:
        over = (most[1] > one) | (most[2] > two) | (most[3] > three)
        chosen += over.astype(jnp.int32)
    level[0] = chosen
    load.wait()

    def pack_row(r, carry):
        for c in range(tile_cols):
            packed[place[0, r * tile_cols + c]] = read_tile(held, r, c)
        return carry

    lax.fori_loop(0, tile_rows, pack_row, 0)


def spatial_kernel(
    tile_rows, tile_cols, me, place, rows_ok, cols_ok, queries, keys, values, mixed, packed_q,
    query_t, key_t, value_t, bias_even, bias_odd,
):
    row_limit, col_limit = rows_ok[me[0]], cols_ok[me[0]]
    wide = tile_cols * AREA
    value_t[:, DH:] = jnp.ones((value_t.shape[0], DH), jnp.bfloat16)

    def lane_bias(r, first, count):
        start = pl.multiple_of((r * tile_cols + first) * AREA, AREA)
        norms = key_norms(key_t[pl.ds(start, count * AREA)])
        lane = lax.broadcasted_iota(jnp.int32, (8, count * AREA), 1) + first * AREA
        valid = (r * TS + ((lane >> 3) & 7) < row_limit) & (
            (lane >> 6) * TS + (lane & 7) < col_limit
        )
        return jnp.where(valid, norms, MASKED)

    def retile_row(r, carry):
        for c in range(tile_cols):
            index = r * tile_cols + c
            span = pl.ds(pl.multiple_of(index * AREA, AREA), AREA)
            tile_q = read_tile(queries, r, c)
            query_t[span] = tile_q
            packed_q[place[1, index]] = tile_q
            key_t[span] = read_tile(keys, r, c)
            value_t[span, :DH] = read_tile(values, r, c)
        bias_even[r] = lane_bias(r, 0, tile_cols)
        bias_odd[r] = lane_bias(r, 1, tile_cols - 2)
        return carry

    lax.fori_loop(0, tile_rows, retile_row, 0)
    lane_tile = lax.broadcasted_iota(jnp.int32, (8, 4 * AREA), 1) >> 6

    def attend_row(r, carry):
        first_row = jnp.clip(r - 1, 0, tile_rows - 3)
        for first_pair in range(0, tile_cols // 2, PAIRS):
            attend_pairs(r, first_row, range(first_pair, min(first_pair + PAIRS, tile_cols // 2)))
        return carry

    def attend_pairs(r, first_row, pairs):
        first_cols = [min(max(2 * pair - 1, 0), tile_cols - 4) for pair in pairs]
        dots, spans = [], []
        for pair, first_col in zip(pairs, first_cols):
            start = (r * tile_cols + 2 * pair) * AREA
            query = query_t[pl.ds(pl.multiple_of(start, AREA), 2 * AREA)]
            starts = [((first_row + step) * tile_cols + first_col) * AREA for step in range(3)]
            spans.append([pl.ds(pl.multiple_of(start, AREA), 4 * AREA) for start in starts])
            dots.append(
                [
                    lax.dot_general(
                        query, key_t[span], NT_DIMS, preferred_element_type=jnp.float32
                    )
                    for span in spans[-1]
                ]
            )
        scores = []
        for pair, first_col, parts in zip(pairs, first_cols, dots):
            scores.append([])
            for step, part in enumerate(parts):
                key_row = first_row + step
                table = bias_odd if first_col % 2 else bias_even
                lane_start = (first_col - first_col % 2) * AREA
                bias = table[key_row, :, lane_start : lane_start + 4 * AREA]
                near_row = jnp.abs(key_row - r) <= 1
                both = []
                for half in range(2):
                    gap = lane_tile + (first_col - 2 * pair - half)
                    near = (gap >= -1) & (gap <= 1) & near_row
                    here = part[half * AREA : (half + 1) * AREA].reshape(TS, 8, 4 * AREA)
                    here = here * SCALE + jnp.where(near, bias, MASKED)[None]
                    both.append(here.reshape(AREA, 4 * AREA))
                scores[-1].append(jnp.concatenate(both, axis=0))
        tops = [jnp.maximum(jnp.maximum(one[0], one[1]), one[2]) for one in scores]
        tops = [jnp.max(top, axis=1, keepdims=True) for top in tops]
        totals = []
        for one, top, where in zip(scores, tops, spans):
            weights = [jnp.exp(score - top).astype(jnp.bfloat16) for score in one]
            parts = [
                jnp.dot(weight, value_t[span], preferred_element_type=jnp.float32)
                for weight, span in zip(weights, where)
            ]
            totals.append((parts[0] + parts[1]) + parts[2])
        for pair, total in zip(pairs, totals):
            result = total[:, :DH] / total[:, DH:]
            for half in range(2):
                valid = row_valid(r, 2 * pair + half, row_limit, col_limit)
                tile = jnp.where(valid, result[half * AREA : (half + 1) * AREA], 0.0)
                spot = place[0, r * tile_cols + 2 * pair + half]
                mixed[spot] = tile.astype(jnp.bfloat16)

    lax.fori_loop(0, tile_rows, attend_row, 0)


def frames_of(mine):
    left = mine < 2
    return mine, jnp.where(left, 0, 3), jnp.where(left, 2, 1), jnp.where(left, 3, 0)


def by_block(picks, lanes):
    block = lax.broadcasted_iota(jnp.int32, (8, lanes), 1) >> 6
    chosen = jnp.full((8, lanes), picks[0], jnp.int32)
    for number in range(1, lanes // AREA):
        chosen = jnp.where(block == number, picks[number], chosen)
    return chosen


def room_left(frames, rows_ok, cols_ok, lanes):
    lane = lax.broadcasted_iota(jnp.int32, (8, lanes), 1)
    row_room = by_block([rows_ok[frame] for frame in frames], lanes) - ((lane >> 3) & 7)
    col_room = by_block([cols_ok[frame] for frame in frames], lanes) - (lane & 7)
    return row_room, col_room


def weigh(queries, keys_here, biases):
    parts, highest = [], []
    dots = [
        lax.dot_general(query, key, NT_DIMS, preferred_element_type=jnp.float32)
        for query, key in zip(queries, keys_here)
    ]
    norms = [key_norms(key) for key in keys_here]
    for dot, norm, bias in zip(dots, norms, biases):
        lanes = dot.shape[1]
        part = dot.reshape(TS, 8, lanes) * SCALE + (norm + bias)[None]
        parts.append(part.reshape(AREA, lanes))
    highest = [jnp.max(part, axis=1, keepdims=True) for part in parts]
    return [jnp.exp(part - top) for part, top in zip(parts, highest)], highest


def mask_bias(allowed, room, row, col, lanes):
    valid = (room[0] > row * TS) & (room[1] > col * TS) & (by_block(allowed, lanes) > 0)
    return jnp.where(valid, 0.0, MASKED)


def mix(weights, values_here):
    ones = jnp.ones(values_here.shape, jnp.bfloat16)
    total = jnp.dot(
        weights,
        jnp.concatenate([values_here, ones], axis=1),
        preferred_element_type=jnp.float32,
    )
    return total[:, :DH], total[:, DH:]


def in_chunks(first, last, body, carry):
    most = 11 if last - first <= 30 else 4
    size = max(option for option in range(1, most + 1) if (last - first) % option == 0)

    if size == last - first:
        return body(list(range(first, last)), carry)

    def chunk(number, carry):
        return body([first + number * size + step for step in range(size)], carry)

    return lax.fori_loop(0, (last - first) // size, chunk, carry)


def is_inner(mine):
    return (mine == 1) | (mine == 2)


def store_sums(ref, first, sums):
    for step in range(3):
        piece = sums.astype(jnp.bfloat16)
        ref[first + step] = piece
        sums = sums - piece.astype(jnp.float32)


def load_sums(ref, first):
    pieces = [ref[first + step].astype(jnp.float32) for step in range(3)]
    return (pieces[0] + pieces[1]) + pieces[2]


def reached(reach, index, least):
    return (reach[1, index] >= least).astype(jnp.int32)


def near_hosted_kernel(
    tile_cols, one, two, three, me, reach, place, order, rows_ok, cols_ok, hosted_q, packed_k,
    far_k, own_s, far_s, mixed,
):
    own, _, far, _ = frames_of(me[0])
    room = room_left((own, far), rows_ok, cols_ok, 2 * AREA)
    lane = lax.broadcasted_iota(jnp.int32, (AREA, DH), 1)

    def near_ones(spots, sums):
        indices = [order[spot] for spot in spots]
        rows = [lax.div(index, tile_cols) for index in indices]
        homes = [place[0, index] for index in indices]
        keys_here = [
            jnp.concatenate([packed_k[home], far_k[jnp.minimum(spot, two - 1)]], axis=0)
            for home, spot in zip(homes, spots)
        ]
        values_here = [
            jnp.concatenate([own_s[home], far_s[jnp.minimum(spot, two - 1)]], axis=0)
            for home, spot in zip(homes, spots)
        ]
        biases = [
            mask_bias(
                (reached(reach, index, 1), reached(reach, index, 2)),
                room, row, index - row * tile_cols, 2 * AREA,
            )
            for index, row in zip(indices, rows)
        ]
        parts, highest = weigh([hosted_q[spot - three] for spot in spots], keys_here, biases)
        totals = [mix(part.astype(jnp.bfloat16), v) for part, v in zip(parts, values_here)]
        for spot, (total, sum_here), top in zip(spots, totals, highest):
            mixed[spot - three] = (total / sum_here).astype(jnp.bfloat16)
            sums = jnp.where(lane == spot, top + jnp.log(sum_here), sums)
        return sums

    @pl.when(is_inner(me[0]))
    def _():
        sums = in_chunks(three, one, near_ones, jnp.zeros((AREA, DH), jnp.float32))
        store_sums(mixed, one - three, sums)


def far_hosted_kernel(
    tile_cols, three, me, reach, place, order, rows_ok, cols_ok, hosted_q, packed_k, far_k,
    far_k2, weights, sums_out,
):
    own, _, far, far2 = frames_of(me[0])
    room = room_left((own, far, far2, own), rows_ok, cols_ok, 4 * AREA)
    lane = lax.broadcasted_iota(jnp.int32, (AREA, DH), 1)
    no = jnp.int32(0)

    def far_ones(spots, sums):
        indices = [order[spot] for spot in spots]
        rows = [lax.div(index, tile_cols) for index in indices]
        homes = [packed_k[place[0, index]] for index in indices]
        keys_here = [
            jnp.concatenate([home, far_k[spot], far_k2[spot], home], axis=0)
            for home, spot in zip(homes, spots)
        ]
        biases = [
            mask_bias(
                tuple(reached(reach, index, least) for least in (1, 2, 3)) + (no,),
                room, row, index - row * tile_cols, 4 * AREA,
            )
            for index, row in zip(indices, rows)
        ]
        parts, highest = weigh([hosted_q[spot] for spot in spots], keys_here, biases)
        for spot, part, top in zip(spots, parts, highest):
            weights[spot] = part.astype(jnp.bfloat16)
            sum_here = jnp.sum(part, axis=1, keepdims=True)
            sums = jnp.where(lane == spot, top + jnp.log(sum_here), sums)
        return sums

    @pl.when(is_inner(me[0]))
    def _():
        sums = in_chunks(0, three, far_ones, jnp.zeros((AREA, DH), jnp.float32))
        store_sums(sums_out, 0, sums)


def far_mix_kernel(three, me, place, order, weights, own_s, far_s, far_s2, sums, mixed):
    def far_ones(spots, carry):
        homes = [own_s[place[0, order[spot]]] for spot in spots]
        totals = [
            mix(weights[spot], jnp.concatenate([home, far_s[spot], far_s2[spot], home], axis=0))
            for spot, home in zip(spots, homes)
        ]
        for spot, (total, sum_here) in zip(spots, totals):
            mixed[spot] = (total / sum_here).astype(jnp.bfloat16)
        return carry

    @pl.when(is_inner(me[0]))
    def _():
        in_chunks(0, three, far_ones, 0)
        mixed[three : three + 3] = sums[...]


def tile_groups(tile_rows, tile_cols, body, carry):
    rows = 1

    def step(number, carry):
        here = [(number * rows + r, c) for r in range(rows) for c in range(tile_cols)]
        for first in range(0, len(here), GROUP):
            carry = body(here[first : first + GROUP], carry)
        return carry

    return lax.fori_loop(0, tile_rows // rows, step, carry)


def two_part(first, rest, spot, split, last, start=0):
    tile = first[jnp.minimum(spot, split - 1)]
    if last > split:
        other = rest[start + jnp.clip(spot - split, 0, last - split - 1)]
        tile = jnp.where(spot < split, tile, other)
    return tile


def own_weights_kernel(
    tile_rows, tile_cols, one, two, me, reach, place, rows_ok, cols_ok, queries, keys, near_k,
    near_rest, far_k, far_k2, weights, sums_out,
):
    mine = me[0]
    inner = is_inner(mine)
    room = room_left(frames_of(mine), rows_ok, cols_ok, 4 * AREA)
    lane = lax.broadcasted_iota(jnp.int32, (AREA, DH), 1)

    def weigh_tiles(here, sums):
        query_list, key_list, biases = [], [], []
        for r, c in here:
            index = r * tile_cols + c
            near = two_part(near_k, near_rest, place[0, index], two, one)
            far = far_k[jnp.minimum(place[1, index], two - 1)]
            far2 = jnp.minimum(place[1, index], two - 1)
            near_reach, far_reach = reach[0, index], reach[1, index]
            allowed = (
                jnp.int32(1),
                (inner & (near_reach >= 1)).astype(jnp.int32),
                (inner & (far_reach >= 1)).astype(jnp.int32),
                (inner & (far_reach >= 2)).astype(jnp.int32),
            )
            biases.append(mask_bias(allowed, room, r, c, 4 * AREA))
            query_list.append(read_tile(queries, r, c))
            key_list.append(
                jnp.concatenate(
                    [read_tile(keys, r, c), near, far, far_k2[far2]], axis=0
                )
            )
        parts, highest = weigh(query_list, key_list, biases)
        totals = [jnp.sum(part, axis=1, keepdims=True) for part in parts]
        for (r, c), part, sum_here, top in zip(here, parts, totals, highest):
            index = r * tile_cols + c
            weights[index] = part.astype(jnp.bfloat16)
            sums = jnp.where(lane == index, top + jnp.log(sum_here), sums)
        return sums

    def weigh_alone(here, sums):
        alone = room_left((mine,), rows_ok, cols_ok, AREA)
        biases = [mask_bias((jnp.int32(1),), alone, r, c, AREA) for r, c in here]
        parts, highest = weigh(
            [read_tile(queries, r, c) for r, c in here],
            [read_tile(keys, r, c) for r, c in here],
            biases,
        )
        totals = [jnp.sum(part, axis=1, keepdims=True) for part in parts]
        for (r, c), part, sum_here, top in zip(here, parts, totals, highest):
            index = r * tile_cols + c
            weights[index, :, :AREA] = part.astype(jnp.bfloat16)
            weights[index, :, AREA:] = jnp.zeros((AREA, 3 * AREA), jnp.bfloat16)
            sums = jnp.where(lane == index, top + jnp.log(sum_here), sums)
        return sums

    def run(body):
        nothing = jnp.zeros((AREA, DH), jnp.float32)
        sums_out[...] = tile_groups(tile_rows, tile_cols, body, nothing)

    pl.when(inner)(lambda: run(weigh_tiles))
    pl.when(jnp.logical_not(inner))(lambda: run(weigh_alone))


def merged(own, own_sums, theirs, their_sums, index, spot):
    lane = lax.broadcasted_iota(jnp.int32, (AREA, DH), 1)
    gap = jnp.where(lane == spot, their_sums, 0.0) - jnp.where(lane == index, own_sums, 0.0)
    share = 1.0 / (1.0 + jnp.exp(jnp.sum(gap, axis=1, keepdims=True)))
    return share * own + (1.0 - share) * theirs.astype(jnp.float32)


def finished(spatial, temporal, valid):
    temporal = temporal.astype(jnp.bfloat16).astype(jnp.float32)
    tile = jnp.where(valid, spatial.astype(jnp.float32) + temporal, 0.0)
    return tile.astype(jnp.bfloat16).reshape(TS, TS, DH)


def tile_store(tile_cols, order, held, out, sems, spot):
    index = order[spot]
    r = lax.div(index, tile_cols)
    target = out.at[pl.ds(r * TS, TS), index - r * tile_cols]
    return pltpu.make_async_copy(held.at[spot], target, sems.at[spot])


def wait_stores(first, last, store):
    def wait(spot, carry):
        store(spot).wait()
        return carry

    lax.fori_loop(first, last, wait, 0)


def own_mix_kernel(
    tile_cols, count, one, two, three, me, reach, place, order, rows_ok, cols_ok, weights,
    own_sums, own_s, near_s, near_rest, far_s, far_s2, near_ones, first_o, out, held, sems,
):
    mine = me[0]
    inner = is_inner(mine)
    row_limit, col_limit = rows_ok[mine], cols_ok[mine]
    my_sums = own_sums[...]
    store = functools.partial(tile_store, tile_cols, order, held, out, sems)

    def mix_tiles(spots, their_sums):
        indices = [order[spot] for spot in spots]
        homes = [place[0, index] for index in indices]
        totals = []
        for spot, index, home in zip(spots, indices, homes):
            near = two_part(near_s, near_rest, home, two, one, one - two)
            far = far_s[jnp.minimum(spot, two - 1)]
            far2 = far_s2[jnp.minimum(spot, three - 1)]
            values_here = jnp.concatenate([own_s[home], near, far, far2], axis=0)
            totals.append(mix(weights[index], values_here))
        results = [total / sum_here for total, sum_here in totals]
        if their_sums is not None:
            for number, (spot, index) in enumerate(zip(spots, indices)):
                theirs = near_ones[spot - three]
                both = merged(results[number], my_sums, theirs, their_sums, index, spot)
                results[number] = jnp.where(reach[1, index] >= 1, both, results[number])
        for spot, index, home, result in zip(spots, indices, homes, results):
            r = lax.div(index, tile_cols)
            valid = row_valid(r, index - r * tile_cols, row_limit, col_limit)
            held[spot] = finished(own_s[home], result, valid)
            store(spot).start()
        return results

    def first_tiles(spots, carry):
        for spot, result in zip(spots, mix_tiles(spots, None)):
            first_o[spot] = result.astype(jnp.bfloat16)
        return carry

    def other_tiles(spots, carry):
        mix_tiles(spots, carry)
        return carry

    in_chunks(0, three, first_tiles, 0)
    if count > one:
        in_chunks(one, count, other_tiles, None)
    if one > three:

        @pl.when(jnp.logical_not(inner))
        def _():
            in_chunks(three, one, other_tiles, load_sums(near_ones, one - three))
            wait_stores(three, one, store)

    wait_stores(0, three, store)
    wait_stores(one, count, store)


def last_kernel(
    tile_cols, one, two, three, me, reach, place, order, rows_ok, cols_ok, done, weights, queries,
    packed_k, near_k, own_s, near_s, near_rest, far_s, late, own_sums, first_o, far_ones, out,
    held, sems,
):
    mine = me[0]
    inner = is_inner(mine)
    row_limit, col_limit = rows_ok[mine], cols_ok[mine]
    store = functools.partial(tile_store, tile_cols, order, held, out, sems)

    def finish(spots, results):
        for spot, result in zip(spots, results):
            index = order[spot]
            r = lax.div(index, tile_cols)
            valid = row_valid(r, index - r * tile_cols, row_limit, col_limit)
            held[spot] = finished(own_s[place[0, index]], result, valid)
            store(spot).start()

    def near_part(first, rest_start, home):
        return two_part(first, near_rest, home, two, one, rest_start)

    def late_mix(spot):
        index = order[spot]
        home = place[0, index]
        near = near_part(near_s, one - two, home)
        values_here = jnp.concatenate(
            [own_s[home], near, far_s[spot], late[spot - three]], axis=0
        )
        return mix(weights[index], values_here)

    def weigh_last(spots):
        room = room_left(frames_of(mine), rows_ok, cols_ok, 4 * AREA)
        query_list, key_list, value_list, biases = [], [], [], []
        for spot in spots:
            index = order[spot]
            r = lax.div(index, tile_cols)
            c = index - r * tile_cols
            home = place[0, index]
            allowed = (
                jnp.int32(1),
                (reach[0, index] >= 1).astype(jnp.int32),
                (reach[1, index] >= 1).astype(jnp.int32),
                jnp.int32(0),
            )
            biases.append(mask_bias(allowed, room, r, c, 4 * AREA))
            query_list.append(read_tile(queries, r, c))
            own, far = packed_k[home], late[spot - three + one - two]
            near = near_part(near_k, 0, home)
            key_list.append(jnp.concatenate([own, near, far, own], axis=0))
            own, far = own_s[home], late[spot - three]
            near = near_part(near_s, one - two, home)
            value_list.append(jnp.concatenate([own, near, far, own], axis=0))
        parts, _ = weigh(query_list, key_list, biases)
        return [part.astype(jnp.bfloat16) for part in parts], value_list

    if one > three:

        @pl.when(inner)
        def _():
            parts, value_list = weigh_last(range(two, one)) if one > two else ([], [])
            totals = [late_mix(spot) for spot in range(three, two)]
            totals += [mix(part, v) for part, v in zip(parts, value_list)]
            finish(range(three, one), [total / sum_here for total, sum_here in totals])
            wait_stores(three, one, store)

    @pl.when(jnp.logical_not(inner))
    def _():
        my_sums = own_sums[...]
        their_sums = load_sums(far_ones, three)

        def far_tiles(spots, carry):
            results = []
            for spot in spots:
                index = order[spot]
                own = first_o[spot].astype(jnp.float32)
                both = merged(own, my_sums, far_ones[spot], their_sums, index, spot)
                results.append(jnp.where(reach[1, index] >= 1, both, own))
            finish(spots, results)
            return carry

        in_chunks(0, three, far_tiles, 0)
        wait_stores(0, three, store)


def run_kernel(
    kernel, out_shape, scalars, arrays, scratch=(), scalar_outs=0, micros=4, from_hbm=0,
    to_hbm=0, in_place=False,
):
    outs = list(out_shape)
    arrays = [
        pltpu.with_memory_space_constraint(array, pltpu.HBM) if number < from_hbm else array
        for number, array in enumerate(arrays)
    ]
    in_hbm = pl.BlockSpec(memory_space=pltpu.HBM)
    in_specs = [in_hbm] * from_hbm + [vector_spec()] * (len(arrays) - from_hbm)
    out_specs = [vector_spec()] * (len(outs) - scalar_outs - to_hbm)
    out_specs += [scalar_spec()] * scalar_outs + [in_hbm] * to_hbm
    return pl.pallas_call(
        kernel,
        out_shape=outs,
        in_specs=[scalar_spec()] * len(scalars) + in_specs,
        out_specs=out_specs,
        scratch_shapes=list(scratch),
        input_output_aliases={len(scalars): 0} if in_place else {},
        compiler_params=pltpu.CompilerParams(vmem_limit_bytes=VMEM_LIMIT),
        cost_estimate=pl.CostEstimate(
            flops=int(micros * 1e9), bytes_accessed=int(micros * 1e6), transcendentals=0
        ),
    )(*scalars, *arrays)


def room_levels(count):
    shares = ((49, 34, 21), (51, 37, 24), (54, 41, 27))
    levels = [tuple(max(count * share // 60, 1) for share in level) for level in shares]
    return levels + [(count, count, count)]


def four_frames(queries, keys, values, back_reach, fwd_reach, valid_rows, valid_cols):
    _, token_rows, token_cols, _ = queries.shape
    tile_rows, tile_cols = token_rows // TS, token_cols // TS
    count = tile_rows * tile_cols
    shape = (token_rows, tile_cols, TS, DH)
    queries, keys, values = queries.reshape(shape), keys.reshape(shape), values.reshape(shape)
    me = lax.axis_index("frame").reshape(1).astype(jnp.int32)
    inward, across, outward = [(0, 1), (3, 2)], [(1, 2), (2, 1)], [(1, 0), (2, 3)]
    levels = room_levels(count)

    def tiles(number):
        return jax.ShapeDtypeStruct((number, AREA, DH), jnp.bfloat16)

    def ints(*sizes):
        return jax.ShapeDtypeStruct(sizes, jnp.int32)

    def send(array, pairs):
        return lax.ppermute(array, "frame", pairs)

    packed_k, reach, place, order, level = run_kernel(
        functools.partial(pack_kernel, tile_rows, tile_cols, levels),
        (tiles(count), ints(2, count), ints(2, count), ints(count), ints(1)),
        (
            me,
            pltpu.with_memory_space_constraint(back_reach, pltpu.HBM),
            pltpu.with_memory_space_constraint(fwd_reach, pltpu.HBM),
        ),
        (keys,),
        scratch=(pltpu.VMEM(shape, jnp.bfloat16), pltpu.SemaphoreType.DMA),
        scalar_outs=4,
        micros=2,
        from_hbm=1,
    )

    def with_room(one, two, three):
        def run(queries, keys, values, packed_k, reach, place, order):
            far_k = send(packed_k[:two], across)
            near_k = send(packed_k[:two], inward)
            own_s, packed_q = run_kernel(
                functools.partial(spatial_kernel, tile_rows, tile_cols),
                (tiles(count), tiles(count)),
                (me, place, valid_rows, valid_cols),
                (queries, keys, values),
                scratch=(
                    pltpu.VMEM((count * AREA, DH), jnp.bfloat16),
                    pltpu.VMEM((count * AREA, DH), jnp.bfloat16),
                    pltpu.VMEM((count * AREA, 2 * DH), jnp.bfloat16),
                    pltpu.VMEM((tile_rows, 8, tile_cols * AREA), jnp.float32),
                    pltpu.VMEM((tile_rows, 8, (tile_cols - 2) * AREA), jnp.float32),
                ),
                micros=10,
            )
            far_s = send(own_s[:two], across)
            near_s = send(own_s[:two], inward)
            hosted_qa = send(packed_q[three:one], inward) if one > three else None
            first_q, far_k = lax.optimization_barrier((packed_q[:three], far_k))
            hosted_qb = send(first_q, inward)
            far_k2 = send(near_k, across)
            far_s2 = send(near_s[:three], across)
            returned_a = near_k
            if one > three:
                (hosted_a,) = run_kernel(
                    functools.partial(near_hosted_kernel, tile_cols, one, two, three),
                    (tiles(one - three + 3),),
                    (me, reach, place, order, valid_rows, valid_cols),
                    (hosted_qa, packed_k, far_k, own_s, far_s),
                    micros=0.6,
                )
                returned_a = send(hosted_a, outward)
            near_rest, late = near_k, near_s
            if one > two:
                rest_k, rest_s, late_s, _ = lax.optimization_barrier(
                    (packed_k[two:one], own_s[two:one], near_s[three:two], near_s)
                )
                near_rest = send(jnp.concatenate([rest_k, rest_s]), inward)
                late = send(jnp.concatenate([late_s, rest_s, rest_k]), across)
            hosted_w, sums = run_kernel(
                functools.partial(far_hosted_kernel, tile_cols, three),
                (jax.ShapeDtypeStruct((three, AREA, 4 * AREA), jnp.bfloat16), tiles(3)),
                (me, reach, place, order, valid_rows, valid_cols),
                (hosted_qb, packed_k, far_k, far_k2),
                micros=0.6,
            )
            (hosted_b,) = run_kernel(
                functools.partial(far_mix_kernel, three),
                (tiles(three + 3),),
                (me, place, order),
                (hosted_w, own_s, far_s, far_s2, sums),
                micros=2,
            )
            returned_b = send(hosted_b, outward)
            hosted_b, near_k = lax.optimization_barrier((hosted_b, near_k))
            own_w, own_sums = run_kernel(
                functools.partial(own_weights_kernel, tile_rows, tile_cols, one, two),
                (
                    jax.ShapeDtypeStruct((count, AREA, 4 * AREA), jnp.bfloat16),
                    jax.ShapeDtypeStruct((AREA, DH), jnp.float32),
                ),
                (me, reach, place, valid_rows, valid_cols),
                (queries, keys, near_k, near_rest, far_k, far_k2),
                micros=1,
            )
            staging = (
                pltpu.VMEM((count, TS, TS, DH), jnp.bfloat16),
                pltpu.SemaphoreType.DMA((count,)),
            )
            first_o, out = run_kernel(
                functools.partial(own_mix_kernel, tile_cols, count, one, two, three),
                (tiles(three), pltpu.HBM(shape, jnp.bfloat16)),
                (me, reach, place, order, valid_rows, valid_cols),
                (own_w, own_sums, own_s, near_s, near_rest, far_s, far_s2, returned_a),
                scratch=staging,
                micros=3,
                to_hbm=1,
            )
            (out,) = run_kernel(
                functools.partial(last_kernel, tile_cols, one, two, three),
                (pltpu.HBM(shape, jnp.bfloat16),),
                (me, reach, place, order, valid_rows, valid_cols),
                (
                    out, own_w, queries, packed_k, near_k, own_s, near_s, near_rest, far_s, late,
                    own_sums, first_o, returned_b,
                ),
                scratch=staging,
                micros=3,
                from_hbm=1,
                to_hbm=1,
                in_place=True,
            )
            return out

        return run

    branches = [with_room(*level) for level in levels]
    operands = (queries, keys, values, packed_k, reach, place, order)
    out = lax.switch(level[0], branches, *operands)
    return out.reshape(1, token_rows, token_cols, DH)


def solution(mesh):
    in_specs = (
        P(("dp", "frame"), None, None, "row"),
        P(("dp", "frame"), None, None, "row"),
        P(("dp", "frame"), None, None, "row"),
        P("dp", None),
        P("dp", None),
        P("dp"),
        P("dp"),
    )
    out_specs = P(("dp", "frame"), None, None, "row")

    def block(*args):
        frames, _, token_cols, channels = args[0].shape
        line = mesh.shape["frame"] == 4 and frames == 1 and channels == DH
        if line and token_cols % (2 * TS) == 0 and 4 <= token_cols // TS:
            return four_frames(*args)
        return per_device(*args)

    return jax.shard_map(
        block, mesh=mesh, in_specs=in_specs, out_specs=out_specs, check_vma=False
    )
```

```python
import functools
import math

import jax
import jax.numpy as jnp
from jax import lax
from jax.experimental import pallas as pl
from jax.experimental.pallas import tpu as pltpu
from jax.sharding import PartitionSpec as P

DH = 128
TS = 8


def group_size(item_count, row_count):
    size = 1
    for option in range(1, item_count + 1):
        if item_count % option == 0 and option * row_count <= 1024:
            size = option
    return size


def attend_group(group_parts):
    query_rows, key_rows, value_rows, allowed = group_parts
    dot_terms = jnp.einsum("gmd,gnd->gmn", query_rows, key_rows, preferred_element_type=jnp.float32)
    query_sq = jnp.einsum("gmd,gmd->gm", query_rows, query_rows, preferred_element_type=jnp.float32)
    key_sq = jnp.einsum("gnd,gnd->gn", key_rows, key_rows, preferred_element_type=jnp.float32)
    distance = query_sq[:, :, None] + key_sq[:, None, :] - 2.0 * dot_terms
    scores = jnp.where(allowed, -distance * (0.5 / math.sqrt(query_rows.shape[2])), -jnp.inf)
    highest = jnp.max(scores, axis=2, keepdims=True)
    weights = jnp.exp(scores - highest)
    totals = jnp.sum(weights, axis=2, keepdims=True)
    mixed = jnp.einsum(
        "gmn,gnd->gmd", weights.astype(jnp.bfloat16), value_rows, preferred_element_type=jnp.float32
    )
    return mixed / totals


def attend_items(query_items, key_items, value_items, masks):
    item_count = query_items.shape[0]
    per_group = group_size(item_count, query_items.shape[1])
    groups = item_count // per_group

    def regroup(array):
        return array.reshape((groups, per_group) + array.shape[1:])

    mixed = lax.map(
        attend_group,
        (regroup(query_items), regroup(key_items), regroup(value_items), regroup(masks)),
    )
    return mixed.reshape((item_count,) + mixed.shape[2:])


def tile_split(block):
    frames, token_rows, token_cols, channels = block.shape
    heads = channels // DH
    return (
        block.reshape(frames, token_rows // TS, TS, token_cols // TS, TS, heads, DH)
        .transpose(5, 0, 1, 3, 2, 4, 6)
        .reshape(heads, frames, token_rows // TS * (token_cols // TS), TS * TS, DH)
    )


def neighbours(tiles, tile_rows, tile_cols):
    heads, frames, count_tiles, area, depth = tiles.shape
    grid = tiles.reshape(heads * frames, tile_rows, tile_cols, area, depth)
    padded = jnp.pad(grid, ((0, 0), (1, 1), (1, 1), (0, 0), (0, 0)))
    views = [
        padded[:, dy : dy + tile_rows, dx : dx + tile_cols] for dy in range(3) for dx in range(3)
    ]
    stacked = jnp.stack(views, axis=3)
    return stacked.reshape(heads * frames * count_tiles, 9 * area, depth)


def pad_tiles(tiles, total):
    return jnp.pad(tiles, ((0, 0), (0, 0), (0, total - tiles.shape[2]), (0, 0), (0, 0)))


def per_device(queries, keys, values, back_reach, fwd_reach, valid_rows, valid_cols):
    frames, token_rows, token_cols, channels = queries.shape
    heads = channels // DH
    tile_rows = token_rows // TS
    tile_cols = token_cols // TS
    count_tiles = tile_rows * tile_cols
    area = TS * TS
    frame_count = lax.axis_size("frame")
    frame_index = lax.axis_index("frame")
    padded_count = (count_tiles + frame_count - 1) // frame_count * frame_count
    tiles_here = padded_count // frame_count
    all_frames = frames * frame_count
    row_ids = jnp.arange(token_rows, dtype=jnp.int32)
    col_ids = jnp.arange(token_cols, dtype=jnp.int32)
    row_ok = row_ids[None, :] < valid_rows[:, None]
    col_ok = col_ids[None, :] < valid_cols[:, None]
    token_valid = row_ok[:, :, None] & col_ok[:, None, :]
    tile_valid_all = (
        token_valid.reshape(all_frames, tile_rows, TS, tile_cols, TS)
        .transpose(0, 1, 3, 2, 4)
        .reshape(all_frames, tile_rows, tile_cols, area)
    )
    tile_valid = lax.dynamic_slice_in_dim(tile_valid_all, frame_index * frames, frames, 0)
    padded_valid = jnp.pad(tile_valid, ((0, 0), (1, 1), (1, 1), (0, 0)))
    near_valid = jnp.stack(
        [
            padded_valid[:, dy : dy + tile_rows, dx : dx + tile_cols]
            for dy in range(3)
            for dx in range(3)
        ],
        axis=3,
    )
    near_valid = near_valid.reshape(frames, count_tiles, 1, 9 * area)
    query_factor = tile_valid.reshape(frames, count_tiles, area).astype(jnp.float32)
    query_t = tile_split(queries)
    key_t = tile_split(keys)
    masks = near_valid[None].reshape(heads * frames * count_tiles, 1, 9 * area)
    spatial = attend_items(
        query_t.reshape(heads * frames * count_tiles, area, DH),
        neighbours(key_t, tile_rows, tile_cols),
        neighbours(tile_split(values), tile_rows, tile_cols),
        masks,
    )
    spatial = spatial.reshape(heads, frames, count_tiles, area, DH)
    spatial_t = (spatial * query_factor[None, :, :, :, None]).astype(jnp.bfloat16)
    triple = jnp.stack(
        [
            pad_tiles(query_t, padded_count),
            pad_tiles(key_t, padded_count),
            pad_tiles(spatial_t, padded_count),
        ]
    )
    sent = lax.all_to_all(triple, "frame", split_axis=3, concat_axis=2, tiled=True)
    query_here, key_here, value_here = (sent[0], sent[1], sent[2])
    start = frame_index * tiles_here
    length = all_frames * area
    frame_of = jnp.arange(length, dtype=jnp.int32) // area
    frame_gap = frame_of[None, :] - frame_of[:, None]
    valid_flat = tile_valid_all.reshape(all_frames, count_tiles, area).transpose(1, 0, 2)
    valid_flat = jnp.pad(
        valid_flat, ((0, padded_count - count_tiles), (0, 0), (0, 0)), constant_values=True
    )
    valid_here = lax.dynamic_slice_in_dim(valid_flat, start, tiles_here, 0)
    back_here = lax.dynamic_slice_in_dim(
        jnp.pad(back_reach.reshape(count_tiles), (0, padded_count - count_tiles)),
        start,
        tiles_here,
        0,
    )
    fwd_here = lax.dynamic_slice_in_dim(
        jnp.pad(fwd_reach.reshape(count_tiles), (0, padded_count - count_tiles)),
        start,
        tiles_here,
        0,
    )
    key_ok = valid_here.reshape(tiles_here, length)
    allowed = (
        (frame_gap[None] >= -back_here[:, None, None])
        & (frame_gap[None] <= fwd_here[:, None, None])
        & key_ok[:, None, :]
    )
    time_masks = allowed[None].reshape(heads * tiles_here, length, length)

    def by_tile(array):
        return array.transpose(0, 2, 1, 3, 4).reshape(heads * tiles_here, length, DH)

    temporal = attend_items(
        by_tile(query_here), by_tile(key_here), by_tile(value_here), time_masks
    ).astype(jnp.bfloat16)
    temporal = temporal.reshape(heads, tiles_here, all_frames, area, DH).transpose(0, 2, 1, 3, 4)
    returned = lax.all_to_all(temporal, "frame", split_axis=1, concat_axis=2, tiled=True)[
        :, :, :count_tiles
    ]
    combined = (spatial_t.astype(jnp.float32) + returned.astype(jnp.float32)) * query_factor[
        None, :, :, :, None
    ]
    combined = combined.astype(jnp.bfloat16).reshape(
        heads, frames, tile_rows, tile_cols, TS, TS, DH
    )
    return combined.transpose(1, 2, 4, 3, 5, 0, 6).reshape(frames, token_rows, token_cols, channels)


SCALE = 1.0 / math.sqrt(DH)
MASKED = -1e30
AREA = TS * TS
GROUP = 10
PAIRS = 5
VMEM_LIMIT = 24 * 1024 * 1024
NT_DIMS = (((1,), (1,)), ((), ()))


def scalar_spec():
    return pl.BlockSpec(memory_space=pltpu.SMEM)


def vector_spec():
    return pl.BlockSpec(memory_space=pltpu.VMEM)


def read_tile(ref, row, col):
    return ref[pl.ds(row * TS, TS), col].reshape(AREA, DH)


def key_norms(keys):
    wide = keys.astype(jnp.float32)
    square = wide * wide
    high = square.astype(jnp.bfloat16)
    low = (square - high.astype(jnp.float32)).astype(jnp.bfloat16)
    ones = jnp.ones((8, 2 * DH), jnp.bfloat16)
    both = jnp.concatenate([high, low], axis=1)
    total = lax.dot_general(ones, both, NT_DIMS, preferred_element_type=jnp.float32)
    return total * (-0.5 * SCALE)


def row_valid(row, col, row_limit, col_limit):
    token = lax.broadcasted_iota(jnp.int32, (AREA, DH), 0)
    return (row * TS + (token >> 3) < row_limit) & (col * TS + (token & 7) < col_limit)


def pack_kernel(
    tile_rows, tile_cols, levels, me, back, fwd, keys, packed, reach, place, order, level, held,
    sem,
):
    load = pltpu.make_async_copy(keys, held, sem)
    load.start()
    left = me[0] < 2
    most = [None] * 4
    tiles = [(r, c) for r in range(tile_rows) for c in range(tile_cols)]
    for way in range(2):
        counts = [jnp.int32(0)] * 4
        for index, (r, c) in enumerate(tiles):
            toward, away = back[r, c], fwd[r, c]
            value = jnp.where(left, toward, away) if way == 0 else jnp.where(left, away, toward)
            reach[way, index] = value
            counts = [counts[v] + (value >= v).astype(jnp.int32) for v in range(4)]
        for v in (1, 2, 3):
            most[v] = counts[v] if way == 0 else jnp.maximum(most[v], counts[v])
        spots = [counts[1], counts[2], counts[3], jnp.int32(0)]
        for index in range(len(tiles)):
            value = jnp.minimum(reach[way, index], 3)
            spot = spots[0]
            for v in (1, 2, 3):
                spot = jnp.where(value == v, spots[v], spot)
            spots = [spots[v] + (value == v).astype(jnp.int32) for v in range(4)]
            place[way, index] = spot
            if way == 1:
                order[spot] = index
    chosen = jnp.int32(0)
    for one, two, three in levels[:-1]:
        over = (most[1] > one) | (most[2] > two) | (most[3] > three)
        chosen += over.astype(jnp.int32)
    level[0] = chosen
    load.wait()

    def pack_row(r, carry):
        for c in range(tile_cols):
            packed[place[0, r * tile_cols + c]] = read_tile(held, r, c)
        return carry

    lax.fori_loop(0, tile_rows, pack_row, 0)


def spatial_kernel(
    tile_rows, tile_cols, me, place, rows_ok, cols_ok, queries, packed_k, values, mixed, packed_q,
    query_t, key_t, value_t, bias_even, bias_odd,
):
    row_limit, col_limit = rows_ok[me[0]], cols_ok[me[0]]
    wide = tile_cols * AREA
    value_t[:, DH:] = jnp.ones((value_t.shape[0], DH), jnp.bfloat16)

    def lane_bias(r, first, count):
        start = pl.multiple_of((r * tile_cols + first) * AREA, AREA)
        norms = key_norms(key_t[pl.ds(start, count * AREA)])
        lane = lax.broadcasted_iota(jnp.int32, (8, count * AREA), 1) + first * AREA
        valid = (r * TS + ((lane >> 3) & 7) < row_limit) & (
            (lane >> 6) * TS + (lane & 7) < col_limit
        )
        return jnp.where(valid, norms, MASKED)

    def retile_row(r, carry):
        for c in range(tile_cols):
            index = r * tile_cols + c
            span = pl.ds(pl.multiple_of(index * AREA, AREA), AREA)
            tile_q = read_tile(queries, r, c)
            query_t[span] = tile_q
            packed_q[place[1, index]] = tile_q
            key_t[span] = packed_k[place[0, index]]
            value_t[span, :DH] = read_tile(values, r, c)
        bias_even[r] = lane_bias(r, 0, tile_cols)
        bias_odd[r] = lane_bias(r, 1, tile_cols - 2)
        return carry

    lax.fori_loop(0, tile_rows, retile_row, 0)
    lane_tile = lax.broadcasted_iota(jnp.int32, (8, 4 * AREA), 1) >> 6

    def attend_row(r, carry):
        first_row = jnp.clip(r - 1, 0, tile_rows - 3)
        for first_pair in range(0, tile_cols // 2, PAIRS):
            attend_pairs(r, first_row, range(first_pair, min(first_pair + PAIRS, tile_cols // 2)))
        return carry

    def attend_pairs(r, first_row, pairs):
        first_cols = [min(max(2 * pair - 1, 0), tile_cols - 4) for pair in pairs]
        dots, spans = [], []
        for pair, first_col in zip(pairs, first_cols):
            start = (r * tile_cols + 2 * pair) * AREA
            query = query_t[pl.ds(pl.multiple_of(start, AREA), 2 * AREA)]
            starts = [((first_row + step) * tile_cols + first_col) * AREA for step in range(3)]
            spans.append([pl.ds(pl.multiple_of(start, AREA), 4 * AREA) for start in starts])
            dots.append(
                [
                    lax.dot_general(
                        query, key_t[span], NT_DIMS, preferred_element_type=jnp.float32
                    )
                    for span in spans[-1]
                ]
            )
        scores = []
        for pair, first_col, parts in zip(pairs, first_cols, dots):
            scores.append([])
            for step, part in enumerate(parts):
                key_row = first_row + step
                table = bias_odd if first_col % 2 else bias_even
                lane_start = (first_col - first_col % 2) * AREA
                bias = table[key_row, :, lane_start : lane_start + 4 * AREA]
                near_row = jnp.abs(key_row - r) <= 1
                both = []
                for half in range(2):
                    gap = lane_tile + (first_col - 2 * pair - half)
                    near = (gap >= -1) & (gap <= 1) & near_row
                    here = part[half * AREA : (half + 1) * AREA].reshape(TS, 8, 4 * AREA)
                    here = here * SCALE + jnp.where(near, bias, MASKED)[None]
                    both.append(here.reshape(AREA, 4 * AREA))
                scores[-1].append(jnp.concatenate(both, axis=0))
        tops = [jnp.maximum(jnp.maximum(one[0], one[1]), one[2]) for one in scores]
        tops = [jnp.max(top, axis=1, keepdims=True) for top in tops]
        totals = []
        for one, top, where in zip(scores, tops, spans):
            weights = [jnp.exp(score - top).astype(jnp.bfloat16) for score in one]
            parts = [
                jnp.dot(weight, value_t[span], preferred_element_type=jnp.float32)
                for weight, span in zip(weights, where)
            ]
            totals.append((parts[0] + parts[1]) + parts[2])
        for pair, total in zip(pairs, totals):
            result = total[:, :DH] / total[:, DH:]
            for half in range(2):
                valid = row_valid(r, 2 * pair + half, row_limit, col_limit)
                tile = jnp.where(valid, result[half * AREA : (half + 1) * AREA], 0.0)
                spot = place[0, r * tile_cols + 2 * pair + half]
                mixed[spot] = tile.astype(jnp.bfloat16)

    lax.fori_loop(0, tile_rows, attend_row, 0)


def frames_of(mine):
    left = mine < 2
    return mine, jnp.where(left, 0, 3), jnp.where(left, 2, 1), jnp.where(left, 3, 0)


def by_block(picks, lanes):
    block = lax.broadcasted_iota(jnp.int32, (8, lanes), 1) >> 6
    chosen = jnp.full((8, lanes), picks[0], jnp.int32)
    for number in range(1, lanes // AREA):
        chosen = jnp.where(block == number, picks[number], chosen)
    return chosen


def room_left(frames, rows_ok, cols_ok, lanes):
    lane = lax.broadcasted_iota(jnp.int32, (8, lanes), 1)
    row_room = by_block([rows_ok[frame] for frame in frames], lanes) - ((lane >> 3) & 7)
    col_room = by_block([cols_ok[frame] for frame in frames], lanes) - (lane & 7)
    return row_room, col_room


def weigh(queries, keys_here, biases):
    parts, highest = [], []
    dots = [
        lax.dot_general(query, key, NT_DIMS, preferred_element_type=jnp.float32)
        for query, key in zip(queries, keys_here)
    ]
    norms = [key_norms(key) for key in keys_here]
    for dot, norm, bias in zip(dots, norms, biases):
        lanes = dot.shape[1]
        part = dot.reshape(TS, 8, lanes) * SCALE + (norm + bias)[None]
        parts.append(part.reshape(AREA, lanes))
    highest = [jnp.max(part, axis=1, keepdims=True) for part in parts]
    return [jnp.exp(part - top) for part, top in zip(parts, highest)], highest


def mask_bias(allowed, room, row, col, lanes):
    valid = (room[0] > row * TS) & (room[1] > col * TS) & (by_block(allowed, lanes) > 0)
    return jnp.where(valid, 0.0, MASKED)


def mix(weights, values_here):
    ones = jnp.ones(values_here.shape, jnp.bfloat16)
    total = jnp.dot(
        weights,
        jnp.concatenate([values_here, ones], axis=1),
        preferred_element_type=jnp.float32,
    )
    return total[:, :DH], total[:, DH:]


def in_chunks(first, last, body, carry, most=None):
    most = most or (11 if last - first <= 30 else 4)
    size = max(option for option in range(1, most + 1) if (last - first) % option == 0)
    if size == last - first:
        return body(list(range(first, last)), carry)

    def chunk(number, carry):
        return body([first + number * size + step for step in range(size)], carry)

    return lax.fori_loop(0, (last - first) // size, chunk, carry)


def is_inner(mine):
    return (mine == 1) | (mine == 2)


def store_sums(ref, first, sums):
    for step in range(3):
        piece = sums.astype(jnp.bfloat16)
        ref[first + step] = piece
        sums = sums - piece.astype(jnp.float32)


def load_sums(ref, first):
    pieces = [ref[first + step].astype(jnp.float32) for step in range(3)]
    return (pieces[0] + pieces[1]) + pieces[2]


def reached(reach, index, least):
    return (reach[1, index] >= least).astype(jnp.int32)


def near_hosted_kernel(
    tile_cols, one, two, three, me, reach, place, order, rows_ok, cols_ok, hosted_q, packed_k,
    far_k, own_s, far_s, mixed,
):
    own, _, far, _ = frames_of(me[0])
    room = room_left((own, far), rows_ok, cols_ok, 2 * AREA)
    lane = lax.broadcasted_iota(jnp.int32, (AREA, DH), 1)

    def near_ones(spots, sums):
        indices = [order[spot] for spot in spots]
        rows = [lax.div(index, tile_cols) for index in indices]
        homes = [place[0, index] for index in indices]
        keys_here = [
            jnp.concatenate([packed_k[home], far_k[jnp.minimum(spot, two - 1)]], axis=0)
            for home, spot in zip(homes, spots)
        ]
        values_here = [
            jnp.concatenate([own_s[home], far_s[jnp.minimum(spot, two - 1)]], axis=0)
            for home, spot in zip(homes, spots)
        ]
        biases = [
            mask_bias(
                (reached(reach, index, 1), reached(reach, index, 2)),
                room, row, index - row * tile_cols, 2 * AREA,
            )
            for index, row in zip(indices, rows)
        ]
        parts, highest = weigh([hosted_q[spot - three] for spot in spots], keys_here, biases)
        totals = [mix(part.astype(jnp.bfloat16), v) for part, v in zip(parts, values_here)]
        for spot, (total, sum_here), top in zip(spots, totals, highest):
            mixed[spot - three] = (total / sum_here).astype(jnp.bfloat16)
            sums = jnp.where(lane == spot, top + jnp.log(sum_here), sums)
        return sums

    @pl.when(is_inner(me[0]))
    def _():
        sums = in_chunks(three, one, near_ones, jnp.zeros((AREA, DH), jnp.float32))
        store_sums(mixed, one - three, sums)


def far_hosted_kernel(
    tile_cols, three, me, reach, place, order, rows_ok, cols_ok, hosted_q, packed_k, far_k,
    far_k2, weights, sums_out,
):
    own, _, far, far2 = frames_of(me[0])
    room = room_left((own, far, far2, own), rows_ok, cols_ok, 4 * AREA)
    lane = lax.broadcasted_iota(jnp.int32, (AREA, DH), 1)
    no = jnp.int32(0)

    def far_ones(spots, sums):
        indices = [order[spot] for spot in spots]
        rows = [lax.div(index, tile_cols) for index in indices]
        homes = [packed_k[place[0, index]] for index in indices]
        keys_here = [
            jnp.concatenate([home, far_k[spot], far_k2[spot], home], axis=0)
            for home, spot in zip(homes, spots)
        ]
        biases = [
            mask_bias(
                tuple(reached(reach, index, least) for least in (1, 2, 3)) + (no,),
                room, row, index - row * tile_cols, 4 * AREA,
            )
            for index, row in zip(indices, rows)
        ]
        parts, highest = weigh([hosted_q[spot] for spot in spots], keys_here, biases)
        for spot, part, top in zip(spots, parts, highest):
            weights[spot] = part.astype(jnp.bfloat16)
            sum_here = jnp.sum(part, axis=1, keepdims=True)
            sums = jnp.where(lane == spot, top + jnp.log(sum_here), sums)
        return sums

    @pl.when(is_inner(me[0]))
    def _():
        sums = in_chunks(0, three, far_ones, jnp.zeros((AREA, DH), jnp.float32))
        store_sums(sums_out, 0, sums)


def far_mix_kernel(three, me, place, order, weights, own_s, far_s, far_s2, sums, mixed):
    def far_ones(spots, carry):
        homes = [own_s[place[0, order[spot]]] for spot in spots]
        totals = [
            mix(weights[spot], jnp.concatenate([home, far_s[spot], far_s2[spot], home], axis=0))
            for spot, home in zip(spots, homes)
        ]
        for spot, (total, sum_here) in zip(spots, totals):
            mixed[spot] = (total / sum_here).astype(jnp.bfloat16)
        return carry

    @pl.when(is_inner(me[0]))
    def _():
        in_chunks(0, three, far_ones, 0)
        mixed[three : three + 3] = sums[...]


def tile_groups(tile_rows, tile_cols, body, carry):
    rows = 1

    def step(number, carry):
        here = [(number * rows + r, c) for r in range(rows) for c in range(tile_cols)]
        for first in range(0, len(here), GROUP):
            carry = body(here[first : first + GROUP], carry)
        return carry

    return lax.fori_loop(0, tile_rows // rows, step, carry)


def two_part(first, rest, spot, split, last, start=0):
    tile = first[jnp.minimum(spot, split - 1)]
    if last > split:
        other = rest[start + jnp.clip(spot - split, 0, last - split - 1)]
        tile = jnp.where(spot < split, tile, other)
    return tile


def own_weights_kernel(
    tile_rows, tile_cols, one, two, me, reach, place, order, rows_ok, cols_ok, queries, packed_k,
    near_k, near_rest, far_k, far_k2, weights, sums_out,
):
    mine = me[0]
    inner = is_inner(mine)
    room = room_left(frames_of(mine), rows_ok, cols_ok, 4 * AREA)
    lane = lax.broadcasted_iota(jnp.int32, (AREA, DH), 1)

    def weigh_tiles(numbers, carry):
        indices, query_list, key_list, biases = [], [], [], []
        for number in numbers:
            spot = number + jnp.where(number < two, 0, one - two)
            index = order[spot]
            r = lax.div(index, tile_cols)
            c = index - r * tile_cols
            home = place[0, index]
            near = two_part(near_k, near_rest, home, two, one)
            far = far_k[jnp.minimum(spot, two - 1)]
            far2 = far_k2[jnp.minimum(spot, two - 1)]
            near_reach, far_reach = reach[0, index], reach[1, index]
            allowed = (
                jnp.int32(1),
                (near_reach >= 1).astype(jnp.int32),
                (far_reach >= 1).astype(jnp.int32),
                (far_reach >= 2).astype(jnp.int32),
            )
            indices.append(index)
            biases.append(mask_bias(allowed, room, r, c, 4 * AREA))
            query_list.append(read_tile(queries, r, c))
            key_list.append(jnp.concatenate([packed_k[home], near, far, far2], axis=0))
        parts, _ = weigh(query_list, key_list, biases)
        for index, part in zip(indices, parts):
            weights[index] = part.astype(jnp.bfloat16)
        return carry

    def weigh_alone(here, sums):
        alone = room_left((mine,), rows_ok, cols_ok, AREA)
        biases = [mask_bias((jnp.int32(1),), alone, r, c, AREA) for r, c in here]
        parts, highest = weigh(
            [read_tile(queries, r, c) for r, c in here],
            [packed_k[place[0, r * tile_cols + c]] for r, c in here],
            biases,
        )
        totals = [jnp.sum(part, axis=1, keepdims=True) for part in parts]
        for (r, c), part, sum_here, top in zip(here, parts, totals, highest):
            index = r * tile_cols + c
            weights[index, :, :AREA] = part.astype(jnp.bfloat16)
            sums = jnp.where(lane == index, top + jnp.log(sum_here), sums)
        return sums

    @pl.when(inner)
    def _():
        in_chunks(0, tile_rows * tile_cols - one + two, weigh_tiles, 0, most=10)

    @pl.when(jnp.logical_not(inner))
    def _():
        nothing = jnp.zeros((AREA, DH), jnp.float32)
        sums_out[...] = tile_groups(tile_rows, tile_cols, weigh_alone, nothing)


def merged(own, own_sums, theirs, their_sums, index, spot):
    lane = lax.broadcasted_iota(jnp.int32, (AREA, DH), 1)
    gap = jnp.where(lane == spot, their_sums, 0.0) - jnp.where(lane == index, own_sums, 0.0)
    share = 1.0 / (1.0 + jnp.exp(jnp.sum(gap, axis=1, keepdims=True)))
    return share * own + (1.0 - share) * theirs.astype(jnp.float32)


def finished(spatial, temporal, valid):
    temporal = temporal.astype(jnp.bfloat16).astype(jnp.float32)
    tile = jnp.where(valid, spatial.astype(jnp.float32) + temporal, 0.0)
    return tile.astype(jnp.bfloat16).reshape(TS, TS, DH)


def tile_store(tile_cols, order, held, out, sems, spot):
    index = order[spot]
    r = lax.div(index, tile_cols)
    target = out.at[pl.ds(r * TS, TS), index - r * tile_cols]
    return pltpu.make_async_copy(held.at[spot], target, sems.at[spot])


def wait_stores(first, last, store):
    def wait(spot, carry):
        store(spot).wait()
        return carry

    lax.fori_loop(first, last, wait, 0)


def own_mix_kernel(
    tile_cols, count, one, two, three, me, reach, place, order, rows_ok, cols_ok, weights,
    own_sums, own_s, near_s, near_rest, far_s, far_s2, near_ones, first_o, out, held, sems,
):
    mine = me[0]
    inner = is_inner(mine)
    row_limit, col_limit = rows_ok[mine], cols_ok[mine]
    store = functools.partial(tile_store, tile_cols, order, held, out, sems)

    def finish(spots, results):
        for spot, result in zip(spots, results):
            index = order[spot]
            r = lax.div(index, tile_cols)
            valid = row_valid(r, index - r * tile_cols, row_limit, col_limit)
            held[spot] = finished(own_s[place[0, index]], result, valid)
            store(spot).start()

    def mix_tiles(spots, carry):
        totals = []
        for spot in spots:
            index = order[spot]
            home = place[0, index]
            near = two_part(near_s, near_rest, home, two, one, one - two)
            far = far_s[jnp.minimum(spot, two - 1)]
            far2 = far_s2[jnp.minimum(spot, three - 1)]
            values_here = jnp.concatenate([own_s[home], near, far, far2], axis=0)
            totals.append(mix(weights[index], values_here))
        finish(spots, [total / sum_here for total, sum_here in totals])
        return carry

    def mix_alone(spots):
        totals = []
        for spot in spots:
            index = order[spot]
            totals.append(mix(weights[index, :, :AREA], own_s[place[0, index]]))
        return [total / sum_here for total, sum_here in totals]

    def first_tiles(spots, carry):
        for spot, result in zip(spots, mix_alone(spots)):
            first_o[spot] = result.astype(jnp.bfloat16)
        return carry

    def merged_tiles(spots, carry):
        my_sums, their_sums = carry
        results = mix_alone(spots)
        for number, spot in enumerate(spots):
            index = order[spot]
            theirs = near_ones[spot - three]
            both = merged(results[number], my_sums, theirs, their_sums, index, spot)
            results[number] = jnp.where(reach[1, index] >= 1, both, results[number])
        finish(spots, results)
        return carry

    def alone_tiles(spots, carry):
        finish(spots, mix_alone(spots))
        return carry

    @pl.when(inner)
    def _():
        in_chunks(0, three, mix_tiles, 0)
        if count > one:
            in_chunks(one, count, mix_tiles, 0)
        wait_stores(0, three, store)

    @pl.when(jnp.logical_not(inner))
    def _():
        in_chunks(0, three, first_tiles, 0)
        if count > one:
            in_chunks(one, count, alone_tiles, 0)
        if one > three:
            in_chunks(three, one, merged_tiles, (own_sums[...], load_sums(near_ones, one - three)))
            wait_stores(three, one, store)

    if count > one:
        wait_stores(one, count, store)


def last_kernel(
    tile_cols, one, two, three, me, reach, place, order, rows_ok, cols_ok, done, weights, queries,
    packed_k, near_k, own_s, near_s, near_rest, far_s, late, own_sums, first_o, far_ones, out,
    held, sems,
):
    mine = me[0]
    inner = is_inner(mine)
    row_limit, col_limit = rows_ok[mine], cols_ok[mine]
    store = functools.partial(tile_store, tile_cols, order, held, out, sems)

    def finish(spots, results):
        for spot, result in zip(spots, results):
            index = order[spot]
            r = lax.div(index, tile_cols)
            valid = row_valid(r, index - r * tile_cols, row_limit, col_limit)
            held[spot] = finished(own_s[place[0, index]], result, valid)
            store(spot).start()

    def near_part(first, rest_start, home):
        return two_part(first, near_rest, home, two, one, rest_start)

    def late_mix(spot):
        index = order[spot]
        home = place[0, index]
        near = near_part(near_s, one - two, home)
        values_here = jnp.concatenate(
            [own_s[home], near, far_s[spot], late[spot - three]], axis=0
        )
        return mix(weights[index], values_here)

    def weigh_last(spots):
        room = room_left(frames_of(mine), rows_ok, cols_ok, 4 * AREA)
        query_list, key_list, value_list, biases = [], [], [], []
        for spot in spots:
            index = order[spot]
            r = lax.div(index, tile_cols)
            c = index - r * tile_cols
            home = place[0, index]
            allowed = (
                jnp.int32(1),
                (reach[0, index] >= 1).astype(jnp.int32),
                (reach[1, index] >= 1).astype(jnp.int32),
                jnp.int32(0),
            )
            biases.append(mask_bias(allowed, room, r, c, 4 * AREA))
            query_list.append(read_tile(queries, r, c))
            own, far = packed_k[home], late[spot - three + one - two]
            near = near_part(near_k, 0, home)
            key_list.append(jnp.concatenate([own, near, far, own], axis=0))
            own, far = own_s[home], late[spot - three]
            near = near_part(near_s, one - two, home)
            value_list.append(jnp.concatenate([own, near, far, own], axis=0))
        parts, _ = weigh(query_list, key_list, biases)
        return [part.astype(jnp.bfloat16) for part in parts], value_list

    if one > three:

        @pl.when(inner)
        def _():
            parts, value_list = weigh_last(range(two, one)) if one > two else ([], [])
            totals = [late_mix(spot) for spot in range(three, two)]
            totals += [mix(part, v) for part, v in zip(parts, value_list)]
            finish(range(three, one), [total / sum_here for total, sum_here in totals])
            wait_stores(three, one, store)

    @pl.when(jnp.logical_not(inner))
    def _():
        my_sums = own_sums[...]
        their_sums = load_sums(far_ones, three)

        def far_tiles(spots, carry):
            results = []
            for spot in spots:
                index = order[spot]
                own = first_o[spot].astype(jnp.float32)
                both = merged(own, my_sums, far_ones[spot], their_sums, index, spot)
                results.append(jnp.where(reach[1, index] >= 1, both, own))
            finish(spots, results)
            return carry

        in_chunks(0, three, far_tiles, 0)
        wait_stores(0, three, store)


def run_kernel(
    kernel, out_shape, scalars, arrays, scratch=(), scalar_outs=0, micros=4, from_hbm=0,
    to_hbm=0, in_place=False,
):
    outs = list(out_shape)
    arrays = [
        pltpu.with_memory_space_constraint(array, pltpu.HBM) if number < from_hbm else array
        for number, array in enumerate(arrays)
    ]
    in_hbm = pl.BlockSpec(memory_space=pltpu.HBM)
    in_specs = [in_hbm] * from_hbm + [vector_spec()] * (len(arrays) - from_hbm)
    out_specs = [vector_spec()] * (len(outs) - scalar_outs - to_hbm)
    out_specs += [scalar_spec()] * scalar_outs + [in_hbm] * to_hbm
    return pl.pallas_call(
        kernel,
        out_shape=outs,
        in_specs=[scalar_spec()] * len(scalars) + in_specs,
        out_specs=out_specs,
        scratch_shapes=list(scratch),
        input_output_aliases={len(scalars): 0} if in_place else {},
        compiler_params=pltpu.CompilerParams(vmem_limit_bytes=VMEM_LIMIT),
        cost_estimate=pl.CostEstimate(
            flops=int(micros * 1e9), bytes_accessed=int(micros * 1e6), transcendentals=0
        ),
    )(*scalars, *arrays)


def room_levels(count):
    shares = ((49, 34, 21), (51, 36, 24), (54, 42, 27))
    levels = [tuple(max(count * share // 60, 1) for share in level) for level in shares]
    return levels + [(count, count, count)]


def four_frames(queries, keys, values, back_reach, fwd_reach, valid_rows, valid_cols):
    _, token_rows, token_cols, _ = queries.shape
    tile_rows, tile_cols = token_rows // TS, token_cols // TS
    count = tile_rows * tile_cols
    shape = (token_rows, tile_cols, TS, DH)
    queries, keys, values = queries.reshape(shape), keys.reshape(shape), values.reshape(shape)
    me = lax.axis_index("frame").reshape(1).astype(jnp.int32)
    inward, across, outward = [(0, 1), (3, 2)], [(1, 2), (2, 1)], [(1, 0), (2, 3)]
    levels = room_levels(count)

    def tiles(number):
        return jax.ShapeDtypeStruct((number, AREA, DH), jnp.bfloat16)

    def ints(*sizes):
        return jax.ShapeDtypeStruct(sizes, jnp.int32)

    def send(array, pairs):
        return lax.ppermute(array, "frame", pairs)

    packed_k, reach, place, order, level = run_kernel(
        functools.partial(pack_kernel, tile_rows, tile_cols, levels),
        (tiles(count), ints(2, count), ints(2, count), ints(count), ints(1)),
        (
            me,
            pltpu.with_memory_space_constraint(back_reach, pltpu.HBM),
            pltpu.with_memory_space_constraint(fwd_reach, pltpu.HBM),
        ),
        (keys,),
        scratch=(pltpu.VMEM(shape, jnp.bfloat16), pltpu.SemaphoreType.DMA),
        scalar_outs=4,
        micros=2,
        from_hbm=1,
    )

    def with_room(one, two, three):
        def run(queries, values, packed_k, reach, place, order):
            far_k = send(packed_k[:two], across)
            near_k = send(packed_k[:two], inward)
            own_s, packed_q = run_kernel(
                functools.partial(spatial_kernel, tile_rows, tile_cols),
                (tiles(count), tiles(count)),
                (me, place, valid_rows, valid_cols),
                (queries, packed_k, values),
                scratch=(
                    pltpu.VMEM((count * AREA, DH), jnp.bfloat16),
                    pltpu.VMEM((count * AREA, DH), jnp.bfloat16),
                    pltpu.VMEM((count * AREA, 2 * DH), jnp.bfloat16),
                    pltpu.VMEM((tile_rows, 8, tile_cols * AREA), jnp.float32),
                    pltpu.VMEM((tile_rows, 8, (tile_cols - 2) * AREA), jnp.float32),
                ),
                micros=10,
            )
            far_s = send(own_s[:two], across)
            near_s = send(own_s[:two], inward)
            hosted_qa = send(packed_q[three:one], inward) if one > three else None
            first_q, far_k = lax.optimization_barrier((packed_q[:three], far_k))
            hosted_qb = send(first_q, inward)
            far_k2 = send(near_k, across)
            far_s2 = send(near_s[:three], across)
            returned_a = near_k
            if one > three:
                (hosted_a,) = run_kernel(
                    functools.partial(near_hosted_kernel, tile_cols, one, two, three),
                    (tiles(one - three + 3),),
                    (me, reach, place, order, valid_rows, valid_cols),
                    (hosted_qa, packed_k, far_k, own_s, far_s),
                    micros=0.6,
                )
                returned_a = send(hosted_a, outward)
            near_rest, late = near_k, near_s
            if one > two:
                rest_k, rest_s, late_s, _ = lax.optimization_barrier(
                    (packed_k[two:one], own_s[two:one], near_s[three:two], near_s)
                )
                near_rest = send(jnp.concatenate([rest_k, rest_s]), inward)
                late = send(jnp.concatenate([late_s, rest_s, rest_k]), across)
            hosted_w, sums = run_kernel(
                functools.partial(far_hosted_kernel, tile_cols, three),
                (jax.ShapeDtypeStruct((three, AREA, 4 * AREA), jnp.bfloat16), tiles(3)),
                (me, reach, place, order, valid_rows, valid_cols),
                (hosted_qb, packed_k, far_k, far_k2),
                micros=0.6,
            )
            (hosted_b,) = run_kernel(
                functools.partial(far_mix_kernel, three),
                (tiles(three + 3),),
                (me, place, order),
                (hosted_w, own_s, far_s, far_s2, sums),
                micros=2,
            )
            returned_b = send(hosted_b, outward)
            hosted_b, near_k = lax.optimization_barrier((hosted_b, near_k))
            own_w, own_sums = run_kernel(
                functools.partial(own_weights_kernel, tile_rows, tile_cols, one, two),
                (
                    jax.ShapeDtypeStruct((count, AREA, 4 * AREA), jnp.bfloat16),
                    jax.ShapeDtypeStruct((AREA, DH), jnp.float32),
                ),
                (me, reach, place, order, valid_rows, valid_cols),
                (queries, packed_k, near_k, near_rest, far_k, far_k2),
                micros=1,
            )
            staging = (
                pltpu.VMEM((count, TS, TS, DH), jnp.bfloat16),
                pltpu.SemaphoreType.DMA((count,)),
            )
            first_o, out = run_kernel(
                functools.partial(own_mix_kernel, tile_cols, count, one, two, three),
                (tiles(three), pltpu.HBM(shape, jnp.bfloat16)),
                (me, reach, place, order, valid_rows, valid_cols),
                (own_w, own_sums, own_s, near_s, near_rest, far_s, far_s2, returned_a),
                scratch=staging,
                micros=3,
                to_hbm=1,
            )
            (out,) = run_kernel(
                functools.partial(last_kernel, tile_cols, one, two, three),
                (pltpu.HBM(shape, jnp.bfloat16),),
                (me, reach, place, order, valid_rows, valid_cols),
                (
                    out, own_w, queries, packed_k, near_k, own_s, near_s, near_rest, far_s, late,
                    own_sums, first_o, returned_b,
                ),
                scratch=staging,
                micros=3,
                from_hbm=1,
                to_hbm=1,
                in_place=True,
            )
            return out

        return run

    branches = [with_room(*level) for level in levels]
    operands = (queries, values, packed_k, reach, place, order)
    out = lax.switch(level[0], branches, *operands)
    return out.reshape(1, token_rows, token_cols, DH)


def solution(mesh):
    in_specs = (
        P(("dp", "frame"), None, None, "row"),
        P(("dp", "frame"), None, None, "row"),
        P(("dp", "frame"), None, None, "row"),
        P("dp", None),
        P("dp", None),
        P("dp"),
        P("dp"),
    )
    out_specs = P(("dp", "frame"), None, None, "row")

    def block(*args):
        frames, _, token_cols, channels = args[0].shape
        line = mesh.shape["frame"] == 4 and frames == 1 and channels == DH
        if line and token_cols % (2 * TS) == 0 and 4 <= token_cols // TS:
            return four_frames(*args)
        return per_device(*args)

    return jax.shard_map(
        block, mesh=mesh, in_specs=in_specs, out_specs=out_specs, check_vma=False
    )
```

```python
import functools
import math

import jax
import jax.numpy as jnp
from jax import lax
from jax.experimental import pallas as pl
from jax.experimental.pallas import tpu as pltpu
from jax.sharding import PartitionSpec as P

DH = 128
TS = 8


def group_size(item_count, row_count):
    size = 1
    for option in range(1, item_count + 1):
        if item_count % option == 0 and option * row_count <= 1024:
            size = option
    return size


def attend_group(group_parts):
    query_rows, key_rows, value_rows, allowed = group_parts
    dot_terms = jnp.einsum("gmd,gnd->gmn", query_rows, key_rows, preferred_element_type=jnp.float32)
    query_sq = jnp.einsum("gmd,gmd->gm", query_rows, query_rows, preferred_element_type=jnp.float32)
    key_sq = jnp.einsum("gnd,gnd->gn", key_rows, key_rows, preferred_element_type=jnp.float32)
    distance = query_sq[:, :, None] + key_sq[:, None, :] - 2.0 * dot_terms
    scores = jnp.where(allowed, -distance * (0.5 / math.sqrt(query_rows.shape[2])), -jnp.inf)
    highest = jnp.max(scores, axis=2, keepdims=True)
    weights = jnp.exp(scores - highest)
    totals = jnp.sum(weights, axis=2, keepdims=True)
    mixed = jnp.einsum(
        "gmn,gnd->gmd", weights.astype(jnp.bfloat16), value_rows, preferred_element_type=jnp.float32
    )
    return mixed / totals


def attend_items(query_items, key_items, value_items, masks):
    item_count = query_items.shape[0]
    per_group = group_size(item_count, query_items.shape[1])
    groups = item_count // per_group

    def regroup(array):
        return array.reshape((groups, per_group) + array.shape[1:])

    mixed = lax.map(
        attend_group,
        (regroup(query_items), regroup(key_items), regroup(value_items), regroup(masks)),
    )
    return mixed.reshape((item_count,) + mixed.shape[2:])


def tile_split(block):
    frames, token_rows, token_cols, channels = block.shape
    heads = channels // DH
    return (
        block.reshape(frames, token_rows // TS, TS, token_cols // TS, TS, heads, DH)
        .transpose(5, 0, 1, 3, 2, 4, 6)
        .reshape(heads, frames, token_rows // TS * (token_cols // TS), TS * TS, DH)
    )


def neighbours(tiles, tile_rows, tile_cols):
    heads, frames, count_tiles, area, depth = tiles.shape
    grid = tiles.reshape(heads * frames, tile_rows, tile_cols, area, depth)
    padded = jnp.pad(grid, ((0, 0), (1, 1), (1, 1), (0, 0), (0, 0)))
    views = [
        padded[:, dy : dy + tile_rows, dx : dx + tile_cols] for dy in range(3) for dx in range(3)
    ]
    stacked = jnp.stack(views, axis=3)
    return stacked.reshape(heads * frames * count_tiles, 9 * area, depth)


def pad_tiles(tiles, total):
    return jnp.pad(tiles, ((0, 0), (0, 0), (0, total - tiles.shape[2]), (0, 0), (0, 0)))


def per_device(queries, keys, values, back_reach, fwd_reach, valid_rows, valid_cols):
    frames, token_rows, token_cols, channels = queries.shape
    heads = channels // DH
    tile_rows = token_rows // TS
    tile_cols = token_cols // TS
    count_tiles = tile_rows * tile_cols
    area = TS * TS
    frame_count = lax.axis_size("frame")
    frame_index = lax.axis_index("frame")
    padded_count = (count_tiles + frame_count - 1) // frame_count * frame_count
    tiles_here = padded_count // frame_count
    all_frames = frames * frame_count
    row_ids = jnp.arange(token_rows, dtype=jnp.int32)
    col_ids = jnp.arange(token_cols, dtype=jnp.int32)
    row_ok = row_ids[None, :] < valid_rows[:, None]
    col_ok = col_ids[None, :] < valid_cols[:, None]
    token_valid = row_ok[:, :, None] & col_ok[:, None, :]
    tile_valid_all = (
        token_valid.reshape(all_frames, tile_rows, TS, tile_cols, TS)
        .transpose(0, 1, 3, 2, 4)
        .reshape(all_frames, tile_rows, tile_cols, area)
    )
    tile_valid = lax.dynamic_slice_in_dim(tile_valid_all, frame_index * frames, frames, 0)
    padded_valid = jnp.pad(tile_valid, ((0, 0), (1, 1), (1, 1), (0, 0)))
    near_valid = jnp.stack(
        [
            padded_valid[:, dy : dy + tile_rows, dx : dx + tile_cols]
            for dy in range(3)
            for dx in range(3)
        ],
        axis=3,
    )
    near_valid = near_valid.reshape(frames, count_tiles, 1, 9 * area)
    query_factor = tile_valid.reshape(frames, count_tiles, area).astype(jnp.float32)
    query_t = tile_split(queries)
    key_t = tile_split(keys)
    masks = near_valid[None].reshape(heads * frames * count_tiles, 1, 9 * area)
    spatial = attend_items(
        query_t.reshape(heads * frames * count_tiles, area, DH),
        neighbours(key_t, tile_rows, tile_cols),
        neighbours(tile_split(values), tile_rows, tile_cols),
        masks,
    )
    spatial = spatial.reshape(heads, frames, count_tiles, area, DH)
    spatial_t = (spatial * query_factor[None, :, :, :, None]).astype(jnp.bfloat16)
    triple = jnp.stack(
        [
            pad_tiles(query_t, padded_count),
            pad_tiles(key_t, padded_count),
            pad_tiles(spatial_t, padded_count),
        ]
    )
    sent = lax.all_to_all(triple, "frame", split_axis=3, concat_axis=2, tiled=True)
    query_here, key_here, value_here = (sent[0], sent[1], sent[2])
    start = frame_index * tiles_here
    length = all_frames * area
    frame_of = jnp.arange(length, dtype=jnp.int32) // area
    frame_gap = frame_of[None, :] - frame_of[:, None]
    valid_flat = tile_valid_all.reshape(all_frames, count_tiles, area).transpose(1, 0, 2)
    valid_flat = jnp.pad(
        valid_flat, ((0, padded_count - count_tiles), (0, 0), (0, 0)), constant_values=True
    )
    valid_here = lax.dynamic_slice_in_dim(valid_flat, start, tiles_here, 0)
    back_here = lax.dynamic_slice_in_dim(
        jnp.pad(back_reach.reshape(count_tiles), (0, padded_count - count_tiles)),
        start,
        tiles_here,
        0,
    )
    fwd_here = lax.dynamic_slice_in_dim(
        jnp.pad(fwd_reach.reshape(count_tiles), (0, padded_count - count_tiles)),
        start,
        tiles_here,
        0,
    )
    key_ok = valid_here.reshape(tiles_here, length)
    allowed = (
        (frame_gap[None] >= -back_here[:, None, None])
        & (frame_gap[None] <= fwd_here[:, None, None])
        & key_ok[:, None, :]
    )
    time_masks = allowed[None].reshape(heads * tiles_here, length, length)

    def by_tile(array):
        return array.transpose(0, 2, 1, 3, 4).reshape(heads * tiles_here, length, DH)

    temporal = attend_items(
        by_tile(query_here), by_tile(key_here), by_tile(value_here), time_masks
    ).astype(jnp.bfloat16)
    temporal = temporal.reshape(heads, tiles_here, all_frames, area, DH).transpose(0, 2, 1, 3, 4)
    returned = lax.all_to_all(temporal, "frame", split_axis=1, concat_axis=2, tiled=True)[
        :, :, :count_tiles
    ]
    combined = (spatial_t.astype(jnp.float32) + returned.astype(jnp.float32)) * query_factor[
        None, :, :, :, None
    ]
    combined = combined.astype(jnp.bfloat16).reshape(
        heads, frames, tile_rows, tile_cols, TS, TS, DH
    )
    return combined.transpose(1, 2, 4, 3, 5, 0, 6).reshape(frames, token_rows, token_cols, channels)


SCALE = 1.0 / math.sqrt(DH)
MASKED = -1e30
AREA = TS * TS
GROUP = 10
PAIRS = 5
VMEM_LIMIT = 24 * 1024 * 1024
NT_DIMS = (((1,), (1,)), ((), ()))


def scalar_spec():
    return pl.BlockSpec(memory_space=pltpu.SMEM)


def vector_spec():
    return pl.BlockSpec(memory_space=pltpu.VMEM)


def read_tile(ref, row, col):
    return ref[pl.ds(row * TS, TS), col].reshape(AREA, DH)


def key_norms(keys):
    wide = keys.astype(jnp.float32)
    square = wide * wide
    high = square.astype(jnp.bfloat16)
    low = (square - high.astype(jnp.float32)).astype(jnp.bfloat16)
    ones = jnp.ones((8, 2 * DH), jnp.bfloat16)
    both = jnp.concatenate([high, low], axis=1)
    total = lax.dot_general(ones, both, NT_DIMS, preferred_element_type=jnp.float32)
    return total * (-0.5 * SCALE)


def row_valid(row, col, row_limit, col_limit):
    token = lax.broadcasted_iota(jnp.int32, (AREA, DH), 0)
    return (row * TS + (token >> 3) < row_limit) & (col * TS + (token & 7) < col_limit)


def pack_kernel(
    tile_rows, tile_cols, levels, me, back, fwd, keys, packed, reach, place, order, level, held,
    sem,
):
    load = pltpu.make_async_copy(keys, held, sem)
    load.start()
    left = me[0] < 2
    most = [None] * 4
    tiles = [(r, c) for r in range(tile_rows) for c in range(tile_cols)]
    for way in range(2):
        counts = [jnp.int32(0)] * 4
        for index, (r, c) in enumerate(tiles):
            toward, away = back[r, c], fwd[r, c]
            value = jnp.where(left, toward, away) if way == 0 else jnp.where(left, away, toward)
            reach[way, index] = value
            counts = [counts[v] + (value >= v).astype(jnp.int32) for v in range(4)]
        for v in (1, 2, 3):
            most[v] = counts[v] if way == 0 else jnp.maximum(most[v], counts[v])
        spots = [counts[1], counts[2], counts[3], jnp.int32(0)]
        for index in range(len(tiles)):
            value = jnp.minimum(reach[way, index], 3)
            spot = spots[0]
            for v in (1, 2, 3):
                spot = jnp.where(value == v, spots[v], spot)
            spots = [spots[v] + (value == v).astype(jnp.int32) for v in range(4)]
            place[way, index] = spot
            if way == 1:
                order[spot] = index
    chosen = jnp.int32(0)
    for one, two, three in levels[:-1]:
        over = (most[1] > one) | (most[2] > two) | (most[3] > three)
        chosen += over.astype(jnp.int32)
    level[0] = chosen
    load.wait()

    def pack_row(r, carry):
        for c in range(tile_cols):
            packed[place[0, r * tile_cols + c]] = read_tile(held, r, c)
        return carry

    lax.fori_loop(0, tile_rows, pack_row, 0)


def spatial_kernel(
    tile_rows, tile_cols, me, place, rows_ok, cols_ok, queries, packed_k, values, mixed, packed_q,
    query_t, key_t, value_t, bias_even, bias_odd,
):
    row_limit, col_limit = rows_ok[me[0]], cols_ok[me[0]]
    wide = tile_cols * AREA
    value_t[:, DH:] = jnp.ones((value_t.shape[0], DH), jnp.bfloat16)

    def lane_bias(r, first, count):
        start = pl.multiple_of((r * tile_cols + first) * AREA, AREA)
        norms = key_norms(key_t[pl.ds(start, count * AREA)])
        lane = lax.broadcasted_iota(jnp.int32, (8, count * AREA), 1) + first * AREA
        valid = (r * TS + ((lane >> 3) & 7) < row_limit) & (
            (lane >> 6) * TS + (lane & 7) < col_limit
        )
        return jnp.where(valid, norms, MASKED)

    def retile_row(r, carry):
        for c in range(tile_cols):
            index = r * tile_cols + c
            span = pl.ds(pl.multiple_of(index * AREA, AREA), AREA)
            tile_q = read_tile(queries, r, c)
            query_t[span] = tile_q
            packed_q[place[1, index]] = tile_q
            key_t[span] = packed_k[place[0, index]]
            value_t[span, :DH] = read_tile(values, r, c)
        bias_even[r] = lane_bias(r, 0, tile_cols)
        bias_odd[r] = lane_bias(r, 1, tile_cols - 2)
        return carry

    lax.fori_loop(0, tile_rows, retile_row, 0)
    lane_tile = lax.broadcasted_iota(jnp.int32, (8, 4 * AREA), 1) >> 6

    def attend_row(r, carry):
        first_row = jnp.clip(r - 1, 0, tile_rows - 3)
        for first_pair in range(0, tile_cols // 2, PAIRS):
            attend_pairs(r, first_row, range(first_pair, min(first_pair + PAIRS, tile_cols // 2)))
        return carry

    def attend_pairs(r, first_row, pairs):
        first_cols = [min(max(2 * pair - 1, 0), tile_cols - 4) for pair in pairs]
        dots, spans = [], []
        for pair, first_col in zip(pairs, first_cols):
            start = (r * tile_cols + 2 * pair) * AREA
            query = query_t[pl.ds(pl.multiple_of(start, AREA), 2 * AREA)]
            starts = [((first_row + step) * tile_cols + first_col) * AREA for step in range(3)]
            spans.append([pl.ds(pl.multiple_of(start, AREA), 4 * AREA) for start in starts])
            dots.append(
                [
                    lax.dot_general(
                        query, key_t[span], NT_DIMS, preferred_element_type=jnp.float32
                    )
                    for span in spans[-1]
                ]
            )
        scores = []
        for pair, first_col, parts in zip(pairs, first_cols, dots):
            scores.append([])
            for step, part in enumerate(parts):
                key_row = first_row + step
                table = bias_odd if first_col % 2 else bias_even
                lane_start = (first_col - first_col % 2) * AREA
                bias = table[key_row, :, lane_start : lane_start + 4 * AREA]
                near_row = jnp.abs(key_row - r) <= 1
                both = []
                for half in range(2):
                    gap = lane_tile + (first_col - 2 * pair - half)
                    near = (gap >= -1) & (gap <= 1) & near_row
                    here = part[half * AREA : (half + 1) * AREA].reshape(TS, 8, 4 * AREA)
                    here = here * SCALE + jnp.where(near, bias, MASKED)[None]
                    both.append(here.reshape(AREA, 4 * AREA))
                scores[-1].append(jnp.concatenate(both, axis=0))
        tops = [jnp.maximum(jnp.maximum(one[0], one[1]), one[2]) for one in scores]
        tops = [jnp.max(top, axis=1, keepdims=True) for top in tops]
        totals = []
        for one, top, where in zip(scores, tops, spans):
            weights = [jnp.exp(score - top).astype(jnp.bfloat16) for score in one]
            parts = [
                jnp.dot(weight, value_t[span], preferred_element_type=jnp.float32)
                for weight, span in zip(weights, where)
            ]
            totals.append((parts[0] + parts[1]) + parts[2])
        for pair, total in zip(pairs, totals):
            result = total[:, :DH] / total[:, DH:]
            for half in range(2):
                valid = row_valid(r, 2 * pair + half, row_limit, col_limit)
                tile = jnp.where(valid, result[half * AREA : (half + 1) * AREA], 0.0)
                spot = place[0, r * tile_cols + 2 * pair + half]
                mixed[spot] = tile.astype(jnp.bfloat16)

    lax.fori_loop(0, tile_rows, attend_row, 0)


def frames_of(mine):
    left = mine < 2
    return mine, jnp.where(left, 0, 3), jnp.where(left, 2, 1), jnp.where(left, 3, 0)


def by_block(picks, lanes):
    block = lax.broadcasted_iota(jnp.int32, (8, lanes), 1) >> 6
    chosen = jnp.full((8, lanes), picks[0], jnp.int32)
    for number in range(1, lanes // AREA):
        chosen = jnp.where(block == number, picks[number], chosen)
    return chosen


def room_left(frames, rows_ok, cols_ok, lanes):
    lane = lax.broadcasted_iota(jnp.int32, (8, lanes), 1)
    row_room = by_block([rows_ok[frame] for frame in frames], lanes) - ((lane >> 3) & 7)
    col_room = by_block([cols_ok[frame] for frame in frames], lanes) - (lane & 7)
    return row_room, col_room


def weigh(queries, keys_here, biases):
    parts, highest = [], []
    dots = [
        lax.dot_general(query, key, NT_DIMS, preferred_element_type=jnp.float32)
        for query, key in zip(queries, keys_here)
    ]
    norms = [key_norms(key) for key in keys_here]
    for dot, norm, bias in zip(dots, norms, biases):
        lanes = dot.shape[1]
        part = dot.reshape(TS, 8, lanes) * SCALE + (norm + bias)[None]
        parts.append(part.reshape(AREA, lanes))
    highest = [jnp.max(part, axis=1, keepdims=True) for part in parts]
    return [jnp.exp(part - top) for part, top in zip(parts, highest)], highest


def mask_bias(allowed, room, row, col, lanes):
    valid = (room[0] > row * TS) & (room[1] > col * TS) & (by_block(allowed, lanes) > 0)
    return jnp.where(valid, 0.0, MASKED)


def mix(weights, values_here):
    ones = jnp.ones(values_here.shape, jnp.bfloat16)
    total = jnp.dot(
        weights,
        jnp.concatenate([values_here, ones], axis=1),
        preferred_element_type=jnp.float32,
    )
    return total[:, :DH], total[:, DH:]


def in_chunks(first, last, body, carry, most=None):
    most = most or (12 if last - first <= 30 else 4)
    size = max(option for option in range(1, most + 1) if (last - first) % option == 0)
    if size == last - first:
        return body(list(range(first, last)), carry)

    def chunk(number, carry):
        return body([first + number * size + step for step in range(size)], carry)

    return lax.fori_loop(0, (last - first) // size, chunk, carry)


def is_inner(mine):
    return (mine == 1) | (mine == 2)


def store_sums(ref, first, sums):
    for step in range(3):
        piece = sums.astype(jnp.bfloat16)
        ref[first + step] = piece
        sums = sums - piece.astype(jnp.float32)


def load_sums(ref, first):
    pieces = [ref[first + step].astype(jnp.float32) for step in range(3)]
    return (pieces[0] + pieces[1]) + pieces[2]


def reached(reach, index, least):
    return (reach[1, index] >= least).astype(jnp.int32)


def near_hosted_kernel(
    tile_cols, one, two, three, me, reach, place, order, rows_ok, cols_ok, hosted_q, packed_k,
    far_k, own_s, far_s, mixed,
):
    own, _, far, _ = frames_of(me[0])
    room = room_left((own, far), rows_ok, cols_ok, 2 * AREA)
    lane = lax.broadcasted_iota(jnp.int32, (AREA, DH), 1)

    def near_ones(spots, sums):
        indices = [order[spot] for spot in spots]
        rows = [lax.div(index, tile_cols) for index in indices]
        homes = [place[0, index] for index in indices]
        keys_here = [
            jnp.concatenate([packed_k[home], far_k[jnp.minimum(spot, two - 1)]], axis=0)
            for home, spot in zip(homes, spots)
        ]
        values_here = [
            jnp.concatenate([own_s[home], far_s[jnp.minimum(spot, two - 1)]], axis=0)
            for home, spot in zip(homes, spots)
        ]
        biases = [
            mask_bias(
                (reached(reach, index, 1), reached(reach, index, 2)),
                room, row, index - row * tile_cols, 2 * AREA,
            )
            for index, row in zip(indices, rows)
        ]
        parts, highest = weigh([hosted_q[spot - three] for spot in spots], keys_here, biases)
        totals = [mix(part.astype(jnp.bfloat16), v) for part, v in zip(parts, values_here)]
        for spot, (total, sum_here), top in zip(spots, totals, highest):
            mixed[spot - three] = (total / sum_here).astype(jnp.bfloat16)
            sums = jnp.where(lane == spot, top + jnp.log(sum_here), sums)
        return sums

    @pl.when(is_inner(me[0]))
    def _():
        sums = in_chunks(three, one, near_ones, jnp.zeros((AREA, DH), jnp.float32))
        store_sums(mixed, one - three, sums)


def far_hosted_kernel(
    tile_cols, three, me, reach, place, order, rows_ok, cols_ok, hosted_q, packed_k, far_k,
    far_k2, weights, sums_out,
):
    own, _, far, far2 = frames_of(me[0])
    room = room_left((own, far, far2, own), rows_ok, cols_ok, 4 * AREA)
    lane = lax.broadcasted_iota(jnp.int32, (AREA, DH), 1)
    no = jnp.int32(0)

    def far_ones(spots, sums):
        indices = [order[spot] for spot in spots]
        rows = [lax.div(index, tile_cols) for index in indices]
        homes = [packed_k[place[0, index]] for index in indices]
        keys_here = [
            jnp.concatenate([home, far_k[spot], far_k2[spot], home], axis=0)
            for home, spot in zip(homes, spots)
        ]
        biases = [
            mask_bias(
                tuple(reached(reach, index, least) for least in (1, 2, 3)) + (no,),
                room, row, index - row * tile_cols, 4 * AREA,
            )
            for index, row in zip(indices, rows)
        ]
        parts, highest = weigh([hosted_q[spot] for spot in spots], keys_here, biases)
        for spot, part, top in zip(spots, parts, highest):
            weights[spot] = part.astype(jnp.bfloat16)
            sum_here = jnp.sum(part, axis=1, keepdims=True)
            sums = jnp.where(lane == spot, top + jnp.log(sum_here), sums)
        return sums

    @pl.when(is_inner(me[0]))
    def _():
        sums = in_chunks(0, three, far_ones, jnp.zeros((AREA, DH), jnp.float32))
        store_sums(sums_out, 0, sums)


def far_mix_kernel(three, me, place, order, weights, own_s, far_s, far_s2, sums, mixed):
    def far_ones(spots, carry):
        homes = [own_s[place[0, order[spot]]] for spot in spots]
        totals = [
            mix(weights[spot], jnp.concatenate([home, far_s[spot], far_s2[spot], home], axis=0))
            for spot, home in zip(spots, homes)
        ]
        for spot, (total, sum_here) in zip(spots, totals):
            mixed[spot] = (total / sum_here).astype(jnp.bfloat16)
        return carry

    @pl.when(is_inner(me[0]))
    def _():
        in_chunks(0, three, far_ones, 0)
        mixed[three : three + 3] = sums[...]


def tile_groups(tile_rows, tile_cols, body, carry):
    rows = 1

    def step(number, carry):
        here = [(number * rows + r, c) for r in range(rows) for c in range(tile_cols)]
        for first in range(0, len(here), GROUP):
            carry = body(here[first : first + GROUP], carry)
        return carry

    return lax.fori_loop(0, tile_rows // rows, step, carry)


def two_part(first, rest, spot, split, last, start=0):
    tile = first[jnp.minimum(spot, split - 1)]
    if last > split:
        other = rest[start + jnp.clip(spot - split, 0, last - split - 1)]
        tile = jnp.where(spot < split, tile, other)
    return tile


def own_weights_kernel(
    tile_rows, tile_cols, one, two, me, reach, place, order, rows_ok, cols_ok, queries, packed_k,
    near_k, near_rest, far_k, far_k2, weights, sums_out,
):
    mine = me[0]
    inner = is_inner(mine)
    room = room_left(frames_of(mine), rows_ok, cols_ok, 4 * AREA)
    lane = lax.broadcasted_iota(jnp.int32, (AREA, DH), 1)

    def weigh_tiles(numbers, carry):
        indices, query_list, key_list, biases = [], [], [], []
        for number in numbers:
            spot = number + jnp.where(number < two, 0, one - two)
            index = order[spot]
            r = lax.div(index, tile_cols)
            c = index - r * tile_cols
            home = place[0, index]
            near = two_part(near_k, near_rest, home, two, one)
            far = far_k[jnp.minimum(spot, two - 1)]
            far2 = far_k2[jnp.minimum(spot, two - 1)]
            near_reach, far_reach = reach[0, index], reach[1, index]
            allowed = (
                jnp.int32(1),
                (near_reach >= 1).astype(jnp.int32),
                (far_reach >= 1).astype(jnp.int32),
                (far_reach >= 2).astype(jnp.int32),
            )
            indices.append(index)
            biases.append(mask_bias(allowed, room, r, c, 4 * AREA))
            query_list.append(read_tile(queries, r, c))
            key_list.append(jnp.concatenate([packed_k[home], near, far, far2], axis=0))
        parts, _ = weigh(query_list, key_list, biases)
        for index, part in zip(indices, parts):
            weights[index] = part.astype(jnp.bfloat16)
        return carry

    def weigh_alone(here, sums):
        alone = room_left((mine,), rows_ok, cols_ok, AREA)
        biases = [mask_bias((jnp.int32(1),), alone, r, c, AREA) for r, c in here]
        parts, highest = weigh(
            [read_tile(queries, r, c) for r, c in here],
            [packed_k[place[0, r * tile_cols + c]] for r, c in here],
            biases,
        )
        totals = [jnp.sum(part, axis=1, keepdims=True) for part in parts]
        for (r, c), part, sum_here, top in zip(here, parts, totals, highest):
            index = r * tile_cols + c
            weights[index, :, :AREA] = part.astype(jnp.bfloat16)
            sums = jnp.where(lane == index, top + jnp.log(sum_here), sums)
        return sums

    @pl.when(inner)
    def _():
        in_chunks(0, tile_rows * tile_cols - one + two, weigh_tiles, 0, most=10)

    @pl.when(jnp.logical_not(inner))
    def _():
        nothing = jnp.zeros((AREA, DH), jnp.float32)
        sums_out[...] = tile_groups(tile_rows, tile_cols, weigh_alone, nothing)


def merged(own, own_sums, theirs, their_sums, index, spot):
    lane = lax.broadcasted_iota(jnp.int32, (AREA, DH), 1)
    gap = jnp.where(lane == spot, their_sums, 0.0) - jnp.where(lane == index, own_sums, 0.0)
    share = 1.0 / (1.0 + jnp.exp(jnp.sum(gap, axis=1, keepdims=True)))
    return share * own + (1.0 - share) * theirs.astype(jnp.float32)


def finished(spatial, temporal, valid):
    temporal = temporal.astype(jnp.bfloat16).astype(jnp.float32)
    tile = jnp.where(valid, spatial.astype(jnp.float32) + temporal, 0.0)
    return tile.astype(jnp.bfloat16).reshape(TS, TS, DH)


def tile_store(tile_cols, order, held, out, sems, spot):
    index = order[spot]
    r = lax.div(index, tile_cols)
    target = out.at[pl.ds(r * TS, TS), index - r * tile_cols]
    return pltpu.make_async_copy(held.at[spot], target, sems.at[spot])


def wait_stores(first, last, store):
    def wait(spot, carry):
        store(spot).wait()
        return carry

    lax.fori_loop(first, last, wait, 0)


def own_mix_kernel(
    tile_cols, count, one, two, three, me, reach, place, order, rows_ok, cols_ok, weights,
    own_sums, own_s, near_s, near_rest, far_s, far_s2, near_ones, first_o, out, held, sems,
):
    mine = me[0]
    inner = is_inner(mine)
    row_limit, col_limit = rows_ok[mine], cols_ok[mine]
    store = functools.partial(tile_store, tile_cols, order, held, out, sems)

    def finish(spots, results):
        for spot, result in zip(spots, results):
            index = order[spot]
            r = lax.div(index, tile_cols)
            valid = row_valid(r, index - r * tile_cols, row_limit, col_limit)
            held[spot] = finished(own_s[place[0, index]], result, valid)
            store(spot).start()

    def mix_tiles(spots, carry):
        totals = []
        for spot in spots:
            index = order[spot]
            home = place[0, index]
            near = two_part(near_s, near_rest, home, two, one, one - two)
            far = far_s[jnp.minimum(spot, two - 1)]
            far2 = far_s2[jnp.minimum(spot, three - 1)]
            values_here = jnp.concatenate([own_s[home], near, far, far2], axis=0)
            totals.append(mix(weights[index], values_here))
        finish(spots, [total / sum_here for total, sum_here in totals])
        return carry

    def mix_alone(spots):
        totals = []
        for spot in spots:
            index = order[spot]
            totals.append(mix(weights[index, :, :AREA], own_s[place[0, index]]))
        return [total / sum_here for total, sum_here in totals]

    def first_tiles(spots, carry):
        for spot, result in zip(spots, mix_alone(spots)):
            first_o[spot] = result.astype(jnp.bfloat16)
        return carry

    def merged_tiles(spots, carry):
        my_sums, their_sums = carry
        results = mix_alone(spots)
        for number, spot in enumerate(spots):
            index = order[spot]
            theirs = near_ones[spot - three]
            both = merged(results[number], my_sums, theirs, their_sums, index, spot)
            results[number] = jnp.where(reach[1, index] >= 1, both, results[number])
        finish(spots, results)
        return carry

    def alone_tiles(spots, carry):
        finish(spots, mix_alone(spots))
        return carry

    @pl.when(inner)
    def _():
        in_chunks(0, three, mix_tiles, 0)
        if count > one:
            in_chunks(one, count, mix_tiles, 0)
        wait_stores(0, three, store)

    @pl.when(jnp.logical_not(inner))
    def _():
        in_chunks(0, three, first_tiles, 0)
        if count > one:
            in_chunks(one, count, alone_tiles, 0)
        if one > three:
            in_chunks(three, one, merged_tiles, (own_sums[...], load_sums(near_ones, one - three)))
            wait_stores(three, one, store)

    if count > one:
        wait_stores(one, count, store)


def last_kernel(
    tile_cols, one, two, three, me, reach, place, order, rows_ok, cols_ok, done, weights, queries,
    packed_k, near_k, own_s, near_s, near_rest, far_s, late, own_sums, first_o, far_ones, out,
    held, sems,
):
    mine = me[0]
    inner = is_inner(mine)
    row_limit, col_limit = rows_ok[mine], cols_ok[mine]
    store = functools.partial(tile_store, tile_cols, order, held, out, sems)

    def finish(spots, results):
        for spot, result in zip(spots, results):
            index = order[spot]
            r = lax.div(index, tile_cols)
            valid = row_valid(r, index - r * tile_cols, row_limit, col_limit)
            held[spot] = finished(own_s[place[0, index]], result, valid)
            store(spot).start()

    def near_part(first, rest_start, home):
        return two_part(first, near_rest, home, two, one, rest_start)

    def late_mix(spot):
        index = order[spot]
        home = place[0, index]
        near = near_part(near_s, one - two, home)
        values_here = jnp.concatenate(
            [own_s[home], near, far_s[spot], late[spot - three]], axis=0
        )
        return mix(weights[index], values_here)

    def weigh_last(spots):
        room = room_left(frames_of(mine), rows_ok, cols_ok, 4 * AREA)
        query_list, key_list, value_list, biases = [], [], [], []
        for spot in spots:
            index = order[spot]
            r = lax.div(index, tile_cols)
            c = index - r * tile_cols
            home = place[0, index]
            allowed = (
                jnp.int32(1),
                (reach[0, index] >= 1).astype(jnp.int32),
                (reach[1, index] >= 1).astype(jnp.int32),
                jnp.int32(0),
            )
            biases.append(mask_bias(allowed, room, r, c, 4 * AREA))
            query_list.append(read_tile(queries, r, c))
            own, far = packed_k[home], late[spot - three + one - two]
            near = near_part(near_k, 0, home)
            key_list.append(jnp.concatenate([own, near, far, own], axis=0))
            own, far = own_s[home], late[spot - three]
            near = near_part(near_s, one - two, home)
            value_list.append(jnp.concatenate([own, near, far, own], axis=0))
        parts, _ = weigh(query_list, key_list, biases)
        return [part.astype(jnp.bfloat16) for part in parts], value_list

    if one > three:

        @pl.when(inner)
        def _():
            parts, value_list = weigh_last(range(two, one)) if one > two else ([], [])
            totals = [late_mix(spot) for spot in range(three, two)]
            totals += [mix(part, v) for part, v in zip(parts, value_list)]
            finish(range(three, one), [total / sum_here for total, sum_here in totals])
            wait_stores(three, one, store)

    @pl.when(jnp.logical_not(inner))
    def _():
        my_sums = own_sums[...]
        their_sums = load_sums(far_ones, three)

        def far_tiles(spots, carry):
            results = []
            for spot in spots:
                index = order[spot]
                own = first_o[spot].astype(jnp.float32)
                both = merged(own, my_sums, far_ones[spot], their_sums, index, spot)
                results.append(jnp.where(reach[1, index] >= 1, both, own))
            finish(spots, results)
            return carry

        in_chunks(0, three, far_tiles, 0)
        wait_stores(0, three, store)


def run_kernel(
    kernel, out_shape, scalars, arrays, scratch=(), scalar_outs=0, micros=4, from_hbm=0,
    to_hbm=0, in_place=False,
):
    outs = list(out_shape)
    arrays = [
        pltpu.with_memory_space_constraint(array, pltpu.HBM) if number < from_hbm else array
        for number, array in enumerate(arrays)
    ]
    in_hbm = pl.BlockSpec(memory_space=pltpu.HBM)
    in_specs = [in_hbm] * from_hbm + [vector_spec()] * (len(arrays) - from_hbm)
    out_specs = [vector_spec()] * (len(outs) - scalar_outs - to_hbm)
    out_specs += [scalar_spec()] * scalar_outs + [in_hbm] * to_hbm
    return pl.pallas_call(
        kernel,
        out_shape=outs,
        in_specs=[scalar_spec()] * len(scalars) + in_specs,
        out_specs=out_specs,
        scratch_shapes=list(scratch),
        input_output_aliases={len(scalars): 0} if in_place else {},
        compiler_params=pltpu.CompilerParams(vmem_limit_bytes=VMEM_LIMIT),
        cost_estimate=pl.CostEstimate(
            flops=int(micros * 1e9), bytes_accessed=int(micros * 1e6), transcendentals=0
        ),
    )(*scalars, *arrays)


def room_levels(count):
    shares = ((49, 34, 22), (51, 36, 24), (54, 42, 27))
    levels = [tuple(max(count * share // 60, 1) for share in level) for level in shares]
    return levels + [(count, count, count)]


def four_frames(queries, keys, values, back_reach, fwd_reach, valid_rows, valid_cols):
    _, token_rows, token_cols, _ = queries.shape
    tile_rows, tile_cols = token_rows // TS, token_cols // TS
    count = tile_rows * tile_cols
    shape = (token_rows, tile_cols, TS, DH)
    queries, keys, values = queries.reshape(shape), keys.reshape(shape), values.reshape(shape)
    me = lax.axis_index("frame").reshape(1).astype(jnp.int32)
    inward, across, outward = [(0, 1), (3, 2)], [(1, 2), (2, 1)], [(1, 0), (2, 3)]
    levels = room_levels(count)

    def tiles(number):
        return jax.ShapeDtypeStruct((number, AREA, DH), jnp.bfloat16)

    def ints(*sizes):
        return jax.ShapeDtypeStruct(sizes, jnp.int32)

    def send(array, pairs):
        return lax.ppermute(array, "frame", pairs)

    packed_k, reach, place, order, level = run_kernel(
        functools.partial(pack_kernel, tile_rows, tile_cols, levels),
        (tiles(count), ints(2, count), ints(2, count), ints(count), ints(1)),
        (
            me,
            pltpu.with_memory_space_constraint(back_reach, pltpu.HBM),
            pltpu.with_memory_space_constraint(fwd_reach, pltpu.HBM),
        ),
        (keys,),
        scratch=(pltpu.VMEM(shape, jnp.bfloat16), pltpu.SemaphoreType.DMA),
        scalar_outs=4,
        micros=2,
        from_hbm=1,
    )

    def with_room(one, two, three):
        def run(queries, values, packed_k, reach, place, order):
            far_k = send(packed_k[:two], across)
            near_k = send(packed_k[:two], inward)
            own_s, packed_q = run_kernel(
                functools.partial(spatial_kernel, tile_rows, tile_cols),
                (tiles(count), tiles(count)),
                (me, place, valid_rows, valid_cols),
                (queries, packed_k, values),
                scratch=(
                    pltpu.VMEM((count * AREA, DH), jnp.bfloat16),
                    pltpu.VMEM((count * AREA, DH), jnp.bfloat16),
                    pltpu.VMEM((count * AREA, 2 * DH), jnp.bfloat16),
                    pltpu.VMEM((tile_rows, 8, tile_cols * AREA), jnp.float32),
                    pltpu.VMEM((tile_rows, 8, (tile_cols - 2) * AREA), jnp.float32),
                ),
                micros=10,
            )
            far_s = send(own_s[:two], across)
            near_s = send(own_s[:two], inward)
            hosted_qa = send(packed_q[three:one], inward) if one > three else None
            first_q, far_k = lax.optimization_barrier((packed_q[:three], far_k))
            hosted_qb = send(first_q, inward)
            far_k2 = send(near_k, across)
            far_s2 = send(near_s[:three], across)
            returned_a = near_k
            if one > three:
                (hosted_a,) = run_kernel(
                    functools.partial(near_hosted_kernel, tile_cols, one, two, three),
                    (tiles(one - three + 3),),
                    (me, reach, place, order, valid_rows, valid_cols),
                    (hosted_qa, packed_k, far_k, own_s, far_s),
                    micros=0.6,
                )
                returned_a = send(hosted_a, outward)
            near_rest, late = near_k, near_s
            if one > two:
                rest_k, rest_s, late_s, _ = lax.optimization_barrier(
                    (packed_k[two:one], own_s[two:one], near_s[three:two], near_s)
                )
                near_rest = send(jnp.concatenate([rest_k, rest_s]), inward)
                late = send(jnp.concatenate([late_s, rest_s, rest_k]), across)
            hosted_w, sums = run_kernel(
                functools.partial(far_hosted_kernel, tile_cols, three),
                (jax.ShapeDtypeStruct((three, AREA, 4 * AREA), jnp.bfloat16), tiles(3)),
                (me, reach, place, order, valid_rows, valid_cols),
                (hosted_qb, packed_k, far_k, far_k2),
                micros=0.6,
            )
            (hosted_b,) = run_kernel(
                functools.partial(far_mix_kernel, three),
                (tiles(three + 3),),
                (me, place, order),
                (hosted_w, own_s, far_s, far_s2, sums),
                micros=2,
            )
            returned_b = send(hosted_b, outward)
            hosted_b, near_k = lax.optimization_barrier((hosted_b, near_k))
            own_w, own_sums = run_kernel(
                functools.partial(own_weights_kernel, tile_rows, tile_cols, one, two),
                (
                    jax.ShapeDtypeStruct((count, AREA, 4 * AREA), jnp.bfloat16),
                    jax.ShapeDtypeStruct((AREA, DH), jnp.float32),
                ),
                (me, reach, place, order, valid_rows, valid_cols),
                (queries, packed_k, near_k, near_rest, far_k, far_k2),
                micros=1,
            )
            staging = (
                pltpu.VMEM((count, TS, TS, DH), jnp.bfloat16),
                pltpu.SemaphoreType.DMA((count,)),
            )
            first_o, out = run_kernel(
                functools.partial(own_mix_kernel, tile_cols, count, one, two, three),
                (tiles(three), pltpu.HBM(shape, jnp.bfloat16)),
                (me, reach, place, order, valid_rows, valid_cols),
                (own_w, own_sums, own_s, near_s, near_rest, far_s, far_s2, returned_a),
                scratch=staging,
                micros=3,
                to_hbm=1,
            )
            (out,) = run_kernel(
                functools.partial(last_kernel, tile_cols, one, two, three),
                (pltpu.HBM(shape, jnp.bfloat16),),
                (me, reach, place, order, valid_rows, valid_cols),
                (
                    out, own_w, queries, packed_k, near_k, own_s, near_s, near_rest, far_s, late,
                    own_sums, first_o, returned_b,
                ),
                scratch=staging,
                micros=3,
                from_hbm=1,
                to_hbm=1,
                in_place=True,
            )
            return out

        return run

    branches = [with_room(*level) for level in levels]
    operands = (queries, values, packed_k, reach, place, order)
    out = lax.switch(level[0], branches, *operands)
    return out.reshape(1, token_rows, token_cols, DH)


def solution(mesh):
    in_specs = (
        P(("dp", "frame"), None, None, "row"),
        P(("dp", "frame"), None, None, "row"),
        P(("dp", "frame"), None, None, "row"),
        P("dp", None),
        P("dp", None),
        P("dp"),
        P("dp"),
    )
    out_specs = P(("dp", "frame"), None, None, "row")

    def block(*args):
        frames, _, token_cols, channels = args[0].shape
        line = mesh.shape["frame"] == 4 and frames == 1 and channels == DH
        if line and token_cols % (2 * TS) == 0 and 4 <= token_cols // TS:
            return four_frames(*args)
        return per_device(*args)

    return jax.shard_map(
        block, mesh=mesh, in_specs=in_specs, out_specs=out_specs, check_vma=False
    )
```

```python
import functools
import math

import jax
import jax.numpy as jnp
from jax import lax
from jax.experimental import pallas as pl
from jax.experimental.pallas import tpu as pltpu
from jax.sharding import PartitionSpec as P

DH = 128
TS = 8


def group_size(item_count, row_count):
    size = 1
    for option in range(1, item_count + 1):
        if item_count % option == 0 and option * row_count <= 1024:
            size = option
    return size


def attend_group(group_parts):
    query_rows, key_rows, value_rows, allowed = group_parts
    dot_terms = jnp.einsum("gmd,gnd->gmn", query_rows, key_rows, preferred_element_type=jnp.float32)
    query_sq = jnp.einsum("gmd,gmd->gm", query_rows, query_rows, preferred_element_type=jnp.float32)
    key_sq = jnp.einsum("gnd,gnd->gn", key_rows, key_rows, preferred_element_type=jnp.float32)
    distance = query_sq[:, :, None] + key_sq[:, None, :] - 2.0 * dot_terms
    scores = jnp.where(allowed, -distance * (0.5 / math.sqrt(query_rows.shape[2])), -jnp.inf)
    highest = jnp.max(scores, axis=2, keepdims=True)
    weights = jnp.exp(scores - highest)
    totals = jnp.sum(weights, axis=2, keepdims=True)
    mixed = jnp.einsum(
        "gmn,gnd->gmd", weights.astype(jnp.bfloat16), value_rows, preferred_element_type=jnp.float32
    )
    return mixed / totals


def attend_items(query_items, key_items, value_items, masks):
    item_count = query_items.shape[0]
    per_group = group_size(item_count, query_items.shape[1])
    groups = item_count // per_group

    def regroup(array):
        return array.reshape((groups, per_group) + array.shape[1:])

    mixed = lax.map(
        attend_group,
        (regroup(query_items), regroup(key_items), regroup(value_items), regroup(masks)),
    )
    return mixed.reshape((item_count,) + mixed.shape[2:])


def tile_split(block):
    frames, token_rows, token_cols, channels = block.shape
    heads = channels // DH
    return (
        block.reshape(frames, token_rows // TS, TS, token_cols // TS, TS, heads, DH)
        .transpose(5, 0, 1, 3, 2, 4, 6)
        .reshape(heads, frames, token_rows // TS * (token_cols // TS), TS * TS, DH)
    )


def neighbours(tiles, tile_rows, tile_cols):
    heads, frames, count_tiles, area, depth = tiles.shape
    grid = tiles.reshape(heads * frames, tile_rows, tile_cols, area, depth)
    padded = jnp.pad(grid, ((0, 0), (1, 1), (1, 1), (0, 0), (0, 0)))
    views = [
        padded[:, dy : dy + tile_rows, dx : dx + tile_cols] for dy in range(3) for dx in range(3)
    ]
    stacked = jnp.stack(views, axis=3)
    return stacked.reshape(heads * frames * count_tiles, 9 * area, depth)


def pad_tiles(tiles, total):
    return jnp.pad(tiles, ((0, 0), (0, 0), (0, total - tiles.shape[2]), (0, 0), (0, 0)))


def per_device(queries, keys, values, back_reach, fwd_reach, valid_rows, valid_cols):
    frames, token_rows, token_cols, channels = queries.shape
    heads = channels // DH
    tile_rows = token_rows // TS
    tile_cols = token_cols // TS
    count_tiles = tile_rows * tile_cols
    area = TS * TS
    frame_count = lax.axis_size("frame")
    frame_index = lax.axis_index("frame")
    padded_count = (count_tiles + frame_count - 1) // frame_count * frame_count
    tiles_here = padded_count // frame_count
    all_frames = frames * frame_count
    row_ids = jnp.arange(token_rows, dtype=jnp.int32)
    col_ids = jnp.arange(token_cols, dtype=jnp.int32)
    row_ok = row_ids[None, :] < valid_rows[:, None]
    col_ok = col_ids[None, :] < valid_cols[:, None]
    token_valid = row_ok[:, :, None] & col_ok[:, None, :]
    tile_valid_all = (
        token_valid.reshape(all_frames, tile_rows, TS, tile_cols, TS)
        .transpose(0, 1, 3, 2, 4)
        .reshape(all_frames, tile_rows, tile_cols, area)
    )
    tile_valid = lax.dynamic_slice_in_dim(tile_valid_all, frame_index * frames, frames, 0)
    padded_valid = jnp.pad(tile_valid, ((0, 0), (1, 1), (1, 1), (0, 0)))
    near_valid = jnp.stack(
        [
            padded_valid[:, dy : dy + tile_rows, dx : dx + tile_cols]
            for dy in range(3)
            for dx in range(3)
        ],
        axis=3,
    )
    near_valid = near_valid.reshape(frames, count_tiles, 1, 9 * area)
    query_factor = tile_valid.reshape(frames, count_tiles, area).astype(jnp.float32)
    query_t = tile_split(queries)
    key_t = tile_split(keys)
    masks = near_valid[None].reshape(heads * frames * count_tiles, 1, 9 * area)
    spatial = attend_items(
        query_t.reshape(heads * frames * count_tiles, area, DH),
        neighbours(key_t, tile_rows, tile_cols),
        neighbours(tile_split(values), tile_rows, tile_cols),
        masks,
    )
    spatial = spatial.reshape(heads, frames, count_tiles, area, DH)
    spatial_t = (spatial * query_factor[None, :, :, :, None]).astype(jnp.bfloat16)
    triple = jnp.stack(
        [
            pad_tiles(query_t, padded_count),
            pad_tiles(key_t, padded_count),
            pad_tiles(spatial_t, padded_count),
        ]
    )
    sent = lax.all_to_all(triple, "frame", split_axis=3, concat_axis=2, tiled=True)
    query_here, key_here, value_here = (sent[0], sent[1], sent[2])
    start = frame_index * tiles_here
    length = all_frames * area
    frame_of = jnp.arange(length, dtype=jnp.int32) // area
    frame_gap = frame_of[None, :] - frame_of[:, None]
    valid_flat = tile_valid_all.reshape(all_frames, count_tiles, area).transpose(1, 0, 2)
    valid_flat = jnp.pad(
        valid_flat, ((0, padded_count - count_tiles), (0, 0), (0, 0)), constant_values=True
    )
    valid_here = lax.dynamic_slice_in_dim(valid_flat, start, tiles_here, 0)
    back_here = lax.dynamic_slice_in_dim(
        jnp.pad(back_reach.reshape(count_tiles), (0, padded_count - count_tiles)),
        start,
        tiles_here,
        0,
    )
    fwd_here = lax.dynamic_slice_in_dim(
        jnp.pad(fwd_reach.reshape(count_tiles), (0, padded_count - count_tiles)),
        start,
        tiles_here,
        0,
    )
    key_ok = valid_here.reshape(tiles_here, length)
    allowed = (
        (frame_gap[None] >= -back_here[:, None, None])
        & (frame_gap[None] <= fwd_here[:, None, None])
        & key_ok[:, None, :]
    )
    time_masks = allowed[None].reshape(heads * tiles_here, length, length)

    def by_tile(array):
        return array.transpose(0, 2, 1, 3, 4).reshape(heads * tiles_here, length, DH)

    temporal = attend_items(
        by_tile(query_here), by_tile(key_here), by_tile(value_here), time_masks
    ).astype(jnp.bfloat16)
    temporal = temporal.reshape(heads, tiles_here, all_frames, area, DH).transpose(0, 2, 1, 3, 4)
    returned = lax.all_to_all(temporal, "frame", split_axis=1, concat_axis=2, tiled=True)[
        :, :, :count_tiles
    ]
    combined = (spatial_t.astype(jnp.float32) + returned.astype(jnp.float32)) * query_factor[
        None, :, :, :, None
    ]
    combined = combined.astype(jnp.bfloat16).reshape(
        heads, frames, tile_rows, tile_cols, TS, TS, DH
    )
    return combined.transpose(1, 2, 4, 3, 5, 0, 6).reshape(frames, token_rows, token_cols, channels)


SCALE = 1.0 / math.sqrt(DH)
MASKED = -1e30
AREA = TS * TS
GROUP = 10
PAIRS = 5
VMEM_LIMIT = 24 * 1024 * 1024
NT_DIMS = (((1,), (1,)), ((), ()))


def scalar_spec():
    return pl.BlockSpec(memory_space=pltpu.SMEM)


def vector_spec():
    return pl.BlockSpec(memory_space=pltpu.VMEM)


def read_tile(ref, row, col):
    return ref[pl.ds(row * TS, TS), col].reshape(AREA, DH)


def key_norms(keys):
    wide = keys.astype(jnp.float32)
    square = wide * wide
    high = square.astype(jnp.bfloat16)
    low = (square - high.astype(jnp.float32)).astype(jnp.bfloat16)
    ones = jnp.ones((8, 2 * DH), jnp.bfloat16)
    both = jnp.concatenate([high, low], axis=1)
    total = lax.dot_general(ones, both, NT_DIMS, preferred_element_type=jnp.float32)
    return total * (-0.5 * SCALE)


def row_valid(row, col, row_limit, col_limit):
    token = lax.broadcasted_iota(jnp.int32, (AREA, DH), 0)
    return (row * TS + (token >> 3) < row_limit) & (col * TS + (token & 7) < col_limit)


def pack_kernel(
    tile_rows, tile_cols, levels, me, back, fwd, keys, packed, reach, place, order, level, held,
    sem,
):
    load = pltpu.make_async_copy(keys, held, sem)
    load.start()
    left = me[0] < 2
    most = [None] * 4
    tiles = [(r, c) for r in range(tile_rows) for c in range(tile_cols)]
    for way in range(2):
        counts = [jnp.int32(0)] * 4
        for index, (r, c) in enumerate(tiles):
            toward, away = back[r, c], fwd[r, c]
            value = jnp.where(left, toward, away) if way == 0 else jnp.where(left, away, toward)
            reach[way, index] = value
            counts = [counts[v] + (value >= v).astype(jnp.int32) for v in range(4)]
        for v in (1, 2, 3):
            most[v] = counts[v] if way == 0 else jnp.maximum(most[v], counts[v])
        spots = [counts[1], counts[2], counts[3], jnp.int32(0)]
        for index in range(len(tiles)):
            value = jnp.minimum(reach[way, index], 3)
            spot = spots[0]
            for v in (1, 2, 3):
                spot = jnp.where(value == v, spots[v], spot)
            spots = [spots[v] + (value == v).astype(jnp.int32) for v in range(4)]
            place[way, index] = spot
            if way == 1:
                order[spot] = index
    chosen = jnp.int32(0)
    for one, two, three in levels[:-1]:
        over = (most[1] > one) | (most[2] > two) | (most[3] > three)
        chosen += over.astype(jnp.int32)
    level[0] = chosen
    load.wait()

    def pack_row(r, carry):
        for c in range(tile_cols):
            packed[place[0, r * tile_cols + c]] = read_tile(held, r, c)
        return carry

    lax.fori_loop(0, tile_rows, pack_row, 0)


def spatial_kernel(
    tile_rows, tile_cols, me, place, rows_ok, cols_ok, queries, packed_k, values, mixed, packed_q,
    query_t, key_t, value_t, bias_even, bias_odd,
):
    row_limit, col_limit = rows_ok[me[0]], cols_ok[me[0]]
    wide = tile_cols * AREA
    value_t[:, DH:] = jnp.ones((value_t.shape[0], DH), jnp.bfloat16)

    def lane_bias(r, first, count):
        start = pl.multiple_of((r * tile_cols + first) * AREA, AREA)
        norms = key_norms(key_t[pl.ds(start, count * AREA)])
        lane = lax.broadcasted_iota(jnp.int32, (8, count * AREA), 1) + first * AREA
        valid = (r * TS + ((lane >> 3) & 7) < row_limit) & (
            (lane >> 6) * TS + (lane & 7) < col_limit
        )
        return jnp.where(valid, norms, MASKED)

    def retile_row(r, carry):
        for c in range(tile_cols):
            index = r * tile_cols + c
            span = pl.ds(pl.multiple_of(index * AREA, AREA), AREA)
            tile_q = read_tile(queries, r, c)
            query_t[span] = tile_q
            packed_q[place[1, index]] = tile_q
            key_t[span] = packed_k[place[0, index]]
            value_t[span, :DH] = read_tile(values, r, c)
        bias_even[r] = lane_bias(r, 0, tile_cols)
        bias_odd[r] = lane_bias(r, 1, tile_cols - 2)
        return carry

    lax.fori_loop(0, tile_rows, retile_row, 0)
    lane_tile = lax.broadcasted_iota(jnp.int32, (8, 4 * AREA), 1) >> 6

    def attend_row(r, carry):
        first_row = jnp.clip(r - 1, 0, tile_rows - 3)
        for first_pair in range(0, tile_cols // 2, PAIRS):
            attend_pairs(r, first_row, range(first_pair, min(first_pair + PAIRS, tile_cols // 2)))
        return carry

    def attend_pairs(r, first_row, pairs):
        first_cols = [min(max(2 * pair - 1, 0), tile_cols - 4) for pair in pairs]
        dots, spans = [], []
        for pair, first_col in zip(pairs, first_cols):
            start = (r * tile_cols + 2 * pair) * AREA
            query = query_t[pl.ds(pl.multiple_of(start, AREA), 2 * AREA)]
            starts = [((first_row + step) * tile_cols + first_col) * AREA for step in range(3)]
            spans.append([pl.ds(pl.multiple_of(start, AREA), 4 * AREA) for start in starts])
            dots.append(
                [
                    lax.dot_general(
                        query, key_t[span], NT_DIMS, preferred_element_type=jnp.float32
                    )
                    for span in spans[-1]
                ]
            )
        scores = []
        for pair, first_col, parts in zip(pairs, first_cols, dots):
            scores.append([])
            for step, part in enumerate(parts):
                key_row = first_row + step
                table = bias_odd if first_col % 2 else bias_even
                lane_start = (first_col - first_col % 2) * AREA
                bias = table[key_row, :, lane_start : lane_start + 4 * AREA]
                near_row = jnp.abs(key_row - r) <= 1
                both = []
                for half in range(2):
                    gap = lane_tile + (first_col - 2 * pair - half)
                    near = (gap >= -1) & (gap <= 1) & near_row
                    here = part[half * AREA : (half + 1) * AREA].reshape(TS, 8, 4 * AREA)
                    here = here * SCALE + jnp.where(near, bias, MASKED)[None]
                    both.append(here.reshape(AREA, 4 * AREA))
                scores[-1].append(jnp.concatenate(both, axis=0))
        tops = [jnp.maximum(jnp.maximum(one[0], one[1]), one[2]) for one in scores]
        tops = [jnp.max(top, axis=1, keepdims=True) for top in tops]
        totals = []
        for one, top, where in zip(scores, tops, spans):
            weights = [jnp.exp(score - top).astype(jnp.bfloat16) for score in one]
            parts = [
                jnp.dot(weight, value_t[span], preferred_element_type=jnp.float32)
                for weight, span in zip(weights, where)
            ]
            totals.append((parts[0] + parts[1]) + parts[2])
        for pair, total in zip(pairs, totals):
            result = total[:, :DH] / total[:, DH:]
            for half in range(2):
                valid = row_valid(r, 2 * pair + half, row_limit, col_limit)
                tile = jnp.where(valid, result[half * AREA : (half + 1) * AREA], 0.0)
                spot = place[0, r * tile_cols + 2 * pair + half]
                mixed[spot] = tile.astype(jnp.bfloat16)

    lax.fori_loop(0, tile_rows, attend_row, 0)


def frames_of(mine):
    left = mine < 2
    return mine, jnp.where(left, 0, 3), jnp.where(left, 2, 1), jnp.where(left, 3, 0)


def by_block(picks, lanes):
    block = lax.broadcasted_iota(jnp.int32, (8, lanes), 1) >> 6
    chosen = jnp.full((8, lanes), picks[0], jnp.int32)
    for number in range(1, lanes // AREA):
        chosen = jnp.where(block == number, picks[number], chosen)
    return chosen


def room_left(frames, rows_ok, cols_ok, lanes):
    lane = lax.broadcasted_iota(jnp.int32, (8, lanes), 1)
    row_room = by_block([rows_ok[frame] for frame in frames], lanes) - ((lane >> 3) & 7)
    col_room = by_block([cols_ok[frame] for frame in frames], lanes) - (lane & 7)
    return row_room, col_room


def weigh(queries, keys_here, biases):
    parts, highest = [], []
    dots = [
        lax.dot_general(query, key, NT_DIMS, preferred_element_type=jnp.float32)
        for query, key in zip(queries, keys_here)
    ]
    norms = [key_norms(key) for key in keys_here]
    for dot, norm, bias in zip(dots, norms, biases):
        lanes = dot.shape[1]
        part = dot.reshape(TS, 8, lanes) * SCALE + (norm + bias)[None]
        parts.append(part.reshape(AREA, lanes))
    highest = [jnp.max(part, axis=1, keepdims=True) for part in parts]
    return [jnp.exp(part - top) for part, top in zip(parts, highest)], highest


def mask_bias(allowed, room, row, col, lanes):
    valid = (room[0] > row * TS) & (room[1] > col * TS) & (by_block(allowed, lanes) > 0)
    return jnp.where(valid, 0.0, MASKED)


def mix(weights, values_here):
    ones = jnp.ones(values_here.shape, jnp.bfloat16)
    total = jnp.dot(
        weights,
        jnp.concatenate([values_here, ones], axis=1),
        preferred_element_type=jnp.float32,
    )
    return total[:, :DH], total[:, DH:]


def in_chunks(first, last, body, carry, most=None):
    most = most or (11 if last - first <= 30 else 4)
    size = max(option for option in range(1, most + 1) if (last - first) % option == 0)
    if size == last - first:
        return body(list(range(first, last)), carry)

    def chunk(number, carry):
        return body([first + number * size + step for step in range(size)], carry)

    return lax.fori_loop(0, (last - first) // size, chunk, carry)


def is_inner(mine):
    return (mine == 1) | (mine == 2)


def store_sums(ref, first, sums):
    for step in range(3):
        piece = sums.astype(jnp.bfloat16)
        ref[first + step] = piece
        sums = sums - piece.astype(jnp.float32)


def load_sums(ref, first):
    pieces = [ref[first + step].astype(jnp.float32) for step in range(3)]
    return (pieces[0] + pieces[1]) + pieces[2]


def reached(reach, index, least):
    return (reach[1, index] >= least).astype(jnp.int32)


def near_hosted_kernel(
    tile_cols, one, two, three, me, reach, place, order, rows_ok, cols_ok, hosted_q, packed_k,
    far_k, own_s, far_s, mixed,
):
    own, _, far, _ = frames_of(me[0])
    room = room_left((own, far), rows_ok, cols_ok, 2 * AREA)
    lane = lax.broadcasted_iota(jnp.int32, (AREA, DH), 1)

    def near_ones(spots, sums):
        indices = [order[spot] for spot in spots]
        rows = [lax.div(index, tile_cols) for index in indices]
        homes = [place[0, index] for index in indices]
        keys_here = [
            jnp.concatenate([packed_k[home], far_k[jnp.minimum(spot, two - 1)]], axis=0)
            for home, spot in zip(homes, spots)
        ]
        values_here = [
            jnp.concatenate([own_s[home], far_s[jnp.minimum(spot, two - 1)]], axis=0)
            for home, spot in zip(homes, spots)
        ]
        biases = [
            mask_bias(
                (reached(reach, index, 1), reached(reach, index, 2)),
                room, row, index - row * tile_cols, 2 * AREA,
            )
            for index, row in zip(indices, rows)
        ]
        parts, highest = weigh([hosted_q[spot - three] for spot in spots], keys_here, biases)
        totals = [mix(part.astype(jnp.bfloat16), v) for part, v in zip(parts, values_here)]
        for spot, (total, sum_here), top in zip(spots, totals, highest):
            mixed[spot - three] = (total / sum_here).astype(jnp.bfloat16)
            sums = jnp.where(lane == spot, top + jnp.log(sum_here), sums)
        return sums

    @pl.when(is_inner(me[0]))
    def _():
        sums = in_chunks(three, one, near_ones, jnp.zeros((AREA, DH), jnp.float32))
        store_sums(mixed, one - three, sums)


def far_hosted_kernel(
    tile_cols, three, me, reach, place, order, rows_ok, cols_ok, hosted_q, packed_k, far_k,
    far_k2, weights, sums_out,
):
    own, _, far, far2 = frames_of(me[0])
    room = room_left((own, far, far2, own), rows_ok, cols_ok, 4 * AREA)
    lane = lax.broadcasted_iota(jnp.int32, (AREA, DH), 1)
    no = jnp.int32(0)

    def far_ones(spots, sums):
        indices = [order[spot] for spot in spots]
        rows = [lax.div(index, tile_cols) for index in indices]
        homes = [packed_k[place[0, index]] for index in indices]
        keys_here = [
            jnp.concatenate([home, far_k[spot], far_k2[spot], home], axis=0)
            for home, spot in zip(homes, spots)
        ]
        biases = [
            mask_bias(
                tuple(reached(reach, index, least) for least in (1, 2, 3)) + (no,),
                room, row, index - row * tile_cols, 4 * AREA,
            )
            for index, row in zip(indices, rows)
        ]
        parts, highest = weigh([hosted_q[spot] for spot in spots], keys_here, biases)
        for spot, part, top in zip(spots, parts, highest):
            weights[spot] = part.astype(jnp.bfloat16)
            sum_here = jnp.sum(part, axis=1, keepdims=True)
            sums = jnp.where(lane == spot, top + jnp.log(sum_here), sums)
        return sums

    @pl.when(is_inner(me[0]))
    def _():
        sums = in_chunks(0, three, far_ones, jnp.zeros((AREA, DH), jnp.float32))
        store_sums(sums_out, 0, sums)


def far_mix_kernel(three, me, place, order, weights, own_s, far_s, far_s2, sums, mixed):
    def far_ones(spots, carry):
        homes = [own_s[place[0, order[spot]]] for spot in spots]
        totals = [
            mix(weights[spot], jnp.concatenate([home, far_s[spot], far_s2[spot], home], axis=0))
            for spot, home in zip(spots, homes)
        ]
        for spot, (total, sum_here) in zip(spots, totals):
            mixed[spot] = (total / sum_here).astype(jnp.bfloat16)
        return carry

    @pl.when(is_inner(me[0]))
    def _():
        in_chunks(0, three, far_ones, 0)
        mixed[three : three + 3] = sums[...]


def tile_groups(tile_rows, tile_cols, body, carry):
    rows = 1

    def step(number, carry):
        here = [(number * rows + r, c) for r in range(rows) for c in range(tile_cols)]
        for first in range(0, len(here), GROUP):
            carry = body(here[first : first + GROUP], carry)
        return carry

    return lax.fori_loop(0, tile_rows // rows, step, carry)


def two_part(first, rest, spot, split, last, start=0):
    tile = first[jnp.minimum(spot, split - 1)]
    if last > split:
        other = rest[start + jnp.clip(spot - split, 0, last - split - 1)]
        tile = jnp.where(spot < split, tile, other)
    return tile


def own_weights_kernel(
    tile_rows, tile_cols, one, two, me, reach, place, order, rows_ok, cols_ok, queries, packed_k,
    near_k, near_rest, far_k, far_k2, weights, sums_out,
):
    mine = me[0]
    inner = is_inner(mine)
    room = room_left(frames_of(mine), rows_ok, cols_ok, 4 * AREA)
    lane = lax.broadcasted_iota(jnp.int32, (AREA, DH), 1)

    def weigh_tiles(numbers, carry):
        indices, query_list, key_list, biases = [], [], [], []
        for number in numbers:
            spot = number + jnp.where(number < two, 0, one - two)
            index = order[spot]
            r = lax.div(index, tile_cols)
            c = index - r * tile_cols
            home = place[0, index]
            near = two_part(near_k, near_rest, home, two, one)
            far = far_k[jnp.minimum(spot, two - 1)]
            far2 = far_k2[jnp.minimum(spot, two - 1)]
            near_reach, far_reach = reach[0, index], reach[1, index]
            allowed = (
                jnp.int32(1),
                (near_reach >= 1).astype(jnp.int32),
                (far_reach >= 1).astype(jnp.int32),
                (far_reach >= 2).astype(jnp.int32),
            )
            indices.append(index)
            biases.append(mask_bias(allowed, room, r, c, 4 * AREA))
            query_list.append(read_tile(queries, r, c))
            key_list.append(jnp.concatenate([packed_k[home], near, far, far2], axis=0))
        parts, _ = weigh(query_list, key_list, biases)
        for index, part in zip(indices, parts):
            weights[index] = part.astype(jnp.bfloat16)
        return carry

    def weigh_alone(here, sums):
        alone = room_left((mine,), rows_ok, cols_ok, AREA)
        biases = [mask_bias((jnp.int32(1),), alone, r, c, AREA) for r, c in here]
        parts, highest = weigh(
            [read_tile(queries, r, c) for r, c in here],
            [packed_k[place[0, r * tile_cols + c]] for r, c in here],
            biases,
        )
        totals = [jnp.sum(part, axis=1, keepdims=True) for part in parts]
        for (r, c), part, sum_here, top in zip(here, parts, totals, highest):
            index = r * tile_cols + c
            weights[index, :, :AREA] = part.astype(jnp.bfloat16)
            sums = jnp.where(lane == index, top + jnp.log(sum_here), sums)
        return sums

    @pl.when(inner)
    def _():
        in_chunks(0, tile_rows * tile_cols - one + two, weigh_tiles, 0, most=10)

    @pl.when(jnp.logical_not(inner))
    def _():
        nothing = jnp.zeros((AREA, DH), jnp.float32)
        sums_out[...] = tile_groups(tile_rows, tile_cols, weigh_alone, nothing)


def merged(own, own_sums, theirs, their_sums, index, spot):
    lane = lax.broadcasted_iota(jnp.int32, (AREA, DH), 1)
    gap = jnp.where(lane == spot, their_sums, 0.0) - jnp.where(lane == index, own_sums, 0.0)
    share = 1.0 / (1.0 + jnp.exp(jnp.sum(gap, axis=1, keepdims=True)))
    return share * own + (1.0 - share) * theirs.astype(jnp.float32)


def finished(spatial, temporal, valid):
    temporal = temporal.astype(jnp.bfloat16).astype(jnp.float32)
    tile = jnp.where(valid, spatial.astype(jnp.float32) + temporal, 0.0)
    return tile.astype(jnp.bfloat16).reshape(TS, TS, DH)


def tile_store(tile_cols, order, held, out, sems, spot):
    index = order[spot]
    r = lax.div(index, tile_cols)
    target = out.at[pl.ds(r * TS, TS), index - r * tile_cols]
    return pltpu.make_async_copy(held.at[spot], target, sems.at[spot])


def wait_stores(first, last, store):
    def wait(spot, carry):
        store(spot).wait()
        return carry

    lax.fori_loop(first, last, wait, 0)


def own_mix_kernel(
    tile_cols, count, one, two, three, me, reach, place, order, rows_ok, cols_ok, weights,
    own_sums, own_s, near_s, near_rest, far_s, far_s2, near_ones, first_o, out, held, sems,
):
    mine = me[0]
    inner = is_inner(mine)
    row_limit, col_limit = rows_ok[mine], cols_ok[mine]
    store = functools.partial(tile_store, tile_cols, order, held, out, sems)

    def finish(spots, results):
        for spot, result in zip(spots, results):
            index = order[spot]
            r = lax.div(index, tile_cols)
            valid = row_valid(r, index - r * tile_cols, row_limit, col_limit)
            held[spot] = finished(own_s[place[0, index]], result, valid)
            store(spot).start()

    def mix_tiles(spots, carry):
        totals = []
        for spot in spots:
            index = order[spot]
            home = place[0, index]
            near = two_part(near_s, near_rest, home, two, one, one - two)
            far = far_s[jnp.minimum(spot, two - 1)]
            far2 = far_s2[jnp.minimum(spot, three - 1)]
            values_here = jnp.concatenate([own_s[home], near, far, far2], axis=0)
            totals.append(mix(weights[index], values_here))
        finish(spots, [total / sum_here for total, sum_here in totals])
        return carry

    def mix_alone(spots):
        totals = []
        for spot in spots:
            index = order[spot]
            totals.append(mix(weights[index, :, :AREA], own_s[place[0, index]]))
        return [total / sum_here for total, sum_here in totals]

    def first_tiles(spots, carry):
        for spot, result in zip(spots, mix_alone(spots)):
            first_o[spot] = result.astype(jnp.bfloat16)
        return carry

    def merged_tiles(spots, carry):
        my_sums, their_sums = carry
        results = mix_alone(spots)
        for number, spot in enumerate(spots):
            index = order[spot]
            theirs = near_ones[spot - three]
            both = merged(results[number], my_sums, theirs, their_sums, index, spot)
            results[number] = jnp.where(reach[1, index] >= 1, both, results[number])
        finish(spots, results)
        return carry

    def alone_tiles(spots, carry):
        finish(spots, mix_alone(spots))
        return carry

    @pl.when(inner)
    def _():
        in_chunks(0, three, mix_tiles, 0)
        if count > one:
            in_chunks(one, count, mix_tiles, 0)
        wait_stores(0, three, store)

    @pl.when(jnp.logical_not(inner))
    def _():
        in_chunks(0, three, first_tiles, 0)
        if count > one:
            in_chunks(one, count, alone_tiles, 0)
        if one > three:
            in_chunks(three, one, merged_tiles, (own_sums[...], load_sums(near_ones, one - three)))
            wait_stores(three, one, store)

    if count > one:
        wait_stores(one, count, store)


def last_kernel(
    tile_cols, one, two, three, me, reach, place, order, rows_ok, cols_ok, done, weights, queries,
    packed_k, near_k, own_s, near_s, near_rest, far_s, late, own_sums, first_o, far_ones, out,
    held, sems,
):
    mine = me[0]
    inner = is_inner(mine)
    row_limit, col_limit = rows_ok[mine], cols_ok[mine]
    store = functools.partial(tile_store, tile_cols, order, held, out, sems)

    def finish(spots, results):
        for spot, result in zip(spots, results):
            index = order[spot]
            r = lax.div(index, tile_cols)
            valid = row_valid(r, index - r * tile_cols, row_limit, col_limit)
            held[spot] = finished(own_s[place[0, index]], result, valid)
            store(spot).start()

    def near_part(first, rest_start, home):
        return two_part(first, near_rest, home, two, one, rest_start)

    def late_mix(spot):
        index = order[spot]
        home = place[0, index]
        near = near_part(near_s, one - two, home)
        values_here = jnp.concatenate(
            [own_s[home], near, far_s[spot], late[spot - three]], axis=0
        )
        return mix(weights[index], values_here)

    def weigh_last(spots):
        room = room_left(frames_of(mine), rows_ok, cols_ok, 4 * AREA)
        query_list, key_list, value_list, biases = [], [], [], []
        for spot in spots:
            index = order[spot]
            r = lax.div(index, tile_cols)
            c = index - r * tile_cols
            home = place[0, index]
            allowed = (
                jnp.int32(1),
                (reach[0, index] >= 1).astype(jnp.int32),
                (reach[1, index] >= 1).astype(jnp.int32),
                jnp.int32(0),
            )
            biases.append(mask_bias(allowed, room, r, c, 4 * AREA))
            query_list.append(read_tile(queries, r, c))
            own, far = packed_k[home], late[spot - three + one - two]
            near = near_part(near_k, 0, home)
            key_list.append(jnp.concatenate([own, near, far, own], axis=0))
            own, far = own_s[home], late[spot - three]
            near = near_part(near_s, one - two, home)
            value_list.append(jnp.concatenate([own, near, far, own], axis=0))
        parts, _ = weigh(query_list, key_list, biases)
        return [part.astype(jnp.bfloat16) for part in parts], value_list

    if one > three:

        @pl.when(inner)
        def _():
            parts, value_list = weigh_last(range(two, one)) if one > two else ([], [])
            totals = [late_mix(spot) for spot in range(three, two)]
            totals += [mix(part, v) for part, v in zip(parts, value_list)]
            finish(range(three, one), [total / sum_here for total, sum_here in totals])
            wait_stores(three, one, store)

    @pl.when(jnp.logical_not(inner))
    def _():
        my_sums = own_sums[...]
        their_sums = load_sums(far_ones, three)

        def far_tiles(spots, carry):
            results = []
            for spot in spots:
                index = order[spot]
                own = first_o[spot].astype(jnp.float32)
                both = merged(own, my_sums, far_ones[spot], their_sums, index, spot)
                results.append(jnp.where(reach[1, index] >= 1, both, own))
            finish(spots, results)
            return carry

        in_chunks(0, three, far_tiles, 0)
        wait_stores(0, three, store)


def run_kernel(
    kernel, out_shape, scalars, arrays, scratch=(), scalar_outs=0, micros=4, from_hbm=0,
    to_hbm=0, in_place=False,
):
    outs = list(out_shape)
    arrays = [
        pltpu.with_memory_space_constraint(array, pltpu.HBM) if number < from_hbm else array
        for number, array in enumerate(arrays)
    ]
    in_hbm = pl.BlockSpec(memory_space=pltpu.HBM)
    in_specs = [in_hbm] * from_hbm + [vector_spec()] * (len(arrays) - from_hbm)
    out_specs = [vector_spec()] * (len(outs) - scalar_outs - to_hbm)
    out_specs += [scalar_spec()] * scalar_outs + [in_hbm] * to_hbm
    return pl.pallas_call(
        kernel,
        out_shape=outs,
        in_specs=[scalar_spec()] * len(scalars) + in_specs,
        out_specs=out_specs,
        scratch_shapes=list(scratch),
        input_output_aliases={len(scalars): 0} if in_place else {},
        compiler_params=pltpu.CompilerParams(vmem_limit_bytes=VMEM_LIMIT),
        cost_estimate=pl.CostEstimate(
            flops=int(micros * 1e9), bytes_accessed=int(micros * 1e6), transcendentals=0
        ),
    )(*scalars, *arrays)


def room_levels(count):
    shares = ((49, 34, 22), (51, 36, 24), (54, 42, 27))
    levels = [tuple(max(count * share // 60, 1) for share in level) for level in shares]
    return levels + [(count, count, count)]


def four_frames(queries, keys, values, back_reach, fwd_reach, valid_rows, valid_cols):
    _, token_rows, token_cols, _ = queries.shape
    tile_rows, tile_cols = token_rows // TS, token_cols // TS
    count = tile_rows * tile_cols
    shape = (token_rows, tile_cols, TS, DH)
    queries, keys, values = queries.reshape(shape), keys.reshape(shape), values.reshape(shape)
    me = lax.axis_index("frame").reshape(1).astype(jnp.int32)
    inward, across, outward = [(0, 1), (3, 2)], [(1, 2), (2, 1)], [(1, 0), (2, 3)]
    levels = room_levels(count)

    def tiles(number):
        return jax.ShapeDtypeStruct((number, AREA, DH), jnp.bfloat16)

    def ints(*sizes):
        return jax.ShapeDtypeStruct(sizes, jnp.int32)

    def send(array, pairs):
        return lax.ppermute(array, "frame", pairs)

    packed_k, reach, place, order, level = run_kernel(
        functools.partial(pack_kernel, tile_rows, tile_cols, levels),
        (tiles(count), ints(2, count), ints(2, count), ints(count), ints(1)),
        (
            me,
            pltpu.with_memory_space_constraint(back_reach, pltpu.HBM),
            pltpu.with_memory_space_constraint(fwd_reach, pltpu.HBM),
        ),
        (keys,),
        scratch=(pltpu.VMEM(shape, jnp.bfloat16), pltpu.SemaphoreType.DMA),
        scalar_outs=4,
        micros=2,
        from_hbm=1,
    )

    def with_room(one, two, three):
        def run(queries, values, packed_k, reach, place, order):
            far_k = send(packed_k[:two], across)
            near_k = send(packed_k[:two], inward)
            own_s, packed_q = run_kernel(
                functools.partial(spatial_kernel, tile_rows, tile_cols),
                (tiles(count), tiles(count)),
                (me, place, valid_rows, valid_cols),
                (queries, packed_k, values),
                scratch=(
                    pltpu.VMEM((count * AREA, DH), jnp.bfloat16),
                    pltpu.VMEM((count * AREA, DH), jnp.bfloat16),
                    pltpu.VMEM((count * AREA, 2 * DH), jnp.bfloat16),
                    pltpu.VMEM((tile_rows, 8, tile_cols * AREA), jnp.float32),
                    pltpu.VMEM((tile_rows, 8, (tile_cols - 2) * AREA), jnp.float32),
                ),
                micros=10,
            )
            far_s = send(own_s[:two], across)
            near_s = send(own_s[:two], inward)
            hosted_qa = send(packed_q[three:one], inward) if one > three else None
            first_q, far_k = lax.optimization_barrier((packed_q[:three], far_k))
            hosted_qb = send(first_q, inward)
            far_k2 = send(near_k, across)
            far_s2 = send(near_s[:three], across)
            returned_a = near_k
            if one > three:
                (hosted_a,) = run_kernel(
                    functools.partial(near_hosted_kernel, tile_cols, one, two, three),
                    (tiles(one - three + 3),),
                    (me, reach, place, order, valid_rows, valid_cols),
                    (hosted_qa, packed_k, far_k, own_s, far_s),
                    micros=0.6,
                )
                returned_a = send(hosted_a, outward)
            near_rest, late = near_k, near_s
            if one > two:
                rest_k, rest_s, late_s, _ = lax.optimization_barrier(
                    (packed_k[two:one], own_s[two:one], near_s[three:two], near_s)
                )
                near_rest = send(jnp.concatenate([rest_k, rest_s]), inward)
                late = send(jnp.concatenate([late_s, rest_s, rest_k]), across)
            hosted_w, sums = run_kernel(
                functools.partial(far_hosted_kernel, tile_cols, three),
                (jax.ShapeDtypeStruct((three, AREA, 4 * AREA), jnp.bfloat16), tiles(3)),
                (me, reach, place, order, valid_rows, valid_cols),
                (hosted_qb, packed_k, far_k, far_k2),
                micros=0.6,
            )
            (hosted_b,) = run_kernel(
                functools.partial(far_mix_kernel, three),
                (tiles(three + 3),),
                (me, place, order),
                (hosted_w, own_s, far_s, far_s2, sums),
                micros=2,
            )
            returned_b = send(hosted_b, outward)
            hosted_b, near_k = lax.optimization_barrier((hosted_b, near_k))
            own_w, own_sums = run_kernel(
                functools.partial(own_weights_kernel, tile_rows, tile_cols, one, two),
                (
                    jax.ShapeDtypeStruct((count, AREA, 4 * AREA), jnp.bfloat16),
                    jax.ShapeDtypeStruct((AREA, DH), jnp.float32),
                ),
                (me, reach, place, order, valid_rows, valid_cols),
                (queries, packed_k, near_k, near_rest, far_k, far_k2),
                micros=1,
            )
            staging = (
                pltpu.VMEM((count, TS, TS, DH), jnp.bfloat16),
                pltpu.SemaphoreType.DMA((count,)),
            )
            first_o, out = run_kernel(
                functools.partial(own_mix_kernel, tile_cols, count, one, two, three),
                (tiles(three), pltpu.HBM(shape, jnp.bfloat16)),
                (me, reach, place, order, valid_rows, valid_cols),
                (own_w, own_sums, own_s, near_s, near_rest, far_s, far_s2, returned_a),
                scratch=staging,
                micros=3,
                to_hbm=1,
            )
            (out,) = run_kernel(
                functools.partial(last_kernel, tile_cols, one, two, three),
                (pltpu.HBM(shape, jnp.bfloat16),),
                (me, reach, place, order, valid_rows, valid_cols),
                (
                    out, own_w, queries, packed_k, near_k, own_s, near_s, near_rest, far_s, late,
                    own_sums, first_o, returned_b,
                ),
                scratch=staging,
                micros=3,
                from_hbm=1,
                to_hbm=1,
                in_place=True,
            )
            return out

        return run

    branches = [with_room(*level) for level in levels]
    operands = (queries, values, packed_k, reach, place, order)
    out = lax.switch(level[0], branches, *operands)
    return out.reshape(1, token_rows, token_cols, DH)


def solution(mesh):
    in_specs = (
        P(("dp", "frame"), None, None, "row"),
        P(("dp", "frame"), None, None, "row"),
        P(("dp", "frame"), None, None, "row"),
        P("dp", None),
        P("dp", None),
        P("dp"),
        P("dp"),
    )
    out_specs = P(("dp", "frame"), None, None, "row")

    def block(*args):
        frames, _, token_cols, channels = args[0].shape
        line = mesh.shape["frame"] == 4 and frames == 1 and channels == DH
        if line and token_cols % (2 * TS) == 0 and 4 <= token_cols // TS:
            return four_frames(*args)
        return per_device(*args)

    return jax.shard_map(
        block, mesh=mesh, in_specs=in_specs, out_specs=out_specs, check_vma=False
    )
```
